32 devices in a mesh: dp: 8 (over z, x), seq: 4 (over y, core).
Axes of the slice: x: 2, y: 2, z: 4, core: 2. Of those that a mesh axis runs over, the one named last changes fastest.
Arguments:
- inputs: bfloat16 [64, 1024, 512], P('dp', 'seq'), may hold values from -6 to 6
- segments: int32 [64, 1024], P('dp', 'seq'), may hold values from 0 to 6, as said below
- cotangent: bfloat16 [64, 1024, 512], P('dp', 'seq'), may hold values from -6 to 6
- gain_attn: float32 [512], P(('dp', 'seq')), may hold values from 0.1 to 1.9
- w_qkv: float32 [512, 1536], P(('dp', 'seq')), may hold values from -0.25 to 0.25
- w_out: float32 [512, 512], P(('dp', 'seq')), may hold values from -2 to 2
- gain_mix: float32 [512], P(('dp', 'seq')), may hold values from 0.1 to 1.9
- w_control: float32 [4, 512], P(None, ('dp', 'seq')), may hold values from -0.1875 to 0.1875
- w_expand: float32 [4, 512, 2048], P(None, ('dp', 'seq')), may hold values from -4 to 4
- w_shrink: float32 [4, 2048, 512], P(None, ('dp', 'seq')), may hold values from -1.5 to 1.5
Outputs:
- output: bfloat16 [64, 1024, 512], P('dp', 'seq')
- grad_inputs: bfloat16 [64, 1024, 512], P('dp', 'seq')
- grad_gain_attn: float32 [512], P(('dp', 'seq'))
- grad_w_qkv: float32 [512, 1536], P(('dp', 'seq'))
- grad_w_out: float32 [512, 512], P(('dp', 'seq'))
- grad_gain_mix: float32 [512], P(('dp', 'seq'))
- grad_w_control: float32 [4, 512], P(None, ('dp', 'seq'))
- grad_w_expand: float32 [4, 512, 2048], P(None, ('dp', 'seq'))
- grad_w_shrink: float32 [4, 2048, 512], P(None, ('dp', 'seq'))
The draws below stay inside these ranges and needn't reach their ends.
Inputs may be any that keep to these rules, and one draw needn't show every extreme that they name: `segments`: each row's segment numbers start at 0 and never fall along the row; a document is the run of positions with one number.
All inputs are finite; a program needn't handle non-finite values.
Results may differ from the reference program's by a relative error of at most 0.033.
Values may be sent and summed in bfloat16 or wider, within the bound.
No kernel may reach another device: no remote copies, remote signals or barrier semaphores. Data moves between devices by JAX's collectives and lax.ppermute only.
A program may use at most 256 MiB of HBM per device.

```python
import math
import jax
import jax.numpy as jnp
from jax import lax

D = 512
HEADS = 8
HEAD_DIM = 64
FF = 2048
EXPERTS = 4
GROUP = 32
SEQLEN = 1024
POS_DEV = 256
ROWS = 64


def draw_segments(key, part):
    key = jax.random.fold_in(key, 7)
    key_early, key_late, key_active, key_pick = jax.random.split(key, 4)
    half_span = max(POS_DEV // 2, 2)
    early = jax.random.randint(key_early, (ROWS, 3), 1, half_span)
    late = jax.random.randint(key_late, (ROWS, 3), SEQLEN - half_span + 1, SEQLEN)
    active = jax.random.randint(key_active, (ROWS, 6), 0, 2)
    chosen = jax.random.randint(key_pick, (), 0, ROWS)
    active = jnp.where(jnp.arange(ROWS)[:, None] == chosen, 1, active)
    bounds = jnp.concatenate([early, late], axis=1)
    places = jnp.arange(SEQLEN)
    crossed = (places[None, None, :] >= bounds[:, :, None]).astype(jnp.int32)
    return jnp.sum(active[:, :, None] * crossed, axis=1).astype(jnp.int32)


def block_scale(own_key, extent, shards, least, high):
    factor_of = 1.0
    for dim, blocks in shards:
        steps = jax.random.uniform(jax.random.fold_in(jax.random.fold_in(own_key, 6), dim), (blocks,), jnp.float32, least / len(shards), high / len(shards))
        factor_of = factor_of * jnp.repeat(jnp.exp(steps), extent[dim] // blocks).reshape((-1,) + (1,) * (len(extent) - 1 - dim))
    return factor_of


def normal_values(own_key, shape, scale, bound, shards=(), kind=jnp.bfloat16):
    entries = scale * jax.random.normal(own_key, shape, jnp.float32)
    if shards:
        entries = entries * block_scale(own_key, shape, shards, -0.22, 0.18)
    return jnp.clip(entries, -bound, bound).astype(kind)


def setup_inputs(seed: int = 0) -> dict:
    arg_keys = jax.random.split(jax.random.key(seed), 11)
    return {
        "inputs": normal_values(arg_keys[0], (ROWS, SEQLEN, D), 1.0, 6.0, ((0, 8), (1, 4))),
        "segments": draw_segments(jax.random.fold_in(arg_keys[10], 71), 0),
        "cotangent": normal_values(arg_keys[2], (ROWS, SEQLEN, D), 1.0, 6.0, ((0, 8), (1, 4))),
        "gain_attn": jnp.clip(1.0 + 0.18 * jax.random.normal(arg_keys[3], (D,), jnp.float32), 0.1, 1.9),
        "w_qkv": normal_values(arg_keys[4], (D, 3 * D), D ** -0.5, 0.25, ((0, 32),), jnp.float32),
        "w_out": normal_values(arg_keys[5], (D, D), (D // 64) ** -0.5, 2.0, ((0, 32),), jnp.float32),
        "gain_mix": jnp.clip(1.0 + 0.18 * jax.random.normal(arg_keys[6], (D,), jnp.float32), 0.1, 1.9),
        "w_control": normal_values(arg_keys[7], (EXPERTS, D), (2 * D) ** -0.5, 0.1875, ((1, 32),), jnp.float32),
        "w_expand": normal_values(arg_keys[8], (EXPERTS, D, FF), (max(D // 256, 1)) ** -0.5, 4.0, ((1, 32),), jnp.float32),
        "w_shrink": normal_values(arg_keys[9], (EXPERTS, FF, D), (max(FF // 128, 1)) ** -0.5, 1.5, ((1, 32),), jnp.float32),
    }


@jax.custom_vjp
def low(v):
    return lax.optimization_barrier(v.astype(jnp.bfloat16)).astype(jnp.float32)

@jax.custom_vjp
def low_back(v):
    return v

def low_keep(v):
    return (low(v), None)

def low_pass(kept, grad):
    return (grad,)

def back_keep(v):
    return (v, None)

def back_low(kept, grad):
    return (low(grad),)
low.defvjp(low_keep, low_pass)
low_back.defvjp(back_keep, back_low)
highest = lax.Precision.HIGHEST
masked_score = -1e+30

def layer_norm(values):
    center = values - lax.optimization_barrier(jnp.mean(values, axis=-1, keepdims=True))
    return center * lax.rsqrt(lax.optimization_barrier(jnp.mean(center * center, axis=-1, keepdims=True)) + 1e-05)

def attend_row(query_heads, key_heads, value_heads, row_segments):
    score_scale = 1.0 / math.sqrt(HEAD_DIM)
    scores = jnp.einsum('qhd,khd->hqk', query_heads, key_heads, precision=highest) * score_scale
    scores = low_back(scores)
    places = jnp.arange(SEQLEN)
    allowed = (places[None, :] <= places[:, None]) & (row_segments[None, :] == row_segments[:, None])
    scores = jnp.where(allowed[None], scores, masked_score)
    probabilities = low(jax.nn.softmax(scores, axis=-1))
    return jnp.einsum('hqk,khd->qhd', probabilities, value_heads, precision=highest)

def block(inputs, gain_attn, w_qkv, w_out, gain_mix, w_control, w_expand, w_shrink, segments):
    first_in = low(layer_norm(inputs) * low(gain_attn))
    projected = jnp.einsum('rsd,de->rse', first_in, low(w_qkv), precision=highest)
    projected = low(low_back(projected))
    query_heads = projected[..., :D].reshape(ROWS, SEQLEN, HEADS, HEAD_DIM)
    key_heads = projected[..., D:2 * D].reshape(ROWS, SEQLEN, HEADS, HEAD_DIM)
    value_heads = projected[..., 2 * D:].reshape(ROWS, SEQLEN, HEADS, HEAD_DIM)
    attended = lax.map(jax.checkpoint(lambda row_item: attend_row(*row_item)), (query_heads, key_heads, value_heads, segments))
    attended = low(low_back(attended.reshape(ROWS, SEQLEN, D)))
    middle = inputs + low_back(jnp.einsum('rsd,de->rse', attended, low(w_out), precision=highest))
    second_in = low(low_back(layer_norm(middle) * low(gain_mix)))
    tokens = second_in.reshape(ROWS // GROUP, GROUP, SEQLEN, D)
    logits = jnp.einsum('gtsd,ed->gtse', tokens, low(w_control), precision=highest)
    weights = jax.nn.softmax(logits, axis=1)
    mixed_tokens = jnp.einsum('gtse,gtsd->gsed', low(weights), tokens, precision=highest)
    mixed_tokens = low(low_back(mixed_tokens))
    hidden_pre = low_back(jnp.einsum('gsed,edf->gsef', mixed_tokens, low(w_expand), precision=highest))
    hidden = low(jax.nn.gelu(hidden_pre, approximate=True))
    results = low_back(jnp.einsum('gsef,efd->gsed', hidden, low(w_shrink), precision=highest))
    spread = lax.optimization_barrier(jnp.sum(weights[..., None] * results[:, None], axis=3))
    spread = low(low_back(spread.reshape(ROWS, SEQLEN, D)))
    return middle + spread

def reference(inputs, segments, cotangent, gain_attn, w_qkv, w_out, gain_mix, w_control, w_expand, w_shrink):

    def forward(layer_in, gain_one, proj_in, proj_out, gain_two, control, expand, shrink):
        return block(layer_in, gain_one, proj_in, proj_out, gain_two, control, expand, shrink, segments)
    primal, pullback = jax.vjp(forward, inputs.astype(jnp.float32), gain_attn, w_qkv, w_out, gain_mix, w_control, w_expand, w_shrink)
    gradients = pullback(cotangent.astype(jnp.float32))
    return (primal.astype(jnp.bfloat16), gradients[0].astype(jnp.bfloat16), gradients[1], gradients[2], gradients[3], gradients[4], gradients[5], gradients[6], gradients[7])
```

```python
import functools
import math

import jax
import jax.numpy as jnp
from jax import lax
from jax.experimental import pallas as pl
from jax.experimental.pallas import tpu as pltpu
from jax.sharding import Mesh
from jax.sharding import PartitionSpec as P

HEADS = 8
GROUP = 32
BLOCK = 256
LANES = 128
VMEM_LIMIT = 60 * 1024 * 1024

LOG2E = math.log2(math.e)
LN2 = math.log(2.0)
BIG = 1e30

bf16 = jnp.bfloat16
f32 = jnp.float32

NN = (((1,), (0,)), ((), ()))
NT = (((1,), (1,)), ((), ()))
TN = (((0,), (0,)), ((), ()))


def dot(a, b, dims=NN):
    return lax.dot_general(a, b, dims, preferred_element_type=f32)


def normalize(values):
    center = values - jnp.mean(values, axis=-1, keepdims=True)
    scaled = lax.rsqrt(jnp.mean(center * center, axis=-1, keepdims=True) + 1e-05)
    return center * scaled, scaled


def norm_back(incoming, normed, scaled):
    return scaled * (
        incoming
        - jnp.mean(incoming, axis=-1, keepdims=True)
        - normed * jnp.mean(incoming * normed, axis=-1, keepdims=True)
    )


def split3(value):
    high = value.astype(bf16).astype(f32)
    rest = value - high
    mid = rest.astype(bf16).astype(f32)
    low = (rest - mid).astype(bf16).astype(f32)
    return high, mid, low


def partner(value, axis, size, mask):
    return lax.ppermute(value, axis, [(i, i ^ mask) for i in range(size)])


def swap_slots(slots, axis):
    size = len(slots)
    return [slots[0]] + [partner(slots[j], axis, size, j) for j in range(1, size)]


def natural(slots, me):
    out = list(slots)
    bit = 1
    while bit < len(out):
        flip = (me & bit) != 0
        out = [jnp.where(flip, out[k ^ bit], out[k]) for k in range(len(out))]
        bit *= 2
    return out


def bits_of(sizes):
    bits = []
    for axis, size in sizes:
        mask = size // 2
        while mask:
            bits.append((axis, size, mask))
            mask //= 2
    return bits


def gather_rows(value, sizes):
    tail = value.shape
    depth = 0
    for axis, size, mask in bits_of(sizes):
        other = partner(value, axis, size, mask)
        high = (lax.axis_index(axis) & mask) != 0
        first, second = jnp.where(high, other, value), jnp.where(high, value, other)
        value = jnp.stack([first, second], axis=depth)
        depth += 1
    return value.reshape((-1,) + tail[1:])


def scatter_rows(value, sizes):
    bits = bits_of(sizes)
    rows = value.shape[0] >> len(bits)
    value = value.reshape((2,) * len(bits) + (rows,) + value.shape[1:])
    for depth in reversed(range(len(bits))):
        axis, size, mask = bits[depth]
        high = ((lax.axis_index(axis) & mask) != 0).astype(jnp.int32)
        keep = lax.dynamic_index_in_dim(value, high, depth, keepdims=False)
        send = lax.dynamic_index_in_dim(value, 1 - high, depth, keepdims=False)
        value = keep.astype(f32) + partner(send.astype(bf16), axis, size, mask).astype(f32)
    return value


def call(kernel, name, grid, in_specs, outs, scratch, args, flops, bytes_accessed):
    return pl.pallas_call(
        kernel,
        grid_spec=pltpu.PrefetchScalarGridSpec(
            num_scalar_prefetch=1,
            grid=grid,
            in_specs=in_specs,
            out_specs=[spec for spec, _, _ in outs],
            scratch_shapes=[pltpu.VMEM(shape, dtype) for shape, dtype in scratch],
        ),
        out_shape=[jax.ShapeDtypeStruct(shape, dtype) for _, shape, dtype in outs],
        compiler_params=pltpu.CompilerParams(vmem_limit_bytes=VMEM_LIMIT),
        cost_estimate=pl.CostEstimate(
            flops=flops, bytes_accessed=bytes_accessed, transcendentals=0
        ),
        name=name,
    )(*args)


def per_row(*shape):
    return pl.BlockSpec((1,) + shape, lambda r, me: (r,) + (0,) * len(shape))


def whole(*shape):
    return pl.BlockSpec(shape, lambda r, me: (0,) * len(shape))


def causal_bias():
    key = lax.broadcasted_iota(jnp.int32, (BLOCK, BLOCK), 0)
    query = lax.broadcasted_iota(jnp.int32, (BLOCK, BLOCK), 1)
    return jnp.where(key <= query, 0.0, -BIG).astype(f32)


def key_features(segment_row, length):
    row = lax.broadcasted_iota(jnp.int32, (LANES, length), 0)
    marks = (row == segment_row) | ((row >= 7) & (row < 10))
    return jnp.where(marks, 1.0, 0.0).astype(f32).T.astype(bf16)


def query_features(segment_row, length):
    row = lax.broadcasted_iota(jnp.int32, (16, length), 0)
    return jnp.where((row < 7) & (row != segment_row), -BIG, 0.0).astype(f32)


def padded_head(head, features, odd):
    blank = jnp.zeros_like(head)
    rest = jnp.zeros((LANES - 16, head.shape[1]), bf16)
    both = [blank, head] if odd else [head, blank]
    return jnp.concatenate(both + [features, rest], axis=0)


def attend_kernel(slot_count, *refs):
    me_ref = refs[0]
    x_refs = refs[1 : 1 + slot_count]
    seg_ref, gain_ref, w_ref = refs[1 + slot_count : 4 + slot_count]
    rest = refs[4 + slot_count :]
    att_refs = rest[:slot_count]
    qt_ref, k_ref, v_ref, q_ref, ot_ref, lse_ref = rest[slot_count : slot_count + 6]
    w_t, k_aux, q_aux, v_t, causal = rest[slot_count + 6 :]
    width = w_ref.shape[0]
    piece = x_refs[0].shape[1]
    length = piece * slot_count
    me = me_ref[0]
    score_scale = LOG2E / math.sqrt(width // HEADS)

    @pl.when(pl.program_id(0) == 0)
    def _():
        w_t[:width] = w_ref[:, :width].T
        w_t[width:] = w_ref[:, 2 * width :].T
        causal[...] = causal_bias()

    segment_row = seg_ref[0]
    q_aux[...] = query_features(segment_row, length)
    k_aux[...] = key_features(segment_row, length)
    gain = gain_ref[...]
    for j in range(slot_count):
        place = pl.ds(pl.multiple_of((me ^ j) * piece, piece), piece)
        normed, _ = normalize(x_refs[j][0].astype(f32))
        first_in = (normed * gain).astype(bf16)
        projected = dot(first_in, w_ref[...])
        q_ref[0, place] = (projected[:, :width] * score_scale).astype(bf16)
        k_ref[0, place] = projected[:, width : 2 * width].astype(bf16)
        v_ref[0, place] = projected[:, 2 * width :].astype(bf16)
        turned = dot(w_t[...], first_in, NT)
        qt_ref[0, :, place] = (turned[:width] * score_scale).astype(bf16)
        v_t[:, place] = turned[width:].astype(bf16)

    def head_pair(pair, carry):
        base = pl.multiple_of(pair * LANES, LANES)
        for odd in range(2):
            rows = pl.ds(pl.multiple_of(pair * LANES + odd * 64, 64), 64)
            for qb in range(length // BLOCK):
                queries = pl.ds(qb * BLOCK, BLOCK)
                feats = q_aux[:, queries].astype(bf16)
                query = padded_head(qt_ref[0, rows, queries], feats, odd)
                scores = []
                for kb in range(qb + 1):
                    keys = pl.ds(kb * BLOCK, BLOCK)
                    key = jnp.concatenate([k_ref[0, keys, pl.ds(base, LANES)], k_aux[keys]], axis=1)
                    score = dot(key, query)
                    scores.append(score + causal[...] if kb == qb else score)
                top = functools.reduce(
                    jnp.maximum, [jnp.max(score, axis=0, keepdims=True) for score in scores]
                )
                total = jnp.zeros((1, BLOCK), f32)
                out = jnp.zeros((64, BLOCK), f32)
                for kb in range(qb + 1):
                    prob = jnp.exp2(scores[kb] - top)
                    total = total + jnp.sum(prob, axis=0, keepdims=True)
                    out = out + dot(v_t[rows, pl.ds(kb * BLOCK, BLOCK)], prob.astype(bf16))
                ot_ref[0, rows, queries] = (out / total).astype(bf16)
                lse_ref[0, pl.ds(pair * 2 + odd, 1), queries] = top + jnp.log2(total)
        return carry

    lax.fori_loop(0, HEADS // 2, head_pair, 0)
    for j in range(slot_count):
        place = pl.ds(pl.multiple_of((me ^ j) * piece, piece), piece)
        att_refs[j][0] = ot_ref[0, :, place].T


def attend(me, x_slots, segment_rows, gain, w_qkv):
    slot_count = len(x_slots)
    rows, piece, width = x_slots[0].shape
    length = piece * slot_count
    outs = [(per_row(piece, width), (rows, piece, width), bf16)] * slot_count + [
        (per_row(width, length), (rows, width, length), bf16),
        (per_row(length, width), (rows, length, width), bf16),
        (per_row(length, width), (rows, length, width), bf16),
        (per_row(length, width), (rows, length, width), bf16),
        (per_row(width, length), (rows, width, length), bf16),
        (per_row(HEADS, length), (rows, HEADS, length), f32),
    ]
    result = call(
        functools.partial(attend_kernel, slot_count),
        "attend",
        (rows,),
        [per_row(piece, width)] * slot_count
        + [per_row(1, length), whole(1, width), whole(width, 3 * width)],
        outs,
        [
            ((2 * width, width), bf16),
            ((length, LANES), bf16),
            ((16, length), f32),
            ((width, length), bf16),
            ((BLOCK, BLOCK), f32),
        ],
        (me, *x_slots, segment_rows, gain, w_qkv),
        rows * length * width * 12000,
        rows * length * width * 16,
    )
    return result[:slot_count], result[slot_count:]


def attend_back_kernel(slot_count, *refs):
    me_ref = refs[0]
    x_refs = refs[1 : 1 + slot_count]
    do_refs = refs[1 + slot_count : 1 + 2 * slot_count]
    rest = refs[1 + 2 * slot_count :]
    seg_ref, gain_ref, w_ref, qt_ref, k_ref, v_ref, q_ref, ot_ref, lse_ref = rest[:9]
    gf_refs = rest[9 : 9 + slot_count]
    dw_ref = rest[9 + slot_count]
    (k_aux, q_aux, v_aux, causal, do, first_t, work_t, k_t, grads, prob, grad_score, delta) = rest[
        10 + slot_count :
    ]
    width = w_ref.shape[0]
    piece = x_refs[0].shape[1]
    length = piece * slot_count
    me = me_ref[0]
    row_id = pl.program_id(0)
    score_scale = 1.0 / math.sqrt(width // HEADS)

    @pl.when(row_id == 0)
    def _():
        causal[...] = causal_bias()
        lane = lax.broadcasted_iota(jnp.int32, (length, LANES), 1)
        v_aux[...] = jnp.where(lane < 3, 1.0, 0.0).astype(bf16)

    segment_row = seg_ref[0]
    q_aux[...] = query_features(segment_row, length)
    k_aux[...] = key_features(segment_row, length)
    gain = gain_ref[...]
    for j in range(slot_count):
        place = pl.ds(pl.multiple_of((me ^ j) * piece, piece), piece)
        normed, _ = normalize(x_refs[j][0].astype(f32))
        first_t[:, place] = (normed * gain).astype(bf16).T
        do[place] = do_refs[j][0]
        turned = do_refs[j][0].T
        work_t[:, place] = turned
        k_t[:, place] = k_ref[0, place].T
        product = turned.astype(f32) * ot_ref[0, :, place].astype(f32)
        delta[:, place] = jnp.sum(product.reshape(HEADS, width // HEADS, piece), axis=1)
    lane = lax.broadcasted_iota(jnp.int32, (1, LANES), 1)
    feature = lax.broadcasted_iota(jnp.int32, (16, BLOCK), 0)
    blocks = length // BLOCK

    def head_pair(pair, carry):
        base = pl.multiple_of(pair * LANES, LANES)
        for odd in range(2):
            rows = pl.ds(pl.multiple_of(pair * LANES + odd * 64, 64), 64)
            head = pl.ds(pair * 2 + odd, 1)
            for qb in range(blocks):
                queries = pl.ds(qb * BLOCK, BLOCK)
                a, b, c = split3(lse_ref[0, head, queries])
                feats = jnp.where(feature == 7, -a, q_aux[:, queries])
                feats = jnp.where(feature == 8, -b, jnp.where(feature == 9, -c, feats))
                query = padded_head(qt_ref[0, rows, queries], feats.astype(bf16), odd)
                a, b, c = split3(delta[head, queries])
                feats = jnp.where(feature == 0, -a, jnp.where(feature == 1, -b, 0.0))
                feats = jnp.where(feature == 2, -c, feats)
                grad = padded_head(work_t[rows, queries], feats.astype(bf16), odd)
                held = pl.ds(odd * length + qb * BLOCK, BLOCK)
                for kb in range(qb + 1):
                    keys = pl.ds(kb * BLOCK, BLOCK)
                    key = jnp.concatenate([k_ref[0, keys, pl.ds(base, LANES)], k_aux[keys]], axis=1)
                    score = dot(key, query)
                    if kb == qb:
                        score = score + causal[...]
                    value = jnp.concatenate(
                        [v_ref[0, keys, pl.ds(base, LANES)], v_aux[keys]], axis=1
                    )
                    grad_prob = dot(value, grad)
                    weight = jnp.exp2(score)
                    prob[keys, held] = weight.astype(bf16)
                    grad_score[keys, held] = (weight * grad_prob).astype(bf16)
                end = (qb + 1) * BLOCK
                grad_q = dot(k_t[rows, 0:end], grad_score[0:end, held])
                work_t[rows, queries] = (grad_q * score_scale).astype(bf16)
        for kb in range(blocks):
            keys = pl.ds(kb * BLOCK, BLOCK)
            later = pl.ds(kb * BLOCK, length - kb * BLOCK)
            grad_v = jnp.zeros((BLOCK, LANES), f32)
            grad_k = jnp.zeros((BLOCK, LANES), f32)
            for odd in range(2):
                mine = (lane >= 64) if odd else (lane < 64)
                held = pl.ds(odd * length + kb * BLOCK, length - kb * BLOCK)
                zero = jnp.zeros((), bf16)
                grad = jnp.where(mine, do[later, pl.ds(base, LANES)], zero)
                query = jnp.where(mine, q_ref[0, later, pl.ds(base, LANES)], zero)
                grad_v = grad_v + dot(prob[keys, held], grad)
                grad_k = grad_k + dot(grad_score[keys, held], query)
            grads[keys, pl.ds(pl.multiple_of(width + pair * LANES, LANES), LANES)] = (
                grad_k * LN2
            ).astype(bf16)
            grads[keys, pl.ds(pl.multiple_of(2 * width + pair * LANES, LANES), LANES)] = (
                grad_v.astype(bf16)
            )
        return carry

    lax.fori_loop(0, HEADS // 2, head_pair, 0)
    for j in range(slot_count):
        place = pl.ds(pl.multiple_of((me ^ j) * piece, piece), piece)
        grads[place, :width] = work_t[:, place].T
        gf_refs[j][0] = dot(grads[place], w_ref[...], NT).astype(bf16)
    update = dot(first_t[...], grads[...])

    @pl.when(row_id == 0)
    def _():
        dw_ref[...] = update

    @pl.when(row_id > 0)
    def _():
        dw_ref[...] += update


def attend_back(me, x_slots, do_slots, segment_rows, gain, w_qkv, saved):
    slot_count = len(x_slots)
    rows, piece, width = x_slots[0].shape
    length = piece * slot_count
    outs = [(per_row(piece, width), (rows, piece, width), bf16)] * slot_count + [
        (whole(width, 3 * width), (width, 3 * width), f32)
    ]
    result = call(
        functools.partial(attend_back_kernel, slot_count),
        "attend_back",
        (rows,),
        [per_row(piece, width)] * (2 * slot_count)
        + [per_row(1, length), whole(1, width), whole(width, 3 * width)]
        + [
            per_row(width, length),
            per_row(length, width),
            per_row(length, width),
            per_row(length, width),
            per_row(width, length),
            per_row(HEADS, length),
        ],
        outs,
        [
            ((length, LANES), bf16),
            ((16, length), f32),
            ((length, LANES), bf16),
            ((BLOCK, BLOCK), f32),
            ((length, width), bf16),
            ((width, length), bf16),
            ((width, length), bf16),
            ((width, length), bf16),
            ((length, 3 * width), bf16),
            ((length, 2 * length), bf16),
            ((length, 2 * length), bf16),
            ((HEADS, length), f32),
        ],
        (me, *x_slots, *do_slots, segment_rows, gain, w_qkv, *saved),
        rows * length * width * 20000,
        rows * length * width * 16,
    )
    return result[:slot_count], result[slot_count]


def middle_of(att_refs, inputs_ref, w_out, me):
    rows, piece, width = att_refs[0].shape
    attended = jnp.concatenate([ref[...] for ref in att_refs], axis=0)
    attended = attended.reshape(-1, width)
    origin = jnp.concatenate(
        [inputs_ref[pl.ds((me ^ j) * rows, rows)] for j in range(len(att_refs))], axis=0
    ).reshape(-1, width)
    return attended, origin.astype(f32) + dot(attended, w_out)


def diagonal(piece):
    place = lax.broadcasted_iota(jnp.int32, (piece, LANES), 0)
    lane = lax.broadcasted_iota(jnp.int32, (piece, LANES), 1)
    return place == lane % piece, lane // piece, lane


def mix_kernel(slot_count, experts, *refs):
    me_ref = refs[0]
    att_refs = refs[1 : 1 + slot_count]
    inputs_ref, cot_ref, w_out_ref, gain_ref, control_ref = refs[1 + slot_count : 6 + slot_count]
    rest = refs[6 + slot_count :]
    pay_refs = rest[:experts]
    second_ref, middle_ref = rest[experts:]
    rows, piece, width = att_refs[0].shape
    tokens = rows * slot_count
    me = me_ref[0]
    _, middle = middle_of(att_refs, inputs_ref, w_out_ref[...], me)
    normed, _ = normalize(middle)
    second = (normed * gain_ref[...]).astype(bf16)
    second_ref[...] = second.reshape(tokens, piece, width)
    middle_ref[...] = middle.reshape(tokens, piece, width)
    grad = jnp.concatenate(
        [cot_ref[pl.ds((me ^ j) * rows, rows)] for j in range(slot_count)], axis=0
    ).reshape(-1, width)
    logits = dot(second, control_ref[...], NT).reshape(tokens, piece, LANES)
    top = jnp.max(logits, axis=0)
    weights = jnp.exp(logits - top)
    total = jnp.sum(weights, axis=0)
    log_total = top + jnp.log(total)
    own, _, lane = diagonal(piece)
    weights = jnp.where(own, weights * (1.0 / total), 0.0)
    spread_out = weights.reshape(-1, LANES).astype(bf16)
    mixed = dot(spread_out, second, TN).astype(bf16)
    grad_results = dot(spread_out, grad, TN).astype(bf16)
    a, b, c = split3(log_total)
    for e in range(experts):
        mine = slice(e * piece, (e + 1) * piece)
        first = slice(e * piece, e * piece + 1)
        stats = jnp.where(lane == 0, a[:, first], jnp.where(lane == 1, b[:, first], c[:, first]))
        pay_refs[e][:, :width] = mixed[mine]
        pay_refs[e][:, width : 2 * width] = grad_results[mine]
        pay_refs[e][:, 2 * width :] = stats.astype(bf16)


def mix(me, att_slots, inputs, cotangent, w_out, gain, control, experts):
    slot_count = len(att_slots)
    rows, positions, width = att_slots[0].shape
    tokens = rows * slot_count
    piece = LANES // experts
    span = pl.BlockSpec((tokens, piece, width), lambda b, me: (0, b, 0))
    pay = (
        pl.BlockSpec((piece, 2 * width + LANES), lambda b, me: (b, 0)),
        (positions, 2 * width + LANES),
        bf16,
    )
    result = call(
        functools.partial(mix_kernel, slot_count, experts),
        "mix",
        (positions // piece,),
        [pl.BlockSpec((rows, piece, width), lambda b, me: (0, b, 0))] * slot_count
        + [span, span, whole(width, width), whole(1, width), whole(LANES, width)],
        [pay] * experts
        + [
            (span, (tokens, positions, width), bf16),
            (span, (tokens, positions, width), f32),
        ],
        [],
        (me, *att_slots, inputs, cotangent, w_out, gain, control),
        tokens * positions * width * 4000,
        tokens * positions * width * 14,
    )
    return result[:experts], result[experts], result[experts + 1]


def expert_kernel(slot_count, *refs):
    pay_refs = refs[1 : 1 + slot_count]
    expand_ref, shrink_ref = refs[1 + slot_count : 3 + slot_count]
    back_ref, grad_expand_ref, grad_shrink_ref = refs[3 + slot_count : 6 + slot_count]
    mixed_acc, grad_acc, mixed_low, grad_low, result_acc, back_acc, stat = refs[6 + slot_count :]
    width = expand_ref.shape[0]
    step = pl.program_id(0)

    @pl.when(step == 0)
    def _():
        logs = []
        for j in range(slot_count):
            stats = pay_refs[j][:, 2 * width :].astype(f32)
            logs.append(stats[:, 0:1] + stats[:, 1:2] + stats[:, 2:3])
        top = functools.reduce(jnp.maximum, logs)
        total = functools.reduce(jnp.add, [jnp.exp(log - top) for log in logs])
        log_total = top + jnp.log(total)
        mixed, grad = 0.0, 0.0
        for j in range(slot_count):
            share = jnp.exp(logs[j] - log_total)
            mixed = mixed + share * pay_refs[j][:, :width].astype(f32)
            grad = grad + share * pay_refs[j][:, width : 2 * width].astype(f32)
        mixed_acc[...] = mixed
        grad_acc[...] = grad
        mixed_low[...] = mixed.astype(bf16)
        grad_low[...] = grad.astype(bf16)
        result_acc[...] = jnp.zeros_like(result_acc)
        back_acc[...] = jnp.zeros_like(back_acc)
        stat[...] = jnp.broadcast_to(log_total, stat.shape)

    mixed, grad = mixed_low[...], grad_low[...]
    expand, shrink = expand_ref[...], shrink_ref[...]
    value = dot(mixed, expand)
    coeff = math.sqrt(2.0 / math.pi)
    square = value * value
    turn = jnp.tanh(coeff * (value + 0.044715 * (square * value)))
    half = 0.5 * (1.0 + turn)
    hidden = (value * half).astype(bf16)
    slope = half + (0.5 * coeff) * value * (1.0 - turn * turn) * (1.0 + (3 * 0.044715) * square)
    result_acc[...] += dot(hidden, shrink)
    grad_pre = (dot(grad, shrink, NT) * slope).astype(bf16)
    back_acc[...] += dot(grad_pre, expand, NT)
    grad_expand_ref[...] = dot(mixed, grad_pre, TN).astype(bf16)
    grad_shrink_ref[...] = dot(hidden, grad, TN).astype(bf16)

    @pl.when(step == pl.num_programs(0) - 1)
    def _():
        results = result_acc[...].astype(bf16)
        back = back_acc[...].astype(bf16)
        back_ref[:, :width] = results
        back_ref[:, width : 2 * width] = back
        inner = jnp.sum(
            results.astype(f32) * grad_acc[...] + back.astype(f32) * mixed_acc[...],
            axis=-1,
            keepdims=True,
        )
        lane = lax.broadcasted_iota(jnp.int32, stat.shape, 1)
        a, b, c = split3(stat[...])
        d, e, f = split3(inner)
        stats = jnp.where(lane == 0, a, jnp.where(lane == 1, b, c))
        stats = jnp.where(lane < 3, stats, jnp.where(lane == 3, d, jnp.where(lane == 4, e, f)))
        back_ref[:, 2 * width :] = stats.astype(bf16)


def expert(me, pay_slots, expand, shrink):
    slot_count = len(pay_slots)
    groups, packed = pay_slots[0].shape
    width, hidden = expand.shape
    chunk = 512
    acc = ((groups, width), f32)
    low = ((groups, width), bf16)
    columns = pl.BlockSpec((width, chunk), lambda f, me: (0, f))
    lines = pl.BlockSpec((chunk, width), lambda f, me: (f, 0))
    return call(
        functools.partial(expert_kernel, slot_count),
        "expert",
        (hidden // chunk,),
        [whole(groups, packed)] * slot_count + [columns, lines],
        [
            (whole(groups, packed), (groups, packed), bf16),
            (columns, (width, hidden), bf16),
            (lines, (hidden, width), bf16),
        ],
        [acc, acc, low, low, acc, acc, ((groups, LANES), f32)],
        (me, *pay_slots, expand, shrink),
        groups * width * hidden * 24,
        width * hidden * 8,
    )


def unmix_kernel(slot_count, experts, *refs):
    me_ref = refs[0]
    ret_refs = refs[1 : 1 + experts]
    att_refs = refs[1 + experts : 1 + experts + slot_count]
    rest = refs[1 + experts + slot_count :]
    second_ref, middle_ref, cot_ref, w_out_ref, gain_ref, control_ref = rest[:6]
    out_ref, grad_middle_ref = rest[6:8]
    back_refs = rest[8 : 8 + slot_count]
    grad_out_ref, grad_control_ref, grad_gain_ref = rest[8 + slot_count :]
    rows, piece, width = att_refs[0].shape
    tokens = rows * slot_count
    me = me_ref[0]

    @pl.when(pl.program_id(0) == 0)
    def _():
        grad_out_ref[...] = jnp.zeros_like(grad_out_ref)
        grad_control_ref[...] = jnp.zeros_like(grad_control_ref)
        grad_gain_ref[...] = jnp.zeros_like(grad_gain_ref)

    second = second_ref[...].reshape(-1, width)
    middle = middle_ref[...].reshape(-1, width)
    cot = jnp.concatenate(
        [cot_ref[pl.ds((me ^ j) * rows, rows)] for j in range(slot_count)], axis=0
    ).reshape(-1, width)
    own, group, _ = diagonal(piece)
    log_total = jnp.zeros((piece, LANES), f32)
    inner = jnp.zeros((piece, LANES), f32)
    for e in range(experts):
        stats = ret_refs[e][:, 2 * width :].astype(f32)
        mine = group == e
        log_total = jnp.where(mine, stats[:, 0:1] + stats[:, 1:2] + stats[:, 2:3], log_total)
        inner = jnp.where(mine, stats[:, 3:4] + stats[:, 4:5] + stats[:, 5:6], inner)
    results = jnp.concatenate([ref[:, :width] for ref in ret_refs], axis=0)
    back = jnp.concatenate([ref[:, width : 2 * width] for ref in ret_refs], axis=0)
    control = control_ref[...]
    logits = dot(second, control, NT).reshape(tokens, piece, LANES)
    weights = jnp.where(own, jnp.exp(logits - log_total), 0.0)
    low = weights.reshape(-1, LANES).astype(bf16)
    output = (middle + dot(low, results).astype(bf16).astype(f32)).astype(bf16)
    grad_weights = (dot(cot, results, NT) + dot(second, back, NT)).reshape(tokens, piece, LANES)
    grad_logits = (weights * (grad_weights - inner)).reshape(-1, LANES).astype(bf16)
    grad_second = dot(low, back) + dot(grad_logits, control)
    grad_second = grad_second.astype(bf16).astype(f32)
    grad_control_ref[...] += dot(grad_logits, second, TN)
    normed, scaled = normalize(middle)
    product = (grad_second * normed).reshape(-1, 8, width)
    grad_gain_ref[...] += jnp.sum(product, axis=0)
    grad_middle = cot.astype(f32) + norm_back(grad_second * gain_ref[...], normed, scaled)
    grad_middle = grad_middle.astype(bf16)
    grad_attended = dot(grad_middle, w_out_ref[...], NT).astype(bf16)
    output = output.reshape(tokens, piece, width)
    grad_attended = grad_attended.reshape(tokens, piece, width)
    grad_middle_ref[...] = grad_middle.reshape(tokens, piece, width)
    for j in range(slot_count):
        mine = slice(j * rows, (j + 1) * rows)
        out_ref[pl.ds((me ^ j) * rows, rows)] = output[mine]
        back_refs[j][...] = grad_attended[mine]
    attended = jnp.concatenate([ref[...] for ref in att_refs], axis=0).reshape(-1, width)
    grad_out_ref[...] += dot(attended, grad_middle, TN)


def unmix(me, ret_slots, att_slots, second, middle, cotangent, w_out, gain, control):
    slot_count, experts = len(att_slots), len(ret_slots)
    rows, positions, width = att_slots[0].shape
    tokens = rows * slot_count
    piece = LANES // experts
    span = pl.BlockSpec((tokens, piece, width), lambda b, me: (0, b, 0))
    part = pl.BlockSpec((rows, piece, width), lambda b, me: (0, b, 0))
    result = call(
        functools.partial(unmix_kernel, slot_count, experts),
        "unmix",
        (positions // piece,),
        [pl.BlockSpec((piece, 2 * width + LANES), lambda b, me: (b, 0))] * experts
        + [part] * slot_count
        + [span, span, span, whole(width, width), whole(1, width), whole(LANES, width)],
        [
            (span, (tokens, positions, width), bf16),
            (span, (tokens, positions, width), bf16),
        ]
        + [(part, (rows, positions, width), bf16)] * slot_count
        + [
            (whole(width, width), (width, width), f32),
            (whole(LANES, width), (LANES, width), f32),
            (whole(8, width), (8, width), f32),
        ],
        [],
        (me, *ret_slots, *att_slots, second, middle, cotangent, w_out, gain, control),
        tokens * positions * width * 6000,
        tokens * positions * width * 20,
    )
    output, grad_middle = result[:2]
    return output, grad_middle, result[2 : 2 + slot_count], result[2 + slot_count :]


def finish_kernel(slot_count, *refs):
    me_ref = refs[0]
    gf_refs = refs[1 : 1 + slot_count]
    inputs_ref, grad_middle_ref, gain_ref, out_ref = refs[1 + slot_count :]
    rows = gf_refs[0].shape[0]
    me = me_ref[0]
    for j in range(slot_count):
        place = pl.ds((me ^ j) * rows, rows)
        normed, scaled = normalize(inputs_ref[place].astype(f32))
        grad = norm_back(gf_refs[j][...].astype(f32) * gain_ref[...], normed, scaled)
        grad = grad + grad_middle_ref[j * rows : (j + 1) * rows].astype(f32)
        out_ref[place] = grad.astype(bf16)


def finish(me, gf_slots, inputs, grad_middle, gain):
    slot_count = len(gf_slots)
    rows, positions, width = gf_slots[0].shape
    tokens = rows * slot_count
    piece = 64
    span = pl.BlockSpec((tokens, piece, width), lambda b, me: (0, b, 0))
    part = pl.BlockSpec((rows, piece, width), lambda b, me: (0, b, 0))
    return call(
        functools.partial(finish_kernel, slot_count),
        "finish",
        (positions // piece,),
        [part] * slot_count + [span, span, whole(1, width)],
        [(span, (tokens, positions, width), bf16)],
        [],
        (me, *gf_slots, inputs, grad_middle, gain),
        tokens * positions * width * 40,
        tokens * positions * width * 8,
    )[0]


def on_device(
    sizes,
    inputs,
    segments,
    cotangent,
    gain_attn,
    w_qkv,
    w_out,
    gain_mix,
    w_control,
    w_expand,
    w_shrink,
):
    groups, members, slots = sizes
    local_rows, positions, width = inputs.shape
    experts = w_expand.shape[0]
    rows = local_rows // slots
    place = (("gq", groups), ("gi", members), ("seq", slots))
    owners = (("gq", groups), ("seq", slots))
    seq_me = lax.axis_index("seq")
    member = lax.axis_index("gi")
    me = seq_me.astype(jnp.int32).reshape(1)

    def row_parts(array):
        return [
            lax.dynamic_slice_in_dim(array, (seq_me ^ j) * rows, rows, axis=0) for j in range(slots)
        ]

    x_slots = swap_slots(row_parts(inputs), "seq")
    segment_rows = jnp.concatenate(natural(swap_slots(row_parts(segments), "seq"), seq_me), axis=1)
    segment_rows = segment_rows[:, None, :]

    small = jnp.concatenate([gain_attn[None], gain_mix[None], w_control], axis=0)
    small = jnp.pad(jnp.transpose(small), ((0, 0), (0, LANES - 2 - experts)))
    packed = jnp.concatenate([w_qkv, w_out, small], axis=1).astype(bf16)
    packed = gather_rows(packed, place)
    proj_in, proj_out = packed[:, : 3 * width], packed[:, 3 * width : 4 * width]
    vectors = jnp.transpose(packed[:, 4 * width :])
    gain_one = vectors[0:1].astype(f32)
    gain_two = vectors[1:2].astype(f32)
    control = natural([vectors[2 + e : 3 + e] for e in range(experts)], member)
    control = jnp.concatenate(
        [jnp.broadcast_to(c, (LANES // experts, width)) for c in control], axis=0
    )

    def to_owner(array):
        array = array.astype(bf16)
        parts = [lax.dynamic_index_in_dim(array, member ^ j, 0, keepdims=False) for j in range(members)]
        array = jnp.stack(natural(swap_slots(parts, "gi"), member))
        array = lax.all_gather(array, ("gq", "seq"), axis=0)
        array = array.reshape((groups, slots) + array.shape[1:])
        array = jnp.swapaxes(array, 1, 2)
        return array.reshape(-1, array.shape[-1])

    expand, shrink = to_owner(w_expand), to_owner(w_shrink)

    att_slots, saved = attend(me, x_slots, segment_rows, gain_one, proj_in)
    att_slots = swap_slots(att_slots, "seq")
    pay_slots, second, middle = mix(
        me, att_slots, inputs, cotangent, proj_out, gain_two, control, experts
    )
    pay_slots = swap_slots(pay_slots, "gi")
    back, grad_expand, grad_shrink = expert(me, pay_slots, expand, shrink)
    ret_slots = swap_slots([back] * members, "gi")
    output, grad_middle, do_slots, sums = unmix(
        me, ret_slots, att_slots, second, middle, cotangent, proj_out, gain_two, control
    )
    grad_out, grad_control, grad_gain = sums

    do_slots = swap_slots(do_slots, "seq")
    gf_slots, grad_in = attend_back(me, x_slots, do_slots, segment_rows, gain_one, proj_in, saved)
    gf_slots = swap_slots(gf_slots, "seq")
    grad_inputs = finish(me, gf_slots, inputs, grad_middle, gain_one)

    def to_places(array):
        lines = array.shape[0] // (groups * members * slots)
        array = array.reshape(groups, members, slots, lines, array.shape[1])
        array = jnp.swapaxes(array, 1, 2).reshape(groups * slots, members, lines, array.shape[-1])
        array = lax.psum_scatter(array, ("gq", "seq"), scatter_dimension=0, tiled=True)[0]
        parts = [lax.dynamic_index_in_dim(array, member ^ j, 0, keepdims=False) for j in range(members)]
        return jnp.stack(natural(swap_slots(parts, "gi"), member)).astype(f32)

    grad_control = grad_control.reshape(experts, LANES // experts, width).sum(axis=1)
    grad_control = jnp.concatenate(
        natural([grad_control[e : e + 1] for e in range(experts)], member), axis=0
    )
    small = jnp.concatenate([grad_gain.sum(axis=0, keepdims=True), grad_control], axis=0)
    small = jnp.pad(jnp.transpose(small), ((0, 0), (0, LANES - 1 - experts)))
    grad_out = scatter_rows(jnp.concatenate([grad_out, small], axis=1), place)
    small = jnp.transpose(grad_out[:, width:])
    grad_in = scatter_rows(grad_in, place)
    weighted = jnp.sum(grad_in * w_qkv.astype(bf16).astype(f32), axis=1)
    return (
        output,
        grad_inputs,
        weighted / gain_attn.astype(bf16).astype(f32),
        grad_in,
        grad_out[:, :width],
        small[0],
        small[1 : 1 + experts],
        to_places(grad_expand),
        to_places(grad_shrink),
    )


def solution(mesh):
    dp_count, seq_count = mesh.shape["dp"], mesh.shape["seq"]

    def run(inputs, *args):
        members = GROUP * dp_count // inputs.shape[0]
        sizes = (dp_count // members, members, seq_count)
        fine = Mesh(mesh.devices.reshape(sizes), ("gq", "gi", "seq"))
        dp, both = ("gq", "gi"), ("gq", "gi", "seq")
        return jax.shard_map(
            functools.partial(on_device, sizes),
            mesh=fine,
            in_specs=(
                P(dp, "seq", None),
                P(dp, "seq"),
                P(dp, "seq", None),
                P(both),
                P(both, None),
                P(both, None),
                P(both),
                P(None, both),
                P(None, both, None),
                P(None, both, None),
            ),
            out_specs=(
                P(dp, "seq", None),
                P(dp, "seq", None),
                P(both),
                P(both, None),
                P(both, None),
                P(both),
                P(None, both),
                P(None, both, None),
                P(None, both, None),
            ),
            check_vma=False,
        )(inputs, *args)

    return run
```

```python
import functools
import math

import jax
import jax.numpy as jnp
from jax import lax
from jax.experimental import pallas as pl
from jax.experimental.pallas import tpu as pltpu
from jax.sharding import Mesh
from jax.sharding import PartitionSpec as P

HEADS = 8
GROUP = 32
BLOCK = 256
LANES = 128
MARKS = 16
VMEM_LIMIT = 60 * 1024 * 1024

LOG2E = math.log2(math.e)
LN2 = math.log(2.0)
BIG = 1e30

bf16 = jnp.bfloat16
f32 = jnp.float32

NN = (((1,), (0,)), ((), ()))
NT = (((1,), (1,)), ((), ()))
TN = (((0,), (0,)), ((), ()))


def dot(a, b, dims=NN):
    return lax.dot_general(a, b, dims, preferred_element_type=f32)


def normalize(values):
    center = values - jnp.mean(values, axis=-1, keepdims=True)
    scaled = lax.rsqrt(jnp.mean(center * center, axis=-1, keepdims=True) + 1e-05)
    return center * scaled, scaled


def norm_back(incoming, normed, scaled):
    return scaled * (
        incoming
        - jnp.mean(incoming, axis=-1, keepdims=True)
        - normed * jnp.mean(incoming * normed, axis=-1, keepdims=True)
    )


def split3(value):
    high = value.astype(bf16).astype(f32)
    rest = value - high
    mid = rest.astype(bf16).astype(f32)
    low = (rest - mid).astype(bf16).astype(f32)
    return high, mid, low


def partner(value, axis, size, mask):
    return lax.ppermute(value, axis, [(i, i ^ mask) for i in range(size)])


def swap_slots(slots, axis):
    size = len(slots)
    return [slots[0]] + [partner(slots[j], axis, size, j) for j in range(1, size)]


def natural(slots, me):
    out = list(slots)
    bit = 1
    while bit < len(out):
        flip = (me & bit) != 0
        out = [jnp.where(flip, out[k ^ bit], out[k]) for k in range(len(out))]
        bit *= 2
    return out


def bits_of(sizes):
    bits = []
    for axis, size in sizes:
        mask = size // 2
        while mask:
            bits.append((axis, size, mask))
            mask //= 2
    return bits


def named(bit):
    axis, _, mask = bit
    return "core" if axis == "seq" and mask == 1 else axis


class Steps:
    def __init__(self, value, sizes, order):
        self.order = [bit for axis in order for bit in reversed(bits_of(sizes)) if named(bit) == axis]
        self.value = value

    def steps(self, axis):
        while self.order and named(self.order[0]) == axis:
            self.step(self.order.pop(0))
        return self

    def finish(self):
        while self.order:
            self.step(self.order.pop(0))
        return self.value


class Doubling(Steps):
    def __init__(self, value, sizes, order, inner=0):
        super().__init__(value, sizes, order)
        self.inner = inner
        self.place = bits_of(sizes)
        self.have = []

    def step(self, bit):
        axis, size, mask = bit
        depth = sum(self.place.index(other) < self.place.index(bit) for other in self.have)
        depth += self.inner if axis == "seq" else 0
        other = partner(self.value, axis, size, mask)
        high = (lax.axis_index(axis) & mask) != 0
        first = jnp.where(high, other, self.value)
        second = jnp.where(high, self.value, other)
        self.value = jnp.stack([first, second], axis=depth)
        self.have.append(bit)

    def at_once(self, axis):
        bits = [bit for bit in self.place if bit[0] == axis]
        self.order = [bit for bit in self.order if bit[0] != axis]
        depth = sum(self.place.index(other) < self.place.index(bits[0]) for other in self.have)
        depth += self.inner if axis == "seq" else 0
        slots = natural(swap_slots([self.value] * 2 ** len(bits), axis), lax.axis_index(axis))
        shape = self.value.shape
        value = jnp.stack(slots, axis=depth)
        self.value = value.reshape(shape[:depth] + (2,) * len(bits) + shape[depth:])
        self.have += bits


class Halving(Steps):
    def __init__(self, value, sizes, order, inner=0):
        super().__init__(value, sizes, order)
        self.left = [bit for bit in bits_of(sizes) if bit in self.order]
        self.inner = inner

    def step(self, bit):
        depth = self.left.index(bit)
        self.left.pop(depth)
        axis, size, mask = bit
        depth += self.inner if axis == "seq" else 0
        high = ((lax.axis_index(axis) & mask) != 0).astype(jnp.int32)
        keep = lax.dynamic_index_in_dim(self.value, high, depth, keepdims=False)
        send = lax.dynamic_index_in_dim(self.value, 1 - high, depth, keepdims=False)
        other = partner(send.astype(bf16), axis, size, mask)
        self.value = keep.astype(f32) + other.astype(f32)


hold = lax.optimization_barrier


def together(values, *sums):
    values, held = lax.optimization_barrier((values, [item.value for item in sums]))
    for item, value in zip(sums, held):
        item.value = value
    return values


def call(kernel, name, grid, in_specs, outs, scratch, args, micros, aliases=None):
    return pl.pallas_call(
        kernel,
        grid_spec=pltpu.PrefetchScalarGridSpec(
            num_scalar_prefetch=1,
            grid=grid,
            in_specs=in_specs,
            out_specs=[spec for spec, _, _ in outs],
            scratch_shapes=[pltpu.VMEM(shape, dtype) for shape, dtype in scratch],
        ),
        out_shape=[jax.ShapeDtypeStruct(shape, dtype) for _, shape, dtype in outs],
        input_output_aliases=aliases or {},
        compiler_params=pltpu.CompilerParams(vmem_limit_bytes=VMEM_LIMIT),
        cost_estimate=pl.CostEstimate(
            flops=int(micros * 1e9), bytes_accessed=1 << 20, transcendentals=0
        ),
        name=name,
    )(*args)


def per_row(*shape):
    return pl.BlockSpec((1,) + shape, lambda r, me: (r,) + (0,) * len(shape))


def whole(*shape):
    return pl.BlockSpec(shape, lambda r, me: (0,) * len(shape))


def by_core(me, pairs):
    odd = me % 2 == 1
    first, second = pairs[:, 0], pairs[:, 1]
    return jnp.where(odd, second, first), jnp.where(odd, first, second)


def causal_bias(step=LANES):
    rows = LANES + step * (BLOCK // LANES - 1)
    key = lax.broadcasted_iota(jnp.int32, (rows, BLOCK), 0)
    query = lax.broadcasted_iota(jnp.int32, (rows, BLOCK), 1)
    query = query + (query // LANES) * (step - LANES)
    return jnp.where(key <= query, 0.0, -BIG).astype(f32)


def key_features(segment_row, length):
    row = lax.broadcasted_iota(jnp.int32, (LANES, length), 0)
    marks = (row == segment_row) | ((row >= 7) & (row < 10))
    return jnp.where(marks, 1.0, 0.0).astype(f32).T.astype(bf16)


def query_features(segment_row, length):
    row = lax.broadcasted_iota(jnp.int32, (16, length), 0)
    return jnp.where((row < 7) & (row != segment_row), -BIG, 0.0).astype(f32)


def padded_head(head, features, odd):
    blank = jnp.zeros_like(head)
    rest = jnp.zeros((LANES - 16, head.shape[1]), bf16)
    both = [blank, head] if odd else [head, blank]
    return jnp.concatenate(both + [features, rest], axis=0)


def attend_queries(part, parts, slots, me, seg_ref, q_t, k_ref, v_t, att_refs, ot_ref, lse_ref, aux):
    k_aux, q_aux, causal = aux
    length = k_ref.shape[1]
    piece = length // slots
    some = piece // parts
    step = piece if parts > 1 else LANES
    segment_row = seg_ref[0]
    q_aux[...] = query_features(segment_row, length)
    k_aux[...] = key_features(segment_row, length)
    blocks = slots * some // BLOCK
    count = BLOCK // some if parts > 1 else 1

    def head_pair(pair, carry):
        base = pl.multiple_of(pair * LANES, LANES)
        for odd in range(2):
            rows = pl.ds(pl.multiple_of(pair * LANES + odd * 64, 64), 64)
            for block in range(blocks):
                if parts > 1:
                    first = block * count * piece + part * some
                    places = [pl.ds(first + i * piece, some) for i in range(count)]
                else:
                    first = block * BLOCK
                    places = [pl.ds(first, BLOCK)]
                feats = jnp.concatenate([q_aux[:, p] for p in places], axis=1).astype(bf16)
                head = jnp.concatenate([q_t[0, rows, p] for p in places], axis=1)
                query = padded_head(head, feats, odd)
                chunks = [(k, min(BLOCK, first - k)) for k in range(0, first, BLOCK)]
                chunks.append((first, causal.shape[0]))
                scores = []
                for start, size in chunks:
                    keys = pl.ds(start, size)
                    key = jnp.concatenate([k_ref[0, keys, pl.ds(base, LANES)], k_aux[keys]], axis=1)
                    score = dot(key, query)
                    scores.append(score + causal[...] if start == first else score)
                top = functools.reduce(
                    jnp.maximum, [jnp.max(score, axis=0, keepdims=True) for score in scores]
                )
                total = jnp.zeros((1, BLOCK), f32)
                out = jnp.zeros((64, BLOCK), f32)
                for (start, size), score in zip(chunks, scores):
                    prob = jnp.exp2(score - top)
                    total = total + jnp.sum(prob, axis=0, keepdims=True)
                    out = out + dot(v_t[0, rows, pl.ds(start, size)], prob.astype(bf16))
                held = pl.ds(block * BLOCK, BLOCK)
                ot_ref[0, rows, held] = (out / total).astype(bf16)
                lse_ref[0, pl.ds(pair * 2 + odd, 1), held] = top + jnp.log2(total)
        return carry

    lax.fori_loop(0, HEADS // 2, head_pair, 0)
    for j in range(slots):
        place = pl.ds(pl.multiple_of((me ^ j) * some, some), some)
        att_refs[j][0] = ot_ref[0, :, place].T


def attend_first_kernel(parts, slots, old, *refs):
    me_ref = refs[0]
    x_refs = refs[1 : 1 + slots]
    gain_ref, w_ref = refs[1 + slots : 3 + slots]
    rest = refs[3 + slots + old :]
    att_refs = rest[:slots]
    seg_ref, qt_ref, k_ref, v_ref, q_ref, vt_ref, ot_ref, lse_ref = rest[slots : slots + 8]
    w_t, *aux = rest[slots + 8 :]
    width = w_ref.shape[0]
    piece = x_refs[0].shape[1] - MARKS
    me = me_ref[0]
    score_scale = LOG2E / math.sqrt(width // HEADS)

    w_t[:width] = w_ref[:, :width].T
    w_t[width:] = w_ref[:, 2 * width :].T
    aux[2][...] = causal_bias(piece if parts > 1 else LANES)
    gain = gain_ref[...]
    for j in range(slots):
        place = pl.ds(pl.multiple_of((me ^ j) * piece, piece), piece)
        marks = x_refs[j][0, piece:].astype(f32)
        seg_ref[0, :, place] = marks[0:1, :piece].astype(jnp.int32)
        normed, _ = normalize(x_refs[j][0, :piece].astype(f32))
        first_in = (normed * gain).astype(bf16)
        projected = dot(first_in, w_ref[...])
        q_ref[0, place] = (projected[:, :width] * score_scale).astype(bf16)
        k_ref[0, place] = projected[:, width : 2 * width].astype(bf16)
        v_ref[0, place] = projected[:, 2 * width :].astype(bf16)
        turned = dot(w_t[...], first_in, NT)
        qt_ref[0, :, place] = (turned[:width] * score_scale).astype(bf16)
        vt_ref[0, :, place] = turned[width:].astype(bf16)
    attend_queries(
        0, parts, slots, me, seg_ref, qt_ref, k_ref, vt_ref, att_refs, ot_ref, lse_ref, aux
    )


def attend_next_kernel(part, parts, slots, *refs):
    me_ref, seg_ref, qt_ref, k_ref, vt_ref = refs[:5]
    att_refs = refs[5 : 5 + slots]
    ot_ref, lse_ref, *aux = refs[5 + slots :]

    @pl.when(pl.program_id(0) == 0)
    def _():
        aux[2][...] = causal_bias(k_ref.shape[1] // slots if parts > 1 else LANES)

    attend_queries(
        part, parts, slots, me_ref[0], seg_ref, qt_ref, k_ref, vt_ref, att_refs, ot_ref, lse_ref, aux
    )


def attend_outs(rows, slots, some, width):
    return [(per_row(some, width), (rows, some, width), bf16)] * slots, [
        (per_row(width, slots * some), (rows, width, slots * some), bf16),
        (per_row(HEADS, slots * some), (rows, HEADS, slots * some), f32),
    ]


def attend_scratch(length, piece, parts):
    span = LANES + (piece if parts > 1 else LANES) * (BLOCK // LANES - 1)
    return [((length, LANES), bf16), ((16, length), f32), ((span, BLOCK), f32)]


def attend_first(me, row, rows, x_slots, gain, w_qkv, parts, old):
    slots = len(x_slots)
    _, packed, width = x_slots[0].shape
    piece = packed - MARKS
    length = piece * slots

    def this(*shape):
        return pl.BlockSpec((1,) + shape, lambda r, me: (row,) + (0,) * len(shape))

    some = piece // parts
    turned = (this(width, length), (rows, width, length), bf16)
    plain = (this(length, width), (rows, length, width), bf16)
    outs = (
        [(this(some, width), (rows, some, width), bf16)] * slots
        + [(this(1, length), (rows, 1, length), jnp.int32)]
        + [turned, plain, plain, plain, turned]
        + [
            (this(width, slots * some), (rows, width, slots * some), bf16),
            (this(HEADS, slots * some), (rows, HEADS, slots * some), f32),
        ]
    )
    result = call(
        functools.partial(attend_first_kernel, parts, slots, len(old)),
        "attend_first",
        (1,),
        [per_row(packed, width)] * slots
        + [whole(1, width), whole(width, 3 * width)]
        + [pl.BlockSpec(memory_space=pl.ANY)] * len(old),
        outs,
        [((2 * width, width), bf16)] + attend_scratch(length, piece, parts),
        (me, *x_slots, gain, w_qkv, *old),
        12,
        {3 + slots + i: i for i in range(len(old))},
    )
    return result


def attend_next(me, part, parts, projected, slots):
    segment_rows, q_t, k, _, _, v_t = projected
    rows, length, width = k.shape
    piece = length // slots
    att, more = attend_outs(rows, slots, piece // parts, width)
    result = call(
        functools.partial(attend_next_kernel, part, parts, slots),
        "attend_next",
        (rows,),
        [
            per_row(1, length),
            per_row(width, length),
            per_row(length, width),
            per_row(width, length),
        ],
        att + more,
        attend_scratch(length, piece, parts),
        (me, segment_rows, q_t, k, v_t),
        28 / parts,
    )
    return result[:slots], result[slots:]


def attend_back_kernel(row, last, parts, slot_count, *refs):
    me_ref = refs[0]
    x_refs = refs[1 : 1 + slot_count]
    rest = refs[1 + slot_count :]
    do_refs, rest = rest[: parts * slot_count], rest[parts * slot_count :]
    seg_ref, gain_ref, w_ref, qt_ref, k_ref, v_ref, q_ref = rest[:7]
    ot_refs, lse_refs = rest[7 : 7 + parts], rest[7 + parts : 7 + 2 * parts]
    rest = rest[7 + 2 * parts :]
    if row:
        before_ref, rest = rest[0], rest[1:]
    gf_refs, rest = rest[:slot_count], rest[slot_count:]
    dw_refs, rest = rest[: 1 + last], rest[1 + last :]
    (
        k_aux, q_aux, v_aux, causal, do, first_t, work_t, k_t, grads, prob, grad_score, delta, lse
    ) = rest
    width = w_ref.shape[0]
    piece = x_refs[0].shape[1] - MARKS
    some = piece // parts
    length = piece * slot_count
    me = me_ref[0]
    score_scale = 1.0 / math.sqrt(width // HEADS)
    causal[...] = causal_bias()
    lane = lax.broadcasted_iota(jnp.int32, (length, LANES), 1)
    v_aux[...] = jnp.where(lane < 3, 1.0, 0.0).astype(bf16)
    for part in range(parts):
        for i in range(slot_count):
            held = pl.ds(i * some, some)
            lse[:, pl.ds(i * piece + part * some, some)] = lse_refs[part][0, :, held]

    segment_row = seg_ref[0]
    q_aux[...] = query_features(segment_row, length)
    k_aux[...] = key_features(segment_row, length)
    gain = gain_ref[...]
    for j in range(slot_count):
        place = pl.ds(pl.multiple_of((me ^ j) * piece, piece), piece)
        normed, _ = normalize(x_refs[j][0, :piece].astype(f32))
        first_t[:, place] = (normed * gain).astype(bf16).T
        k_t[:, place] = k_ref[0, place].T
        for part in range(parts):
            start = (me ^ j) * piece + part * some
            place = pl.ds(pl.multiple_of(start, some), some)
            held = pl.ds(pl.multiple_of((me ^ j) * some, some), some)
            grad = do_refs[part * slot_count + j][0]
            do[place] = grad
            turned = grad.T
            work_t[:, place] = turned
            product = turned.astype(f32) * ot_refs[part][0, :, held].astype(f32)
            delta[:, place] = jnp.sum(product.reshape(HEADS, width // HEADS, some), axis=1)
    lane = lax.broadcasted_iota(jnp.int32, (1, LANES), 1)
    feature = lax.broadcasted_iota(jnp.int32, (16, BLOCK), 0)
    blocks = length // BLOCK

    def head_pair(pair, carry):
        base = pl.multiple_of(pair * LANES, LANES)
        for odd in range(2):
            rows = pl.ds(pl.multiple_of(pair * LANES + odd * 64, 64), 64)
            head = pl.ds(pair * 2 + odd, 1)
            for qb in range(blocks):
                queries = pl.ds(qb * BLOCK, BLOCK)
                a, b, c = split3(lse[head, queries])
                feats = jnp.where(feature == 7, -a, q_aux[:, queries])
                feats = jnp.where(feature == 8, -b, jnp.where(feature == 9, -c, feats))
                query = padded_head(qt_ref[0, rows, queries], feats.astype(bf16), odd)
                a, b, c = split3(delta[head, queries])
                feats = jnp.where(feature == 0, -a, jnp.where(feature == 1, -b, 0.0))
                feats = jnp.where(feature == 2, -c, feats)
                grad = padded_head(work_t[rows, queries], feats.astype(bf16), odd)
                held = pl.ds(odd * length + qb * BLOCK, BLOCK)
                for kb in range(qb + 1):
                    keys = pl.ds(kb * BLOCK, BLOCK)
                    key = jnp.concatenate([k_ref[0, keys, pl.ds(base, LANES)], k_aux[keys]], axis=1)
                    score = dot(key, query)
                    if kb == qb:
                        score = score + causal[...]
                    value = jnp.concatenate(
                        [v_ref[0, keys, pl.ds(base, LANES)], v_aux[keys]], axis=1
                    )
                    grad_prob = dot(value, grad)
                    weight = jnp.exp2(score)
                    prob[keys, held] = weight.astype(bf16)
                    grad_score[keys, held] = (weight * grad_prob).astype(bf16)
                end = (qb + 1) * BLOCK
                grad_q = dot(k_t[rows, 0:end], grad_score[0:end, held])
                work_t[rows, queries] = (grad_q * score_scale).astype(bf16)
        for kb in range(blocks):
            keys = pl.ds(kb * BLOCK, BLOCK)
            later = pl.ds(kb * BLOCK, length - kb * BLOCK)
            grad_v = jnp.zeros((BLOCK, LANES), f32)
            grad_k = jnp.zeros((BLOCK, LANES), f32)
            for odd in range(2):
                mine = (lane >= 64) if odd else (lane < 64)
                held = pl.ds(odd * length + kb * BLOCK, length - kb * BLOCK)
                zero = jnp.zeros((), bf16)
                grad = jnp.where(mine, do[later, pl.ds(base, LANES)], zero)
                query = jnp.where(mine, q_ref[0, later, pl.ds(base, LANES)], zero)
                grad_v = grad_v + dot(prob[keys, held], grad)
                grad_k = grad_k + dot(grad_score[keys, held], query)
            grads[keys, pl.ds(pl.multiple_of(width + pair * LANES, LANES), LANES)] = (
                grad_k * LN2
            ).astype(bf16)
            grads[keys, pl.ds(pl.multiple_of(2 * width + pair * LANES, LANES), LANES)] = (
                grad_v.astype(bf16)
            )
        return carry

    lax.fori_loop(0, HEADS // 2, head_pair, 0)
    for j in range(slot_count):
        place = pl.ds(pl.multiple_of((me ^ j) * piece, piece), piece)
        grads[place, :width] = work_t[:, place].T
        gf_refs[j][0] = dot(grads[place], w_ref[...], NT).astype(bf16)
    update = dot(first_t[...], grads[...])
    if row:
        update = before_ref[...] + update
    if last:
        keep, send = by_core(me, update.reshape(-1, 2, *dw_refs[0].shape[1:]))
        dw_refs[0][...] = keep
        dw_refs[1][...] = send.astype(bf16)
    else:
        dw_refs[0][...] = update


def attend_back(me, row, rows, shards, x_slots, do_parts, gain, w_qkv, projected, kept, before):
    slot_count, parts = len(x_slots), len(do_parts)
    _, packed, width = x_slots[0].shape
    piece = packed - MARKS
    length = piece * slot_count
    some = piece // parts
    last = row == rows - 1

    def this(*shape):
        return pl.BlockSpec((1,) + shape, lambda r, me: (row,) + (0,) * len(shape))

    half = (shards // 2, width // shards, 3 * width)
    outs = [(per_row(piece, width), (1, piece, width), bf16)] * slot_count
    if last:
        outs += [(whole(*half), half, f32), (whole(*half), half, bf16)]
    else:
        outs += [(whole(width, 3 * width), (width, 3 * width), f32)]
    segment_rows, q_t, k, v, q, _ = projected
    result = call(
        functools.partial(attend_back_kernel, row, last, parts, slot_count),
        "attend_back",
        (1,),
        [per_row(packed, width)] * slot_count
        + [this(some, width)] * (parts * slot_count)
        + [this(1, length), whole(1, width), whole(width, 3 * width)]
        + [this(width, length)]
        + [this(length, width)] * 3
        + [this(width, some * slot_count)] * parts
        + [this(HEADS, some * slot_count)] * parts
        + ([whole(width, 3 * width)] if row else []),
        outs,
        [
            ((length, LANES), bf16),
            ((16, length), f32),
            ((length, LANES), bf16),
            ((BLOCK, BLOCK), f32),
            ((length, width), bf16),
            ((width, length), bf16),
            ((width, length), bf16),
            ((width, length), bf16),
            ((length, 3 * width), bf16),
            ((length, 2 * length), bf16),
            ((length, 2 * length), bf16),
            ((HEADS, length), f32),
            ((HEADS, length), f32),
        ],
        (
            me,
            *x_slots,
            *[do for part in do_parts for do in part],
            segment_rows,
            gain,
            w_qkv,
            q_t,
            k,
            v,
            q,
            *[o for o, _ in kept],
            *[l for _, l in kept],
            *([before] if row else []),
        ),
        28,
    )
    return result[:slot_count], result[slot_count:]


def middle_of(att_refs, inputs_ref, w_out, me):
    rows, piece, width = att_refs[0].shape
    attended = jnp.concatenate([ref[...] for ref in att_refs], axis=0)
    attended = attended.reshape(-1, width)
    origin = jnp.concatenate(
        [inputs_ref[pl.ds((me ^ j) * rows, rows)] for j in range(len(att_refs))], axis=0
    ).reshape(-1, width)
    return attended, origin.astype(f32) + dot(attended, w_out)


def diagonal(piece):
    place = lax.broadcasted_iota(jnp.int32, (piece, LANES), 0)
    lane = lax.broadcasted_iota(jnp.int32, (piece, LANES), 1)
    return place == lane % piece, lane // piece, lane


def mix_kernel(slot_count, experts, *refs):
    me_ref = refs[0]
    att_refs = refs[1 : 1 + slot_count]
    inputs_ref, cot_ref, w_out_ref, gain_ref, control_ref = refs[1 + slot_count : 6 + slot_count]
    rest = refs[6 + slot_count :]
    pay_refs = rest[:experts]
    second_ref, middle_ref = rest[experts:]
    rows, piece, width = att_refs[0].shape
    tokens = rows * slot_count
    me = me_ref[0]
    _, middle = middle_of(att_refs, inputs_ref, w_out_ref[...], me)
    normed, _ = normalize(middle)
    second = (normed * gain_ref[...]).astype(bf16)
    second_ref[...] = second.reshape(tokens, piece, width)
    middle_ref[...] = middle.reshape(tokens, piece, width)
    grad = jnp.concatenate(
        [cot_ref[pl.ds((me ^ j) * rows, rows)] for j in range(slot_count)], axis=0
    ).reshape(-1, width)
    logits = dot(second, control_ref[...], NT).reshape(tokens, piece, LANES)
    top = jnp.max(logits, axis=0)
    weights = jnp.exp(logits - top)
    total = jnp.sum(weights, axis=0)
    log_total = top + jnp.log(total)
    own, _, lane = diagonal(piece)
    weights = jnp.where(own, weights * (1.0 / total), 0.0)
    spread_out = weights.reshape(-1, LANES).astype(bf16)
    mixed = dot(spread_out, second, TN).astype(bf16)
    grad_results = dot(spread_out, grad, TN).astype(bf16)
    a, b, c = split3(log_total)
    for e in range(experts):
        mine = slice(e * piece, (e + 1) * piece)
        first = slice(e * piece, e * piece + 1)
        stats = jnp.where(lane == 0, a[:, first], jnp.where(lane == 1, b[:, first], c[:, first]))
        pay_refs[e][:, :width] = mixed[mine]
        pay_refs[e][:, width : 2 * width] = grad_results[mine]
        pay_refs[e][:, 2 * width :] = stats.astype(bf16)


def mix(me, part, att_slots, inputs, cotangent, w_out, gain, control, experts):
    slot_count = len(att_slots)
    rows, positions, width = att_slots[0].shape
    tokens = rows * slot_count
    piece = LANES // experts
    steps = positions // piece
    span = pl.BlockSpec((tokens, piece, width), lambda b, me: (0, b, 0))
    shifted = pl.BlockSpec((tokens, piece, width), lambda b, me: (0, part * steps + b, 0))
    pay = (
        pl.BlockSpec((piece, 2 * width + LANES), lambda b, me: (b, 0)),
        (positions, 2 * width + LANES),
        bf16,
    )
    result = call(
        functools.partial(mix_kernel, slot_count, experts),
        "mix",
        (steps,),
        [pl.BlockSpec((rows, piece, width), lambda b, me: (0, b, 0))] * slot_count
        + [shifted, shifted, whole(width, width), whole(1, width), whole(LANES, width)],
        [pay] * experts
        + [
            (span, (tokens, positions, width), bf16),
            (span, (tokens, positions, width), f32),
        ],
        [],
        (me, *att_slots, inputs, cotangent, w_out, gain, control),
        positions * 12 / 256,
    )
    return result[:experts], result[experts], result[experts + 1]


def expert_kernel(part, parts, tiled, slot_count, *refs):
    me_ref = refs[0]
    pay_refs = refs[1 : 1 + slot_count]
    rest = refs[1 + slot_count :]
    count = 4 if tiled else 2
    weight_refs, rest = rest[:count], rest[count:]
    expand_ref = weight_refs[0]
    last = part == parts - 1
    earlier, rest = rest[: 4 * part], rest[4 * part :]
    if last:
        back_ref, keep_ref, send_ref = rest[:3]
        mixed_acc, grad_acc, result_acc, back_acc, stat, *more, mixed_low, grad_low = rest[3:]
    else:
        back_ref, mixed_low, grad_low, hidden_ref, pre_ref = rest[:5]
        mixed_acc, grad_acc, result_acc, back_acc, stat, *more = rest[5:]
    me = me_ref[0]
    width = expand_ref.shape[-1]
    step = pl.program_id(0)

    @pl.when(step == 0)
    def _():
        logs = []
        for j in range(slot_count):
            stats = pay_refs[j][:, 2 * width :].astype(f32)
            logs.append(stats[:, 0:1] + stats[:, 1:2] + stats[:, 2:3])
        top = functools.reduce(jnp.maximum, logs)
        total = functools.reduce(jnp.add, [jnp.exp(log - top) for log in logs])
        log_total = top + jnp.log(total)
        mixed, grad = 0.0, 0.0
        for j in range(slot_count):
            share = jnp.exp(logs[j] - log_total)
            mixed = mixed + share * pay_refs[j][:, :width].astype(f32)
            grad = grad + share * pay_refs[j][:, width : 2 * width].astype(f32)
        mixed_acc[...] = mixed
        grad_acc[...] = grad
        mixed_low[...] = mixed.astype(bf16)
        grad_low[...] = grad.astype(bf16)
        result_acc[...] = jnp.zeros_like(result_acc)
        back_acc[...] = jnp.zeros_like(back_acc)
        stat[...] = jnp.broadcast_to(log_total, stat.shape)

    mixed, grad = mixed_low[...], grad_low[...]
    if tiled:
        for i in range(2):
            own, other = weight_refs[2 * i][...], weight_refs[2 * i + 1][...]
            odd = me % 2 == 1
            more[i][:, 0] = jnp.where(odd, other, own)
            more[i][:, 1] = jnp.where(odd, own, other)
        expand, shrink = [ref[...].reshape(-1, width) for ref in more]
    else:
        expand, shrink = [ref[...].reshape(-1, width) for ref in weight_refs]
    value = dot(mixed, expand)
    coeff = math.sqrt(2.0 / math.pi)
    square = value * value
    turn = jnp.tanh(coeff * (value + 0.044715 * (square * value)))
    half = 0.5 * (1.0 + turn)
    hidden = (value * half).astype(bf16)
    slope = half + (0.5 * coeff) * value * (1.0 - turn * turn) * (1.0 + (3 * 0.044715) * square)
    result_acc[...] += dot(hidden, shrink)
    grad_pre = (dot(grad, shrink, NT) * slope).astype(bf16)
    back_acc[...] += dot(grad_pre, expand, NT)
    if last:
        sets = [earlier[4 * i : 4 * i + 4] for i in range(part)]
        mixed = jnp.concatenate([m[...] for m, _, _, _ in sets] + [mixed], axis=0)
        grad = jnp.concatenate([g[...] for _, g, _, _ in sets] + [grad], axis=0)
        hidden = jnp.concatenate([h[...] for _, _, h, _ in sets] + [hidden], axis=0)
        grad_pre = jnp.concatenate([p[...] for _, _, _, p in sets] + [grad_pre], axis=0)
        grad_expand = dot(mixed, grad_pre, TN).astype(bf16)
        grad_shrink = dot(hidden, grad, TN).astype(bf16)
        if tiled:
            shards = 2 * keep_ref.shape[0]
            lines = width // shards
            both = keep_ref.shape[1]
            keep, send = by_core(me, grad_expand.reshape(shards // 2, 2, lines, width))
            place = pl.ds(pl.multiple_of(step * lines, lines), lines)
            keep_ref[:, place] = keep
            send_ref[:, place] = send
            count = 2 * width // both // 2
            keep, send = by_core(me, grad_shrink.reshape(count, 2, both // 2, width))
            place = pl.ds(step * count, count)
            keep_ref[place, both // 2 :] = keep
            send_ref[place, both // 2 :] = send
        else:
            keep_ref[...] = grad_expand.reshape(keep_ref.shape)
            send_ref[...] = grad_shrink.reshape(send_ref.shape)
    else:
        hidden_ref[...] = hidden
        pre_ref[...] = grad_pre

    @pl.when(step == pl.num_programs(0) - 1)
    def _():
        results = result_acc[...].astype(bf16)
        back = back_acc[...].astype(bf16)
        back_ref[:, :width] = results
        back_ref[:, width : 2 * width] = back
        inner = jnp.sum(
            results.astype(f32) * grad_acc[...] + back.astype(f32) * mixed_acc[...],
            axis=-1,
            keepdims=True,
        )
        lane = lax.broadcasted_iota(jnp.int32, stat.shape, 1)
        a, b, c = split3(stat[...])
        d, e, f = split3(inner)
        stats = jnp.where(lane == 0, a, jnp.where(lane == 1, b, c))
        stats = jnp.where(lane < 3, stats, jnp.where(lane == 3, d, jnp.where(lane == 4, e, f)))
        back_ref[:, 2 * width :] = stats.astype(bf16)


def pack_expert(expand, shrink):
    experts, lines, hidden = expand.shape
    width = shrink.shape[-1]
    expand = expand.reshape(experts, lines, hidden // width, width)
    expand = jnp.swapaxes(expand, 1, 2).reshape(experts, -1, width)
    return jnp.concatenate([expand, shrink], axis=1)


def unpack_expert(packed, lines):
    experts, both, width = packed.shape
    expand = packed[:, : both // 2].reshape(experts, -1, lines, width)
    expand = jnp.swapaxes(expand, 1, 2).reshape(experts, lines, -1)
    return expand, packed[:, both // 2 :]


def expert(me, core, part, parts, pay_slots, halves, earlier):
    slot_count = len(pay_slots)
    groups, packed = pay_slots[0].shape
    shards = 2 * halves[0][0].shape[0]
    tail, width = halves[0][0].shape[1:]
    hidden = shards * tail
    chunks = hidden // width
    lines = width // shards
    acc = ((groups, width), f32)
    low = ((groups, width), bf16)
    tiled = lines % 16 == 0
    group = shards // chunks // 2
    if tiled:
        columns = pl.BlockSpec((shards // 2, lines, width), lambda f, me: (0, f, 0))
        lower = pl.BlockSpec((group, tail, width), lambda f, me: (f, 0, 0))
        weights = [*halves[0], *halves[1]]
        specs = [columns, columns, lower, lower]
        built = [((shards // 2, 2, lines, width), bf16), ((group, 2, tail, width), bf16)]
        both = (shards // 2, 2 * tail, width)
        grads = [(whole(*both), both, bf16)] * 2
    else:
        odd = core == 1
        weights = [
            jnp.stack([jnp.where(odd, b, a), jnp.where(odd, a, b)], axis=1) for a, b in halves
        ]
        expand = weights[0].reshape(shards, chunks, lines, width)
        expand = jnp.swapaxes(expand, 0, 1).reshape(chunks, width, width)
        weights = [expand, weights[1].reshape(chunks, width, width)]
        specs = [pl.BlockSpec((1, width, width), lambda f, me: (f, 0, 0))] * 2
        built = []
        grads = [(specs[0], (chunks, width, width), bf16)] * 2
    token = whole(groups, width)
    inner = pl.BlockSpec((groups, width), lambda f, me: (0, f))
    last = part == parts - 1
    outs = [(whole(groups, packed), (groups, packed), bf16)]
    scratch = [acc, acc, acc, acc, ((groups, LANES), f32)] + built
    if last:
        outs += grads
        scratch += [low, low]
    else:
        outs += [(token, (groups, width), bf16)] * 2 + [(inner, (groups, hidden), bf16)] * 2
    result = call(
        functools.partial(expert_kernel, part, parts, tiled, slot_count),
        "expert",
        (chunks,),
        [whole(groups, packed)] * slot_count + specs + [token, token, inner, inner] * part,
        outs,
        scratch,
        (me, *pay_slots, *weights, *earlier),
        7,
    )
    more = list(result[1:])
    if last and not tiled:
        grad = jnp.swapaxes(more[0].reshape(chunks, shards, lines, width), 0, 1)
        more = [grad.reshape(shards, tail, width), more[1].reshape(shards, tail, width)]
        more = jnp.concatenate(more, axis=1).reshape(shards // 2, 2, 2 * tail, width)
        odd = core == 1
        more = [
            jnp.where(odd, more[:, 1], more[:, 0]),
            jnp.where(odd, more[:, 0], more[:, 1]),
        ]
    return result[0], more


def unmix_kernel(slot_count, experts, part, *refs):
    me_ref = refs[0]
    ret_refs = refs[1 : 1 + experts]
    att_refs = refs[1 + experts : 1 + experts + slot_count]
    rest = refs[1 + experts + slot_count :]
    second_ref, middle_ref, cot_ref, w_out_ref, gain_ref, control_ref = rest[:6]
    rest = rest[6:]
    if part:
        old_out_ref, old_control_ref, old_gain_ref = rest[2:5]
        rest = rest[5:]
    out_ref, grad_middle_ref = rest[:2]
    back_refs = rest[2 : 2 + slot_count]
    grad_out_ref, grad_control_ref, grad_gain_ref = rest[2 + slot_count :]
    rows, piece, width = att_refs[0].shape
    tokens = rows * slot_count
    me = me_ref[0]

    @pl.when(pl.program_id(0) == 0)
    def _():
        if part:
            grad_out_ref[...] = old_out_ref[...]
            grad_control_ref[...] = old_control_ref[...]
            grad_gain_ref[...] = old_gain_ref[...]
        else:
            grad_out_ref[...] = jnp.zeros_like(grad_out_ref)
            grad_control_ref[...] = jnp.zeros_like(grad_control_ref)
            grad_gain_ref[...] = jnp.zeros_like(grad_gain_ref)

    second = second_ref[...].reshape(-1, width)
    middle = middle_ref[...].reshape(-1, width)
    cot = jnp.concatenate(
        [cot_ref[pl.ds((me ^ j) * rows, rows)] for j in range(slot_count)], axis=0
    ).reshape(-1, width)
    own, group, _ = diagonal(piece)
    log_total = jnp.zeros((piece, LANES), f32)
    inner = jnp.zeros((piece, LANES), f32)
    for e in range(experts):
        stats = ret_refs[e][:, 2 * width :].astype(f32)
        mine = group == e
        log_total = jnp.where(mine, stats[:, 0:1] + stats[:, 1:2] + stats[:, 2:3], log_total)
        inner = jnp.where(mine, stats[:, 3:4] + stats[:, 4:5] + stats[:, 5:6], inner)
    results = jnp.concatenate([ref[:, :width] for ref in ret_refs], axis=0)
    back = jnp.concatenate([ref[:, width : 2 * width] for ref in ret_refs], axis=0)
    control = control_ref[...]
    logits = dot(second, control, NT).reshape(tokens, piece, LANES)
    weights = jnp.where(own, jnp.exp(logits - log_total), 0.0)
    low = weights.reshape(-1, LANES).astype(bf16)
    output = (middle + dot(low, results).astype(bf16).astype(f32)).astype(bf16)
    grad_weights = (dot(cot, results, NT) + dot(second, back, NT)).reshape(tokens, piece, LANES)
    grad_logits = (weights * (grad_weights - inner)).reshape(-1, LANES).astype(bf16)
    grad_second = dot(low, back) + dot(grad_logits, control)
    grad_second = grad_second.astype(bf16).astype(f32)
    grad_control_ref[...] += dot(grad_logits, second, TN)
    normed, scaled = normalize(middle)
    product = (grad_second * normed).reshape(-1, 8, width)
    grad_gain_ref[...] += jnp.sum(product, axis=0)
    grad_middle = cot.astype(f32) + norm_back(grad_second * gain_ref[...], normed, scaled)
    grad_middle = grad_middle.astype(bf16)
    grad_attended = dot(grad_middle, w_out_ref[...], NT).astype(bf16)
    output = output.reshape(tokens, piece, width)
    grad_attended = grad_attended.reshape(tokens, piece, width)
    grad_middle_ref[...] = grad_middle.reshape(tokens, piece, width)
    for j in range(slot_count):
        mine = slice(j * rows, (j + 1) * rows)
        out_ref[pl.ds((me ^ j) * rows, rows)] = output[mine]
        back_refs[j][...] = grad_attended[mine]
    attended = jnp.concatenate([ref[...] for ref in att_refs], axis=0).reshape(-1, width)
    grad_out_ref[...] += dot(attended, grad_middle, TN)


def unmix(me, part, ret_slots, att_slots, second, middle, cotangent, w_out, gain, control, before):
    slot_count, experts = len(att_slots), len(ret_slots)
    rows, positions, width = att_slots[0].shape
    tokens = rows * slot_count
    piece = LANES // experts
    steps = positions // piece
    span = pl.BlockSpec((tokens, piece, width), lambda b, me: (0, b, 0))
    shifted = pl.BlockSpec((tokens, piece, width), lambda b, me: (0, part * steps + b, 0))
    slot = pl.BlockSpec((rows, piece, width), lambda b, me: (0, b, 0))
    full = (shifted, cotangent.shape, bf16)
    sums = [
        (whole(width, width), (width, width), f32),
        (whole(LANES, width), (LANES, width), f32),
        (whole(8, width), (8, width), f32),
    ]
    count = 1 + experts + slot_count + 6
    result = call(
        functools.partial(unmix_kernel, slot_count, experts, part),
        "unmix",
        (steps,),
        [pl.BlockSpec((piece, 2 * width + LANES), lambda b, me: (b, 0))] * experts
        + [slot] * slot_count
        + [span, span, shifted, whole(width, width), whole(1, width), whole(LANES, width)]
        + ([pl.BlockSpec(memory_space=pl.ANY)] * 2 + [spec for spec, _, _ in sums] if part else []),
        [full, full] + [(slot, (rows, positions, width), bf16)] * slot_count + sums,
        [],
        (me, *ret_slots, *att_slots, second, middle, cotangent, w_out, gain, control, *before),
        positions * 17 / 256,
        {count: 0, count + 1: 1} if part else None,
    )
    do_slots = result[2 : 2 + slot_count]
    return do_slots, result[:2] + result[2 + slot_count :]


def finish_kernel(slot_count, row_count, *refs):
    me_ref = refs[0]
    gf_refs = refs[1 : 1 + slot_count * row_count]
    inputs_ref, grad_middle_ref, gain_ref, out_ref = refs[1 + slot_count * row_count :]
    me = me_ref[0]
    for j in range(slot_count):
        for row in range(row_count):
            place = (me ^ j) * row_count + row
            normed, scaled = normalize(inputs_ref[place].astype(f32))
            incoming = gf_refs[row * slot_count + j][0].astype(f32) * gain_ref[...]
            grad = norm_back(incoming, normed, scaled)
            grad = grad + grad_middle_ref[j * row_count + row].astype(f32)
            out_ref[place] = grad.astype(bf16)


def finish(me, gf_rows, inputs, grad_middle, gain):
    slot_count, row_count = len(gf_rows[0]), len(gf_rows)
    tokens, positions, width = inputs.shape
    piece = 64
    span = pl.BlockSpec((tokens, piece, width), lambda b, me: (0, b, 0))
    slot = pl.BlockSpec((1, piece, width), lambda b, me: (0, b, 0))
    return call(
        functools.partial(finish_kernel, slot_count, row_count),
        "finish",
        (positions // piece,),
        [slot] * (slot_count * row_count) + [span, span, whole(1, width)],
        [(span, (tokens, positions, width), bf16)],
        [],
        (me, *[gf for row in gf_rows for gf in row], inputs, grad_middle, gain),
        6,
    )[0]


def on_device(
    sizes,
    inputs,
    segments,
    cotangent,
    gain_attn,
    w_qkv,
    w_out,
    gain_mix,
    w_control,
    w_expand,
    w_shrink,
):
    groups, members, slots = sizes
    local_rows, positions, width = inputs.shape
    experts = w_expand.shape[0]
    rows = local_rows // slots
    place = (("gq", groups), ("gi", members), ("seq", slots))
    owners = (("gq", groups), ("seq", slots))
    seq_me = lax.axis_index("seq")
    member = lax.axis_index("gi")
    me = seq_me.astype(jnp.int32).reshape(1)

    parts = 2 if positions % BLOCK == 0 else 1

    def row_parts(array):
        return [
            lax.dynamic_slice_in_dim(array, (seq_me ^ j) * rows, rows, axis=0) for j in range(slots)
        ]

    marks = segments.astype(bf16)[:, None, :]
    marks = jnp.pad(marks, ((0, 0), (0, MARKS - 1), (0, width - positions)))
    x_parts = row_parts(jnp.concatenate([inputs, marks], axis=1))
    x_parts = [[x[row : row + 1] for x in x_parts] for row in range(rows)]
    x_rows = [swap_slots(x_parts[0], "seq")]

    small = jnp.concatenate([gain_attn[None], gain_mix[None], w_control], axis=0)
    small = jnp.pad(jnp.transpose(small), ((0, 0), (0, LANES - 2 - experts)))
    packed = jnp.concatenate([w_qkv, w_out, small], axis=1).astype(bf16)
    packed = Doubling(packed, place, ("gq", "seq", "core"))
    packed.at_once("gi")
    packed.steps("gq")

    def member_parts(array):
        return [
            lax.dynamic_index_in_dim(array, member ^ j, 0, keepdims=False) for j in range(members)
        ]

    weights = member_parts(pack_expert(w_expand.astype(bf16), w_shrink.astype(bf16)))
    weights = jnp.stack(natural(swap_slots(weights, "gi"), member))
    x_rows[0], x_parts, packed.value, weights = hold(
        (x_rows[0], x_parts, packed.value, weights)
    )
    tail = weights.shape[1] // 2
    halves = [
        Doubling(half, owners, ("gq", "seq"), 1) for half in (weights[:, :tail], weights[:, tail:])
    ]
    halves[0].steps("gq")
    halves[1].value = together(halves[1].value, halves[0])
    halves[1].steps("gq")
    packed.steps("seq").steps("core")
    x_rows[0], x_parts = together((x_rows[0], x_parts), packed, *halves)
    packed = packed.value.reshape(width, -1)
    proj_in, proj_out = packed[:, : 3 * width], packed[:, 3 * width : 4 * width]
    vectors = jnp.transpose(packed[:, 4 * width :])
    gain_one = vectors[0:1].astype(f32)
    gain_two = vectors[1:2].astype(f32)
    control = natural([vectors[2 + e : 3 + e] for e in range(experts)], member)
    control = jnp.concatenate(
        [jnp.broadcast_to(c, (LANES // experts, width)) for c in control], axis=0
    )

    old = []
    for row in range(rows):
        old = attend_first(me, row, rows, x_rows[row], gain_one, proj_in, parts, old)
        if row + 1 < rows:
            x_rows.append(swap_slots(x_parts[row + 1], "seq"))
            old, x_rows[row + 1] = together((old, x_rows[row + 1]), halves[0])
        if row == max(0, rows - 2):
            halves[0].steps("seq")
        if row == rows - 1:
            old = together(old, *halves)
    halves[1].steps("seq")
    att, projected, kept = old[:slots], old[slots : slots + 6], old[slots + 6 :]
    att_parts, kept = [swap_slots(att, "seq")], [kept]
    for part in range(1, parts):
        att, more = attend_next(me, part, parts, projected, slots)
        att, att_parts[-1] = hold((att, att_parts[-1]))
        att_parts.append(swap_slots(att, "seq"))
        kept.append(more)
    pay_parts, second_parts, middle_parts = [], [], []
    for part in range(parts):
        pay, second, middle = mix(
            me, part, att_parts[part], inputs, cotangent, proj_out, gain_two, control, experts
        )
        if part == 0:
            pay, second, middle = together((pay, second, middle), halves[1])
            halves = [half.value.reshape(-1, *half.value.shape[-2:]) for half in halves]
            halves = [(half, partner(half, "seq", slots, 1)) for half in halves]
        pay_parts.append(swap_slots(pay, "gi"))
        second_parts.append(second)
        middle_parts.append(middle)
    ret_parts, earlier = [], []
    for part in range(parts):
        back, more = expert(me, seq_me % 2, part, parts, pay_parts[part], halves, earlier)
        earlier = earlier + list(more)
        if part + 1 < parts:
            pay_parts[part + 1], back = hold((pay_parts[part + 1], back))
        elif part:
            back, more, ret_parts = hold((back, more, ret_parts))
        ret_parts.append(swap_slots([back] * members, "gi"))

    keep, send = more
    bits = [2] * len(bits_of((("gq", groups),)))
    bits += [members] + [2] * (len(bits_of((("seq", slots),))) - 1)
    total = keep.astype(f32) + partner(send, "seq", slots, 1).astype(f32)
    sum_expert = Halving(total.reshape(*bits, *total.shape[1:]), owners, ("seq", "gq"), 1)
    do_parts, before = [], []
    for part in range(parts):
        do, before = unmix(
            me,
            part,
            ret_parts[part],
            att_parts[part],
            second_parts[part],
            middle_parts[part],
            cotangent,
            proj_out,
            gain_two,
            control,
            before,
        )
        do, before = together((do, before), sum_expert)
        if part == 0:
            sum_expert.steps("seq")
        do_parts.append(swap_slots(do, "seq"))
    output, grad_middle, grad_out, grad_control, grad_gain = before
    grad_control = grad_control.reshape(experts, LANES // experts, width).sum(axis=1)
    grad_control = jnp.concatenate(
        natural([grad_control[e : e + 1] for e in range(experts)], member), axis=0
    )
    small = jnp.concatenate([grad_gain.sum(axis=0, keepdims=True), grad_control], axis=0)
    small = jnp.pad(jnp.transpose(small), ((0, 0), (0, LANES - 1 - experts)))
    every_bit = [2] * len(bits_of(place))
    grad_out = jnp.concatenate([grad_out, small], axis=1)
    sum_out = Halving(grad_out.reshape(*every_bit, -1, width + LANES), place, ("core",))
    sum_out.left = bits_of(place)
    sum_out.steps("core")
    do_parts = together(do_parts, sum_out, sum_expert)
    sum_expert.steps("gq")

    gf_rows, grad_in = [], None
    for row in range(rows):
        gf_slots, grad_in = attend_back(
            me,
            row,
            rows,
            groups * members * slots,
            x_rows[row],
            do_parts,
            gain_one,
            proj_in,
            projected,
            kept,
            grad_in,
        )
        grad_in = grad_in[0] if row < rows - 1 else grad_in
        if row == 0:
            gf_slots, grad_in = together((gf_slots, grad_in), sum_expert)
            columns = swap_slots(
                [p if j == 0 else p.astype(bf16) for j, p in enumerate(member_parts(sum_expert.value))],
                "gi",
            )
        if row == rows - 1:
            gf_slots, grad_in, columns, gf_rows = hold((gf_slots, grad_in, columns, gf_rows))
        gf_rows.append(swap_slots(gf_slots, "seq"))
    columns = jnp.stack([c.astype(f32) for c in natural(columns, member)])
    grad_expand, grad_shrink = unpack_expert(columns, width // (groups * members * slots))
    keep, send = grad_in
    total = keep + partner(send, "seq", slots, 1).astype(f32)
    total = total.reshape(*every_bit[1:], *total.shape[1:])
    total = jnp.concatenate([total, sum_out.value], axis=-1)
    sum_in = Halving(total, place, ("gi", "gq", "seq"))
    sum_in.step(sum_in.order.pop(0))
    gf_rows[-1] = together(gf_rows[-1], sum_in)
    sum_in.steps("gi")
    grad_inputs = finish(me, gf_rows, inputs, grad_middle, gain_one)
    grad_inputs = together(grad_inputs, sum_in)
    total = sum_in.finish()
    grad_in, grad_out = total[:, : 3 * width], total[:, 3 * width :]
    small = jnp.transpose(grad_out[:, width:])
    weighted = jnp.sum(grad_in * w_qkv.astype(bf16).astype(f32), axis=1)
    return (
        output,
        grad_inputs,
        weighted / gain_attn.astype(bf16).astype(f32),
        grad_in,
        grad_out[:, :width],
        small[0],
        small[1 : 1 + experts],
        grad_expand,
        grad_shrink,
    )


def solution(mesh):
    dp_count, seq_count = mesh.shape["dp"], mesh.shape["seq"]

    def run(inputs, *args):
        members = GROUP * dp_count // inputs.shape[0]
        sizes = (dp_count // members, members, seq_count)
        fine = Mesh(mesh.devices.reshape(sizes), ("gq", "gi", "seq"))
        dp, both = ("gq", "gi"), ("gq", "gi", "seq")
        return jax.shard_map(
            functools.partial(on_device, sizes),
            mesh=fine,
            in_specs=(
                P(dp, "seq", None),
                P(dp, "seq"),
                P(dp, "seq", None),
                P(both),
                P(both, None),
                P(both, None),
                P(both),
                P(None, both),
                P(None, both, None),
                P(None, both, None),
            ),
            out_specs=(
                P(dp, "seq", None),
                P(dp, "seq", None),
                P(both),
                P(both, None),
                P(both, None),
                P(both),
                P(None, both),
                P(None, both, None),
                P(None, both, None),
            ),
            check_vma=False,
        )(inputs, *args)

    return run
```

```python
import functools
import math

import jax
import jax.numpy as jnp
from jax import lax
from jax.experimental import pallas as pl
from jax.experimental.pallas import tpu as pltpu
from jax.sharding import Mesh
from jax.sharding import PartitionSpec as P

HEADS = 8
GROUP = 32
BLOCK = 256
LANES = 128
MARKS = 16
VMEM_LIMIT = 60 * 1024 * 1024

LOG2E = math.log2(math.e)
LN2 = math.log(2.0)
BIG = 1e30

bf16 = jnp.bfloat16
f32 = jnp.float32

NN = (((1,), (0,)), ((), ()))
NT = (((1,), (1,)), ((), ()))
TN = (((0,), (0,)), ((), ()))


def dot(a, b, dims=NN):
    return lax.dot_general(a, b, dims, preferred_element_type=f32)


def normalize(values):
    center = values - jnp.mean(values, axis=-1, keepdims=True)
    scaled = lax.rsqrt(jnp.mean(center * center, axis=-1, keepdims=True) + 1e-05)
    return center * scaled, scaled


def norm_back(incoming, normed, scaled):
    return scaled * (
        incoming
        - jnp.mean(incoming, axis=-1, keepdims=True)
        - normed * jnp.mean(incoming * normed, axis=-1, keepdims=True)
    )


def split3(value):
    high = value.astype(bf16).astype(f32)
    rest = value - high
    mid = rest.astype(bf16).astype(f32)
    low = (rest - mid).astype(bf16).astype(f32)
    return high, mid, low


def partner(value, axis, size, mask):
    return lax.ppermute(value, axis, [(i, i ^ mask) for i in range(size)])


def swap_slots(slots, axis):
    size = len(slots)
    return [slots[0]] + [partner(slots[j], axis, size, j) for j in range(1, size)]


def natural(slots, me):
    out = list(slots)
    bit = 1
    while bit < len(out):
        flip = (me & bit) != 0
        out = [jnp.where(flip, out[k ^ bit], out[k]) for k in range(len(out))]
        bit *= 2
    return out


def bits_of(sizes):
    bits = []
    for axis, size in sizes:
        mask = size // 2
        while mask:
            bits.append((axis, size, mask))
            mask //= 2
    return bits


def named(bit):
    axis, _, mask = bit
    return "core" if axis == "seq" and mask == 1 else axis


class Steps:
    def __init__(self, value, sizes, order):
        self.order = [bit for axis in order for bit in reversed(bits_of(sizes)) if named(bit) == axis]
        self.value = value

    def steps(self, axis):
        while self.order and named(self.order[0]) == axis:
            self.step(self.order.pop(0))
        return self

    def finish(self):
        while self.order:
            self.step(self.order.pop(0))
        return self.value


class Doubling(Steps):
    def __init__(self, value, sizes, order, inner=0):
        super().__init__(value, sizes, order)
        self.inner = inner
        self.place = bits_of(sizes)
        self.have = []

    def step(self, bit):
        axis, size, mask = bit
        depth = sum(self.place.index(other) < self.place.index(bit) for other in self.have)
        depth += self.inner if axis == "seq" else 0
        other = partner(self.value, axis, size, mask)
        high = (lax.axis_index(axis) & mask) != 0
        first = jnp.where(high, other, self.value)
        second = jnp.where(high, self.value, other)
        self.value = jnp.stack([first, second], axis=depth)
        self.have.append(bit)

    def at_once(self, axis):
        bits = [bit for bit in self.place if bit[0] == axis]
        self.order = [bit for bit in self.order if bit[0] != axis]
        depth = sum(self.place.index(other) < self.place.index(bits[0]) for other in self.have)
        depth += self.inner if axis == "seq" else 0
        slots = natural(swap_slots([self.value] * 2 ** len(bits), axis), lax.axis_index(axis))
        shape = self.value.shape
        value = jnp.stack(slots, axis=depth)
        self.value = value.reshape(shape[:depth] + (2,) * len(bits) + shape[depth:])
        self.have += bits


class Halving(Steps):
    def __init__(self, value, sizes, order, inner=0):
        super().__init__(value, sizes, order)
        self.sizes = sizes
        self.left = [bit for bit in bits_of(sizes) if bit in self.order]
        self.inner = inner

    def prepare(self):
        bit = self.order.pop(0)
        depth = self.left.index(bit)
        self.left.pop(depth)
        axis, size, mask = bit
        depth += self.inner if axis == "seq" else 0
        high = ((lax.axis_index(axis) & mask) != 0).astype(jnp.int32)
        keep = lax.dynamic_index_in_dim(self.value, high, depth, keepdims=False)
        send = lax.dynamic_index_in_dim(self.value, 1 - high, depth, keepdims=False)
        self.value = (keep, send.astype(bf16))
        self.link = bit

    def exchange(self):
        axis, size, mask = self.link
        keep, send = self.value
        self.value = (keep, partner(send, axis, size, mask))

    def combine(self):
        self.value = functools.reduce(jnp.add, [part.astype(f32) for part in self.value])

    def step(self, bit):
        self.order.insert(0, bit)
        self.prepare()
        self.exchange()
        self.combine()

    def at_once(self, axes):
        bits = [bit for bit in self.left if bit[0] in axes]
        self.order = [bit for bit in self.order if bit not in bits]
        depth = self.left.index(bits[0])
        if self.inner or bits != self.left[depth : depth + len(bits)]:
            raise NotImplementedError
        self.left = [bit for bit in self.left if bit not in bits]
        shape = self.value.shape
        value = self.value.reshape(shape[:depth] + (2 ** len(bits),) + shape[depth + len(bits) :])
        place, names = 0, []
        for axis, size, mask in bits:
            place = 2 * place + ((lax.axis_index(axis) & mask) != 0).astype(jnp.int32)
            if axis not in names:
                names.append(axis)
        total = [lax.dynamic_index_in_dim(value, place, depth, keepdims=False)]
        sizes = [size for axis, size in self.sizes if axis in names]
        for j in range(1, 2 ** len(bits)):
            piece = lax.dynamic_index_in_dim(value, place ^ j, depth, keepdims=False)
            masks = {axis: 0 for axis in names}
            for i, (axis, _, mask) in enumerate(bits):
                if j >> (len(bits) - 1 - i) & 1:
                    masks[axis] |= mask
            pairs = []
            for source in range(math.prod(sizes)):
                target, rest, unit = 0, source, 1
                for axis, size in reversed(list(zip(names, sizes))):
                    target += ((rest % size) ^ masks[axis]) * unit
                    rest, unit = rest // size, unit * size
                pairs.append((source, target))
            total.append(lax.ppermute(piece.astype(bf16), tuple(names), pairs))
        self.value = total


hold = lax.optimization_barrier


def together(values, *sums):
    values, held = lax.optimization_barrier((values, [item.value for item in sums]))
    for item, value in zip(sums, held):
        item.value = value
    return values


def call(kernel, name, grid, in_specs, outs, scratch, args, micros, aliases=None):
    return pl.pallas_call(
        kernel,
        grid_spec=pltpu.PrefetchScalarGridSpec(
            num_scalar_prefetch=1,
            grid=grid,
            in_specs=in_specs,
            out_specs=[spec for spec, _, _ in outs],
            scratch_shapes=[pltpu.VMEM(shape, dtype) for shape, dtype in scratch],
        ),
        out_shape=[jax.ShapeDtypeStruct(shape, dtype) for _, shape, dtype in outs],
        input_output_aliases=aliases or {},
        compiler_params=pltpu.CompilerParams(vmem_limit_bytes=VMEM_LIMIT),
        cost_estimate=pl.CostEstimate(
            flops=int(micros * 1e9), bytes_accessed=1 << 20, transcendentals=0
        ),
        name=name,
    )(*args)


def per_row(*shape):
    return pl.BlockSpec((1,) + shape, lambda r, me: (r,) + (0,) * len(shape))


def whole(*shape):
    return pl.BlockSpec(shape, lambda r, me: (0,) * len(shape))


def fourth(width):
    return pl.BlockSpec((width, width), lambda b, me: (0, 3))


def by_core(me, pairs):
    odd = me % 2 == 1
    first, second = pairs[:, 0], pairs[:, 1]
    return jnp.where(odd, second, first), jnp.where(odd, first, second)


def causal_bias(step=LANES):
    rows = LANES + step * (BLOCK // LANES - 1)
    key = lax.broadcasted_iota(jnp.int32, (rows, BLOCK), 0)
    query = lax.broadcasted_iota(jnp.int32, (rows, BLOCK), 1)
    query = query + (query // LANES) * (step - LANES)
    return jnp.where(key <= query, 0.0, -BIG).astype(f32)


def key_features(segment_row, length):
    row = lax.broadcasted_iota(jnp.int32, (LANES, length), 0)
    marks = (row == segment_row) | ((row >= 7) & (row < 10))
    return jnp.where(marks, 1.0, 0.0).astype(f32).T.astype(bf16)


def query_features(segment_row, length):
    row = lax.broadcasted_iota(jnp.int32, (16, length), 0)
    return jnp.where((row < 7) & (row != segment_row), -BIG, 0.0).astype(f32)


def padded_head(head, features, odd):
    blank = jnp.zeros_like(head)
    rest = jnp.zeros((LANES - 16, head.shape[1]), bf16)
    both = [blank, head] if odd else [head, blank]
    return jnp.concatenate(both + [features, rest], axis=0)


def attend_queries(part, parts, slots, me, seg_ref, q_t, k_ref, v_t, att_refs, ot_ref, lse_ref, aux):
    k_aux, q_aux, causal = aux
    length = k_ref.shape[1]
    piece = length // slots
    some = piece // parts
    step = piece if parts > 1 else LANES
    segment_row = seg_ref[0]
    q_aux[...] = query_features(segment_row, length)
    k_aux[...] = key_features(segment_row, length)
    blocks = slots * some // BLOCK
    count = BLOCK // some if parts > 1 else 1

    def head_pair(pair, carry):
        base = pl.multiple_of(pair * LANES, LANES)
        for odd in range(2):
            rows = pl.ds(pl.multiple_of(pair * LANES + odd * 64, 64), 64)
            for block in range(blocks):
                if parts > 1:
                    first = block * count * piece + part * some
                    places = [pl.ds(first + i * piece, some) for i in range(count)]
                else:
                    first = block * BLOCK
                    places = [pl.ds(first, BLOCK)]
                feats = jnp.concatenate([q_aux[:, p] for p in places], axis=1).astype(bf16)
                head = jnp.concatenate([q_t[0, rows, p] for p in places], axis=1)
                query = padded_head(head, feats, odd)
                chunks = [(k, min(BLOCK, first - k)) for k in range(0, first, BLOCK)]
                chunks.append((first, causal.shape[0]))
                scores = []
                for start, size in chunks:
                    keys = pl.ds(start, size)
                    key = jnp.concatenate([k_ref[0, keys, pl.ds(base, LANES)], k_aux[keys]], axis=1)
                    score = dot(key, query)
                    scores.append(score + causal[...] if start == first else score)
                top = functools.reduce(
                    jnp.maximum, [jnp.max(score, axis=0, keepdims=True) for score in scores]
                )
                total = jnp.zeros((1, BLOCK), f32)
                out = jnp.zeros((64, BLOCK), f32)
                for (start, size), score in zip(chunks, scores):
                    prob = jnp.exp2(score - top)
                    total = total + jnp.sum(prob, axis=0, keepdims=True)
                    out = out + dot(v_t[0, rows, pl.ds(start, size)], prob.astype(bf16))
                held = pl.ds(block * BLOCK, BLOCK)
                ot_ref[0, rows, held] = (out / total).astype(bf16)
                lse_ref[0, pl.ds(pair * 2 + odd, 1), held] = top + jnp.log2(total)
        return carry

    lax.fori_loop(0, HEADS // 2, head_pair, 0)
    for j in range(slots):
        place = pl.ds(pl.multiple_of((me ^ j) * some, some), some)
        att_refs[j][0] = ot_ref[0, :, place].T


def attend_first_kernel(parts, slots, old, *refs):
    me_ref = refs[0]
    x_refs = refs[1 : 1 + slots]
    vector_ref, w_ref = refs[1 + slots : 3 + slots]
    rest = refs[3 + slots + old :]
    att_refs = rest[:slots]
    seg_ref, qt_ref, k_ref, v_ref, q_ref, vt_ref, ot_ref, lse_ref = rest[slots : slots + 8]
    w_t, *aux = rest[slots + 8 :]
    width = w_ref.shape[0]
    piece = x_refs[0].shape[1] - MARKS
    me = me_ref[0]
    score_scale = LOG2E / math.sqrt(width // HEADS)

    w_t[:width] = w_ref[:, :width].T
    w_t[width:] = w_ref[:, 2 * width :].T
    aux[2][...] = causal_bias(piece if parts > 1 else LANES)
    gain = vector_ref[...].astype(f32).T[0:1]
    for j in range(slots):
        place = pl.ds(pl.multiple_of((me ^ j) * piece, piece), piece)
        marks = x_refs[j][0, piece:].astype(f32)
        seg_ref[0, :, place] = marks[0:1, :piece].astype(jnp.int32)
        normed, _ = normalize(x_refs[j][0, :piece].astype(f32))
        first_in = (normed * gain).astype(bf16)
        projected = dot(first_in, w_ref[...])
        q_ref[0, place] = (projected[:, :width] * score_scale).astype(bf16)
        k_ref[0, place] = projected[:, width : 2 * width].astype(bf16)
        v_ref[0, place] = projected[:, 2 * width :].astype(bf16)
        turned = dot(w_t[...], first_in, NT)
        qt_ref[0, :, place] = (turned[:width] * score_scale).astype(bf16)
        vt_ref[0, :, place] = turned[width:].astype(bf16)
    attend_queries(
        0, parts, slots, me, seg_ref, qt_ref, k_ref, vt_ref, att_refs, ot_ref, lse_ref, aux
    )


def attend_next_kernel(part, parts, slots, *refs):
    me_ref, seg_ref, qt_ref, k_ref, vt_ref = refs[:5]
    att_refs = refs[5 : 5 + slots]
    ot_ref, lse_ref, *aux = refs[5 + slots :]

    @pl.when(pl.program_id(0) == 0)
    def _():
        aux[2][...] = causal_bias(k_ref.shape[1] // slots if parts > 1 else LANES)

    attend_queries(
        part, parts, slots, me_ref[0], seg_ref, qt_ref, k_ref, vt_ref, att_refs, ot_ref, lse_ref, aux
    )


def attend_outs(rows, slots, some, width):
    return [(per_row(some, width), (rows, some, width), bf16)] * slots, [
        (per_row(width, slots * some), (rows, width, slots * some), bf16),
        (per_row(HEADS, slots * some), (rows, HEADS, slots * some), f32),
    ]


def attend_scratch(length, piece, parts):
    span = LANES + (piece if parts > 1 else LANES) * (BLOCK // LANES - 1)
    return [((length, LANES), bf16), ((16, length), f32), ((span, BLOCK), f32)]


def attend_first(me, row, rows, x_slots, weights, parts, old):
    slots = len(x_slots)
    _, packed, width = x_slots[0].shape
    piece = packed - MARKS
    length = piece * slots

    def this(*shape):
        return pl.BlockSpec((1,) + shape, lambda r, me: (row,) + (0,) * len(shape))

    some = piece // parts
    turned = (this(width, length), (rows, width, length), bf16)
    plain = (this(length, width), (rows, length, width), bf16)
    outs = (
        [(this(some, width), (rows, some, width), bf16)] * slots
        + [(this(1, length), (rows, 1, length), jnp.int32)]
        + [turned, plain, plain, plain, turned]
        + [
            (this(width, slots * some), (rows, width, slots * some), bf16),
            (this(HEADS, slots * some), (rows, HEADS, slots * some), f32),
        ]
    )
    result = call(
        functools.partial(attend_first_kernel, parts, slots, len(old)),
        "attend_first",
        (1,),
        [per_row(packed, width)] * slots
        + [
            pl.BlockSpec((width, LANES), lambda r, me: (0, 4 * width // LANES)),
            whole(width, 3 * width),
        ]
        + [pl.BlockSpec(memory_space=pl.ANY)] * len(old),
        outs,
        [((2 * width, width), bf16)] + attend_scratch(length, piece, parts),
        (me, *x_slots, weights, weights, *old),
        12,
        {3 + slots + i: i for i in range(len(old))},
    )
    return result


def attend_next(me, part, parts, projected, slots):
    segment_rows, q_t, k, _, _, v_t = projected
    rows, length, width = k.shape
    piece = length // slots
    att, more = attend_outs(rows, slots, piece // parts, width)
    result = call(
        functools.partial(attend_next_kernel, part, parts, slots),
        "attend_next",
        (rows,),
        [
            per_row(1, length),
            per_row(width, length),
            per_row(length, width),
            per_row(width, length),
        ],
        att + more,
        attend_scratch(length, piece, parts),
        (me, segment_rows, q_t, k, v_t),
        28 / parts,
    )
    return result[:slots], result[slots:]


def attend_back_kernel(row, last, parts, slot_count, *refs):
    me_ref = refs[0]
    x_refs = refs[1 : 1 + slot_count]
    rest = refs[1 + slot_count :]
    do_refs, rest = rest[: parts * slot_count], rest[parts * slot_count :]
    seg_ref, gain_ref, w_ref, qt_ref, k_ref, v_ref, q_ref = rest[:7]
    ot_refs, lse_refs = rest[7 : 7 + parts], rest[7 + parts : 7 + 2 * parts]
    rest = rest[7 + 2 * parts :]
    if row:
        before_ref, rest = rest[0], rest[1:]
    gf_refs, rest = rest[:slot_count], rest[slot_count:]
    dw_refs, rest = rest[: 1 + last], rest[1 + last :]
    (
        k_aux, q_aux, v_aux, causal, do, first_t, work_t, k_t, grads, prob, grad_score, delta, lse
    ) = rest
    width = w_ref.shape[0]
    piece = x_refs[0].shape[1] - MARKS
    some = piece // parts
    length = piece * slot_count
    me = me_ref[0]
    score_scale = 1.0 / math.sqrt(width // HEADS)
    causal[...] = causal_bias()
    lane = lax.broadcasted_iota(jnp.int32, (length, LANES), 1)
    v_aux[...] = jnp.where(lane < 3, 1.0, 0.0).astype(bf16)
    for part in range(parts):
        for i in range(slot_count):
            held = pl.ds(i * some, some)
            lse[:, pl.ds(i * piece + part * some, some)] = lse_refs[part][0, :, held]

    segment_row = seg_ref[0]
    q_aux[...] = query_features(segment_row, length)
    k_aux[...] = key_features(segment_row, length)
    gain = gain_ref[...]
    for j in range(slot_count):
        place = pl.ds(pl.multiple_of((me ^ j) * piece, piece), piece)
        normed, _ = normalize(x_refs[j][0, :piece].astype(f32))
        first_t[:, place] = (normed * gain).astype(bf16).T
        k_t[:, place] = k_ref[0, place].T
        for part in range(parts):
            start = (me ^ j) * piece + part * some
            place = pl.ds(pl.multiple_of(start, some), some)
            held = pl.ds(pl.multiple_of((me ^ j) * some, some), some)
            grad = do_refs[part * slot_count + j][0]
            do[place] = grad
            turned = grad.T
            work_t[:, place] = turned
            product = turned.astype(f32) * ot_refs[part][0, :, held].astype(f32)
            delta[:, place] = jnp.sum(product.reshape(HEADS, width // HEADS, some), axis=1)
    lane = lax.broadcasted_iota(jnp.int32, (1, LANES), 1)
    feature = lax.broadcasted_iota(jnp.int32, (16, BLOCK), 0)
    blocks = length // BLOCK

    def head_pair(pair, carry):
        base = pl.multiple_of(pair * LANES, LANES)
        for odd in range(2):
            rows = pl.ds(pl.multiple_of(pair * LANES + odd * 64, 64), 64)
            head = pl.ds(pair * 2 + odd, 1)
            for qb in range(blocks):
                queries = pl.ds(qb * BLOCK, BLOCK)
                a, b, c = split3(lse[head, queries])
                feats = jnp.where(feature == 7, -a, q_aux[:, queries])
                feats = jnp.where(feature == 8, -b, jnp.where(feature == 9, -c, feats))
                query = padded_head(qt_ref[0, rows, queries], feats.astype(bf16), odd)
                a, b, c = split3(delta[head, queries])
                feats = jnp.where(feature == 0, -a, jnp.where(feature == 1, -b, 0.0))
                feats = jnp.where(feature == 2, -c, feats)
                grad = padded_head(work_t[rows, queries], feats.astype(bf16), odd)
                held = pl.ds(odd * length + qb * BLOCK, BLOCK)
                for kb in range(qb + 1):
                    keys = pl.ds(kb * BLOCK, BLOCK)
                    key = jnp.concatenate([k_ref[0, keys, pl.ds(base, LANES)], k_aux[keys]], axis=1)
                    score = dot(key, query)
                    if kb == qb:
                        score = score + causal[...]
                    value = jnp.concatenate(
                        [v_ref[0, keys, pl.ds(base, LANES)], v_aux[keys]], axis=1
                    )
                    grad_prob = dot(value, grad)
                    weight = jnp.exp2(score)
                    prob[keys, held] = weight.astype(bf16)
                    grad_score[keys, held] = (weight * grad_prob).astype(bf16)
                end = (qb + 1) * BLOCK
                grad_q = dot(k_t[rows, 0:end], grad_score[0:end, held])
                work_t[rows, queries] = (grad_q * score_scale).astype(bf16)
        for kb in range(blocks):
            keys = pl.ds(kb * BLOCK, BLOCK)
            later = pl.ds(kb * BLOCK, length - kb * BLOCK)
            grad_v = jnp.zeros((BLOCK, LANES), f32)
            grad_k = jnp.zeros((BLOCK, LANES), f32)
            for odd in range(2):
                mine = (lane >= 64) if odd else (lane < 64)
                held = pl.ds(odd * length + kb * BLOCK, length - kb * BLOCK)
                zero = jnp.zeros((), bf16)
                grad = jnp.where(mine, do[later, pl.ds(base, LANES)], zero)
                query = jnp.where(mine, q_ref[0, later, pl.ds(base, LANES)], zero)
                grad_v = grad_v + dot(prob[keys, held], grad)
                grad_k = grad_k + dot(grad_score[keys, held], query)
            grads[keys, pl.ds(pl.multiple_of(width + pair * LANES, LANES), LANES)] = (
                grad_k * LN2
            ).astype(bf16)
            grads[keys, pl.ds(pl.multiple_of(2 * width + pair * LANES, LANES), LANES)] = (
                grad_v.astype(bf16)
            )
        return carry

    lax.fori_loop(0, HEADS // 2, head_pair, 0)
    for j in range(slot_count):
        place = pl.ds(pl.multiple_of((me ^ j) * piece, piece), piece)
        grads[place, :width] = work_t[:, place].T
        gf_refs[j][0] = dot(grads[place], w_ref[...], NT).astype(bf16)
    update = dot(first_t[...], grads[...])
    if row:
        update = before_ref[...] + update
    if last:
        keep, send = by_core(me, update.reshape(-1, 2, *dw_refs[0].shape[1:]))
        dw_refs[0][...] = keep
        dw_refs[1][...] = send.astype(bf16)
    else:
        dw_refs[0][...] = update


def attend_back(me, row, rows, shards, x_slots, do_parts, gain, w_qkv, projected, kept, before):
    slot_count, parts = len(x_slots), len(do_parts)
    _, packed, width = x_slots[0].shape
    piece = packed - MARKS
    length = piece * slot_count
    some = piece // parts
    last = row == rows - 1

    def this(*shape):
        return pl.BlockSpec((1,) + shape, lambda r, me: (row,) + (0,) * len(shape))

    half = (shards // 2, width // shards, 3 * width)
    outs = [(per_row(piece, width), (1, piece, width), bf16)] * slot_count
    if last:
        outs += [(whole(*half), half, f32), (whole(*half), half, bf16)]
    else:
        outs += [(whole(width, 3 * width), (width, 3 * width), f32)]
    segment_rows, q_t, k, v, q, _ = projected
    result = call(
        functools.partial(attend_back_kernel, row, last, parts, slot_count),
        "attend_back",
        (1,),
        [per_row(packed, width)] * slot_count
        + [this(some, width)] * (parts * slot_count)
        + [this(1, length), whole(1, width), whole(width, 3 * width)]
        + [this(width, length)]
        + [this(length, width)] * 3
        + [this(width, some * slot_count)] * parts
        + [this(HEADS, some * slot_count)] * parts
        + ([whole(width, 3 * width)] if row else []),
        outs,
        [
            ((length, LANES), bf16),
            ((16, length), f32),
            ((length, LANES), bf16),
            ((BLOCK, BLOCK), f32),
            ((length, width), bf16),
            ((width, length), bf16),
            ((width, length), bf16),
            ((width, length), bf16),
            ((length, 3 * width), bf16),
            ((length, 2 * length), bf16),
            ((length, 2 * length), bf16),
            ((HEADS, length), f32),
            ((HEADS, length), f32),
        ],
        (
            me,
            *x_slots,
            *[do for part in do_parts for do in part],
            segment_rows,
            gain,
            w_qkv,
            q_t,
            k,
            v,
            q,
            *[o for o, _ in kept],
            *[l for _, l in kept],
            *([before] if row else []),
        ),
        28,
    )
    return result[:slot_count], result[slot_count:]


def middle_of(att_refs, inputs_ref, w_out, me):
    rows, piece, width = att_refs[0].shape
    attended = jnp.concatenate([ref[...] for ref in att_refs], axis=0)
    attended = attended.reshape(-1, width)
    origin = jnp.concatenate(
        [inputs_ref[pl.ds((me ^ j) * rows, rows)] for j in range(len(att_refs))], axis=0
    ).reshape(-1, width)
    return attended, origin.astype(f32) + dot(attended, w_out)


def diagonal(piece):
    place = lax.broadcasted_iota(jnp.int32, (piece, LANES), 0)
    lane = lax.broadcasted_iota(jnp.int32, (piece, LANES), 1)
    return place == lane % piece, lane // piece, lane


def mix_kernel(slot_count, experts, *refs):
    me_ref = refs[0]
    att_refs = refs[1 : 1 + slot_count]
    inputs_ref, cot_ref, w_out_ref, gain_ref, control_ref = refs[1 + slot_count : 6 + slot_count]
    rest = refs[6 + slot_count :]
    pay_refs = rest[:experts]
    second_ref, middle_ref = rest[experts:]
    rows, piece, width = att_refs[0].shape
    tokens = rows * slot_count
    me = me_ref[0]
    _, middle = middle_of(att_refs, inputs_ref, w_out_ref[...], me)
    normed, _ = normalize(middle)
    second = (normed * gain_ref[...]).astype(bf16)
    second_ref[...] = second.reshape(tokens, piece, width)
    middle_ref[...] = middle.reshape(tokens, piece, width)
    grad = jnp.concatenate(
        [cot_ref[pl.ds((me ^ j) * rows, rows)] for j in range(slot_count)], axis=0
    ).reshape(-1, width)
    logits = dot(second, control_ref[...], NT).reshape(tokens, piece, LANES)
    top = jnp.max(logits, axis=0)
    weights = jnp.exp(logits - top)
    total = jnp.sum(weights, axis=0)
    log_total = top + jnp.log(total)
    own, _, lane = diagonal(piece)
    weights = jnp.where(own, weights * (1.0 / total), 0.0)
    spread_out = weights.reshape(-1, LANES).astype(bf16)
    mixed = dot(spread_out, second, TN).astype(bf16)
    grad_results = dot(spread_out, grad, TN).astype(bf16)
    a, b, c = split3(log_total)
    for e in range(experts):
        mine = slice(e * piece, (e + 1) * piece)
        first = slice(e * piece, e * piece + 1)
        stats = jnp.where(lane == 0, a[:, first], jnp.where(lane == 1, b[:, first], c[:, first]))
        pay_refs[e][:, :width] = mixed[mine]
        pay_refs[e][:, width : 2 * width] = grad_results[mine]
        pay_refs[e][:, 2 * width :] = stats.astype(bf16)


def mix(me, part, att_slots, inputs, cotangent, w_out, gain, control, experts):
    slot_count = len(att_slots)
    rows, positions, width = att_slots[0].shape
    tokens = rows * slot_count
    piece = LANES // experts
    steps = positions // piece
    span = pl.BlockSpec((tokens, piece, width), lambda b, me: (0, b, 0))
    shifted = pl.BlockSpec((tokens, piece, width), lambda b, me: (0, part * steps + b, 0))
    pay = (
        pl.BlockSpec((piece, 2 * width + LANES), lambda b, me: (b, 0)),
        (positions, 2 * width + LANES),
        bf16,
    )
    result = call(
        functools.partial(mix_kernel, slot_count, experts),
        "mix",
        (steps,),
        [pl.BlockSpec((rows, piece, width), lambda b, me: (0, b, 0))] * slot_count
        + [shifted, shifted, fourth(width), whole(1, width), whole(LANES, width)],
        [pay] * experts
        + [
            (span, (tokens, positions, width), bf16),
            (span, (tokens, positions, width), f32),
        ],
        [],
        (me, *att_slots, inputs, cotangent, w_out, gain, control),
        positions * 12 / 256,
    )
    return result[:experts], result[experts], result[experts + 1]


def expert_kernel(part, parts, tiled, slot_count, *refs):
    me_ref = refs[0]
    pay_refs = refs[1 : 1 + slot_count]
    rest = refs[1 + slot_count :]
    count = 4 if tiled else 2
    weight_refs, rest = rest[:count], rest[count:]
    expand_ref = weight_refs[0]
    last = part == parts - 1
    earlier, rest = rest[: 4 * part], rest[4 * part :]
    if last:
        back_ref, keep_ref, send_ref = rest[:3]
        mixed_acc, grad_acc, result_acc, back_acc, stat, *more, mixed_low, grad_low = rest[3:]
    else:
        back_ref, mixed_low, grad_low, hidden_ref, pre_ref = rest[:5]
        mixed_acc, grad_acc, result_acc, back_acc, stat, *more = rest[5:]
    me = me_ref[0]
    width = expand_ref.shape[-1]
    step = pl.program_id(0)

    @pl.when(step == 0)
    def _():
        logs = []
        for j in range(slot_count):
            stats = pay_refs[j][:, 2 * width :].astype(f32)
            logs.append(stats[:, 0:1] + stats[:, 1:2] + stats[:, 2:3])
        top = functools.reduce(jnp.maximum, logs)
        total = functools.reduce(jnp.add, [jnp.exp(log - top) for log in logs])
        log_total = top + jnp.log(total)
        mixed, grad = 0.0, 0.0
        for j in range(slot_count):
            share = jnp.exp(logs[j] - log_total)
            mixed = mixed + share * pay_refs[j][:, :width].astype(f32)
            grad = grad + share * pay_refs[j][:, width : 2 * width].astype(f32)
        mixed_acc[...] = mixed
        grad_acc[...] = grad
        mixed_low[...] = mixed.astype(bf16)
        grad_low[...] = grad.astype(bf16)
        result_acc[...] = jnp.zeros_like(result_acc)
        back_acc[...] = jnp.zeros_like(back_acc)
        stat[...] = jnp.broadcast_to(log_total, stat.shape)

    mixed, grad = mixed_low[...], grad_low[...]
    if tiled:
        for i in range(2):
            own, other = weight_refs[2 * i][...], weight_refs[2 * i + 1][...]
            odd = me % 2 == 1
            more[i][:, 0] = jnp.where(odd, other, own)
            more[i][:, 1] = jnp.where(odd, own, other)
        expand, shrink = [ref[...].reshape(-1, width) for ref in more]
    else:
        expand, shrink = [ref[...].reshape(-1, width) for ref in weight_refs]
    value = dot(mixed, expand)
    coeff = math.sqrt(2.0 / math.pi)
    square = value * value
    turn = jnp.tanh(coeff * (value + 0.044715 * (square * value)))
    half = 0.5 * (1.0 + turn)
    hidden = (value * half).astype(bf16)
    slope = half + (0.5 * coeff) * value * (1.0 - turn * turn) * (1.0 + (3 * 0.044715) * square)
    result_acc[...] += dot(hidden, shrink)
    grad_pre = (dot(grad, shrink, NT) * slope).astype(bf16)
    back_acc[...] += dot(grad_pre, expand, NT)
    if last:
        sets = [earlier[4 * i : 4 * i + 4] for i in range(part)]
        mixed = jnp.concatenate([m[...] for m, _, _, _ in sets] + [mixed], axis=0)
        grad = jnp.concatenate([g[...] for _, g, _, _ in sets] + [grad], axis=0)
        hidden = jnp.concatenate([h[...] for _, _, h, _ in sets] + [hidden], axis=0)
        grad_pre = jnp.concatenate([p[...] for _, _, _, p in sets] + [grad_pre], axis=0)
        grad_expand = dot(mixed, grad_pre, TN).astype(bf16)
        grad_shrink = dot(hidden, grad, TN).astype(bf16)
        if tiled:
            shards = 2 * keep_ref.shape[0]
            lines = width // shards
            both = keep_ref.shape[1]
            keep, send = by_core(me, grad_expand.reshape(shards // 2, 2, lines, width))
            place = pl.ds(pl.multiple_of(step * lines, lines), lines)
            keep_ref[:, place] = keep
            send_ref[:, place] = send
            count = 2 * width // both // 2
            keep, send = by_core(me, grad_shrink.reshape(count, 2, both // 2, width))
            place = pl.ds(step * count, count)
            keep_ref[place, both // 2 :] = keep
            send_ref[place, both // 2 :] = send
        else:
            keep_ref[...] = grad_expand.reshape(keep_ref.shape)
            send_ref[...] = grad_shrink.reshape(send_ref.shape)
    else:
        hidden_ref[...] = hidden
        pre_ref[...] = grad_pre

    @pl.when(step == pl.num_programs(0) - 1)
    def _():
        results = result_acc[...].astype(bf16)
        back = back_acc[...].astype(bf16)
        back_ref[:, :width] = results
        back_ref[:, width : 2 * width] = back
        inner = jnp.sum(
            results.astype(f32) * grad_acc[...] + back.astype(f32) * mixed_acc[...],
            axis=-1,
            keepdims=True,
        )
        lane = lax.broadcasted_iota(jnp.int32, stat.shape, 1)
        a, b, c = split3(stat[...])
        d, e, f = split3(inner)
        stats = jnp.where(lane == 0, a, jnp.where(lane == 1, b, c))
        stats = jnp.where(lane < 3, stats, jnp.where(lane == 3, d, jnp.where(lane == 4, e, f)))
        back_ref[:, 2 * width :] = stats.astype(bf16)


def pack_expert(expand, shrink):
    experts, lines, hidden = expand.shape
    width = shrink.shape[-1]
    expand = expand.reshape(experts, lines, hidden // width, width)
    expand = jnp.swapaxes(expand, 1, 2).reshape(experts, -1, width)
    return jnp.concatenate([expand, shrink], axis=1)


def unpack_expert(packed, lines):
    experts, both, width = packed.shape
    expand = packed[:, : both // 2].reshape(experts, -1, lines, width)
    expand = jnp.swapaxes(expand, 1, 2).reshape(experts, lines, -1)
    return expand, packed[:, both // 2 :]


def expert(me, core, part, parts, pay_slots, halves, earlier):
    slot_count = len(pay_slots)
    groups, packed = pay_slots[0].shape
    shards = 2 * halves[0][0].shape[0]
    tail, width = halves[0][0].shape[1:]
    hidden = shards * tail
    chunks = hidden // width
    lines = width // shards
    acc = ((groups, width), f32)
    low = ((groups, width), bf16)
    tiled = lines % 16 == 0
    group = shards // chunks // 2
    if tiled:
        columns = pl.BlockSpec((shards // 2, lines, width), lambda f, me: (0, f, 0))
        lower = pl.BlockSpec((group, tail, width), lambda f, me: (f, 0, 0))
        weights = [*halves[0], *halves[1]]
        specs = [columns, columns, lower, lower]
        built = [((shards // 2, 2, lines, width), bf16), ((group, 2, tail, width), bf16)]
        both = (shards // 2, 2 * tail, width)
        grads = [(whole(*both), both, bf16)] * 2
    else:
        odd = core == 1
        weights = [
            jnp.stack([jnp.where(odd, b, a), jnp.where(odd, a, b)], axis=1) for a, b in halves
        ]
        expand = weights[0].reshape(shards, chunks, lines, width)
        expand = jnp.swapaxes(expand, 0, 1).reshape(chunks, width, width)
        weights = [expand, weights[1].reshape(chunks, width, width)]
        specs = [pl.BlockSpec((1, width, width), lambda f, me: (f, 0, 0))] * 2
        built = []
        grads = [(specs[0], (chunks, width, width), bf16)] * 2
    token = whole(groups, width)
    inner = pl.BlockSpec((groups, width), lambda f, me: (0, f))
    last = part == parts - 1
    outs = [(whole(groups, packed), (groups, packed), bf16)]
    scratch = [acc, acc, acc, acc, ((groups, LANES), f32)] + built
    if last:
        outs += grads
        scratch += [low, low]
    else:
        outs += [(token, (groups, width), bf16)] * 2 + [(inner, (groups, hidden), bf16)] * 2
    result = call(
        functools.partial(expert_kernel, part, parts, tiled, slot_count),
        "expert",
        (chunks,),
        [whole(groups, packed)] * slot_count + specs + [token, token, inner, inner] * part,
        outs,
        scratch,
        (me, *pay_slots, *weights, *earlier),
        7,
    )
    more = list(result[1:])
    if last and not tiled:
        grad = jnp.swapaxes(more[0].reshape(chunks, shards, lines, width), 0, 1)
        more = [grad.reshape(shards, tail, width), more[1].reshape(shards, tail, width)]
        more = jnp.concatenate(more, axis=1).reshape(shards // 2, 2, 2 * tail, width)
        odd = core == 1
        more = [
            jnp.where(odd, more[:, 1], more[:, 0]),
            jnp.where(odd, more[:, 0], more[:, 1]),
        ]
    return result[0], more


def unmix_kernel(slot_count, experts, part, last, *refs):
    me_ref = refs[0]
    ret_refs = refs[1 : 1 + experts]
    att_refs = refs[1 + experts : 1 + experts + slot_count]
    rest = refs[1 + experts + slot_count :]
    second_ref, middle_ref, cot_ref, w_out_ref, gain_ref, control_ref = rest[:6]
    rest = rest[6:]
    if part:
        old_out_ref, old_control_ref, old_gain_ref = rest[2:5]
        rest = rest[5:]
    out_ref, grad_middle_ref = rest[:2]
    back_refs = rest[2 : 2 + slot_count]
    rest = rest[2 + slot_count :]
    if last:
        keep_ref, send_ref, grad_out_ref, grad_control_ref, grad_gain_ref, small = rest
    else:
        grad_out_ref, grad_control_ref, grad_gain_ref = rest
    rows, piece, width = att_refs[0].shape
    tokens = rows * slot_count
    me = me_ref[0]

    @pl.when(pl.program_id(0) == 0)
    def _():
        if part:
            grad_out_ref[...] = old_out_ref[...]
            grad_control_ref[...] = old_control_ref[...]
            grad_gain_ref[...] = old_gain_ref[...]
        else:
            grad_out_ref[...] = jnp.zeros_like(grad_out_ref)
            grad_control_ref[...] = jnp.zeros_like(grad_control_ref)
            grad_gain_ref[...] = jnp.zeros_like(grad_gain_ref)

    second = second_ref[...].reshape(-1, width)
    middle = middle_ref[...].reshape(-1, width)
    cot = jnp.concatenate(
        [cot_ref[pl.ds((me ^ j) * rows, rows)] for j in range(slot_count)], axis=0
    ).reshape(-1, width)
    own, group, _ = diagonal(piece)
    log_total = jnp.zeros((piece, LANES), f32)
    inner = jnp.zeros((piece, LANES), f32)
    for e in range(experts):
        stats = ret_refs[e][:, 2 * width :].astype(f32)
        mine = group == e
        log_total = jnp.where(mine, stats[:, 0:1] + stats[:, 1:2] + stats[:, 2:3], log_total)
        inner = jnp.where(mine, stats[:, 3:4] + stats[:, 4:5] + stats[:, 5:6], inner)
    results = jnp.concatenate([ref[:, :width] for ref in ret_refs], axis=0)
    back = jnp.concatenate([ref[:, width : 2 * width] for ref in ret_refs], axis=0)
    control = control_ref[...]
    logits = dot(second, control, NT).reshape(tokens, piece, LANES)
    weights = jnp.where(own, jnp.exp(logits - log_total), 0.0)
    low = weights.reshape(-1, LANES).astype(bf16)
    output = (middle + dot(low, results).astype(bf16).astype(f32)).astype(bf16)
    grad_weights = (dot(cot, results, NT) + dot(second, back, NT)).reshape(tokens, piece, LANES)
    grad_logits = (weights * (grad_weights - inner)).reshape(-1, LANES).astype(bf16)
    grad_second = dot(low, back) + dot(grad_logits, control)
    grad_second = grad_second.astype(bf16).astype(f32)
    grad_control_ref[...] += dot(grad_logits, second, TN)
    normed, scaled = normalize(middle)
    product = (grad_second * normed).reshape(-1, 8, width)
    grad_gain_ref[...] += jnp.sum(product, axis=0)
    grad_middle = cot.astype(f32) + norm_back(grad_second * gain_ref[...], normed, scaled)
    grad_middle = grad_middle.astype(bf16)
    grad_attended = dot(grad_middle, w_out_ref[...], NT).astype(bf16)
    output = output.reshape(tokens, piece, width)
    grad_attended = grad_attended.reshape(tokens, piece, width)
    grad_middle_ref[...] = grad_middle.reshape(tokens, piece, width)
    for j in range(slot_count):
        mine = slice(j * rows, (j + 1) * rows)
        out_ref[pl.ds((me ^ j) * rows, rows)] = output[mine]
        back_refs[j][...] = grad_attended[mine]
    attended = jnp.concatenate([ref[...] for ref in att_refs], axis=0).reshape(-1, width)
    grad_out_ref[...] += dot(attended, grad_middle, TN)

    if last:

        @pl.when(pl.program_id(0) == pl.num_programs(0) - 1)
        def _():
            small[...] = jnp.zeros_like(small)
            small[0:1] = jnp.sum(grad_gain_ref[...], axis=0, keepdims=True)
            for e in range(experts):
                total = grad_control_ref[e * piece : (e + 1) * piece]
                place = pl.ds(1 + (me_ref[1] ^ e), 1)
                small[place] = jnp.sum(total, axis=0, keepdims=True)
            blocks, lines = keep_ref.shape[:2]
            for columns, value in (
                (slice(0, width), grad_out_ref[...]),
                (slice(width, width + LANES), small[...].T),
            ):
                keep, send = by_core(me, value.reshape(blocks, 2, lines, -1))
                keep_ref[:, :, columns] = keep
                send_ref[:, :, columns] = send.astype(bf16)


def unmix(
    me, part, last, shards, ret_slots, att_slots, second, middle, cotangent, w_out, gain, control, before
):
    slot_count, experts = len(att_slots), len(ret_slots)
    rows, positions, width = att_slots[0].shape
    tokens = rows * slot_count
    piece = LANES // experts
    steps = positions // piece
    span = pl.BlockSpec((tokens, piece, width), lambda b, me: (0, b, 0))
    shifted = pl.BlockSpec((tokens, piece, width), lambda b, me: (0, part * steps + b, 0))
    slot = pl.BlockSpec((rows, piece, width), lambda b, me: (0, b, 0))
    full = (shifted, cotangent.shape, bf16)
    sums = [
        (whole(width, width), (width, width), f32),
        (whole(LANES, width), (LANES, width), f32),
        (whole(8, width), (8, width), f32),
    ]
    count = 1 + experts + slot_count + 6
    scratch = []
    made = sums
    if last:
        half = (shards // 2, width // shards, width + LANES)
        made = [(whole(*half), half, f32), (whole(*half), half, bf16)]
        scratch = [(shape, dtype) for _, shape, dtype in sums] + [((LANES, width), f32)]
    result = call(
        functools.partial(unmix_kernel, slot_count, experts, part, last),
        "unmix",
        (steps,),
        [pl.BlockSpec((piece, 2 * width + LANES), lambda b, me: (b, 0))] * experts
        + [slot] * slot_count
        + [span, span, shifted, fourth(width), whole(1, width), whole(LANES, width)]
        + ([pl.BlockSpec(memory_space=pl.ANY)] * 2 + [spec for spec, _, _ in sums] if part else []),
        [full, full] + [(slot, (rows, positions, width), bf16)] * slot_count + made,
        scratch,
        (me, *ret_slots, *att_slots, second, middle, cotangent, w_out, gain, control, *before),
        positions * 17 / 256,
        {count: 0, count + 1: 1} if part else None,
    )
    do_slots = result[2 : 2 + slot_count]
    return do_slots, result[:2] + result[2 + slot_count :]


def finish_kernel(slot_count, row_count, *refs):
    me_ref = refs[0]
    gf_refs = refs[1 : 1 + slot_count * row_count]
    inputs_ref, grad_middle_ref, gain_ref, out_ref = refs[1 + slot_count * row_count :]
    me = me_ref[0]
    for j in range(slot_count):
        for row in range(row_count):
            place = (me ^ j) * row_count + row
            normed, scaled = normalize(inputs_ref[place].astype(f32))
            incoming = gf_refs[row * slot_count + j][0].astype(f32) * gain_ref[...]
            grad = norm_back(incoming, normed, scaled)
            grad = grad + grad_middle_ref[j * row_count + row].astype(f32)
            out_ref[place] = grad.astype(bf16)


def finish(me, gf_rows, inputs, grad_middle, gain):
    slot_count, row_count = len(gf_rows[0]), len(gf_rows)
    tokens, positions, width = inputs.shape
    piece = 64
    span = pl.BlockSpec((tokens, piece, width), lambda b, me: (0, b, 0))
    slot = pl.BlockSpec((1, piece, width), lambda b, me: (0, b, 0))
    return call(
        functools.partial(finish_kernel, slot_count, row_count),
        "finish",
        (positions // piece,),
        [slot] * (slot_count * row_count) + [span, span, whole(1, width)],
        [(span, (tokens, positions, width), bf16)],
        [],
        (me, *[gf for row in gf_rows for gf in row], inputs, grad_middle, gain),
        6,
    )[0]


def on_device(
    sizes,
    inputs,
    segments,
    cotangent,
    gain_attn,
    w_qkv,
    w_out,
    gain_mix,
    w_control,
    w_expand,
    w_shrink,
):
    groups, members, slots = sizes
    local_rows, positions, width = inputs.shape
    experts = w_expand.shape[0]
    rows = local_rows // slots
    place = (("gq", groups), ("gi", members), ("seq", slots))
    owners = (("gq", groups), ("seq", slots))
    seq_me = lax.axis_index("seq")
    member = lax.axis_index("gi")
    me = jnp.stack([seq_me, member]).astype(jnp.int32)

    parts = 2 if positions % BLOCK == 0 else 1

    def row_parts(array):
        return [
            lax.dynamic_slice_in_dim(array, (seq_me ^ j) * rows, rows, axis=0) for j in range(slots)
        ]

    marks = segments.astype(bf16)[:, None, :]
    marks = jnp.pad(marks, ((0, 0), (0, MARKS - 1), (0, width - positions)))
    x_parts = row_parts(jnp.concatenate([inputs, marks], axis=1))
    x_parts = [[x[row : row + 1] for x in x_parts] for row in range(rows)]
    x_rows = [[x_parts[0][0]]]

    def send_some(slots_of, done, first, last):
        for j in range(first, last):
            done.append(partner(slots_of[j], "seq", slots, j))

    small = jnp.concatenate([gain_attn[None], gain_mix[None], w_control], axis=0)
    small = jnp.pad(jnp.transpose(small), ((0, 0), (0, LANES - 2 - experts)))
    packed = jnp.concatenate([w_qkv, w_out, small], axis=1).astype(bf16)
    packed = Doubling(packed, place, ("seq", "gq", "core"))
    send_some(x_parts[0], x_rows[0], 1, slots // 2 + 1)
    packed.steps("seq")
    x_rows, x_parts, w_expand, w_shrink = together((x_rows, x_parts, w_expand, w_shrink), packed)

    def member_parts(array):
        return [
            lax.dynamic_index_in_dim(array, member ^ j, 0, keepdims=False) for j in range(members)
        ]

    send_some(x_parts[0], x_rows[0], slots // 2 + 1, slots)
    weights = member_parts(pack_expert(w_expand.astype(bf16), w_shrink.astype(bf16)))
    weights = swap_slots(weights, "gi")
    packed.steps("gq")
    x_rows, x_parts, weights = together((x_rows, x_parts, weights), packed)
    packed.at_once("gi")
    weights = jnp.stack(natural(weights, member))
    x_rows, x_parts, weights = together((x_rows, x_parts, weights), packed)
    packed.steps("core")
    x_rows, x_parts, weights = together((x_rows, x_parts, weights), packed)
    tail = weights.shape[1] // 2
    halves = [
        Doubling(half, owners, ("gq", "seq"), 1) for half in (weights[:, :tail], weights[:, tail:])
    ]
    halves[0].steps("gq")
    packed = packed.value.reshape(width, -1)

    old = []
    for row in range(rows):
        old = attend_first(me, row, rows, x_rows[row], packed, parts, old)
        if row + 1 < rows:
            x_rows.append(swap_slots(x_parts[row + 1], "seq"))
            old, x_rows[row + 1] = together((old, x_rows[row + 1]), *halves)
        if row == max(0, rows - 2):
            halves[0].steps("seq")
            halves[1].steps("gq")
        if row == rows - 1:
            old = together(old, *halves)
    vectors = jnp.transpose(packed[:, 4 * width :])
    gain_one = vectors[0:1].astype(f32)
    gain_two = vectors[1:2].astype(f32)
    control = natural([vectors[2 + e : 3 + e] for e in range(experts)], member)
    control = jnp.concatenate(
        [jnp.broadcast_to(c, (LANES // experts, width)) for c in control], axis=0
    )
    att, projected, kept = old[:slots], old[slots : slots + 6], old[slots + 6 :]
    att_parts, kept = [swap_slots(att, "seq")], [kept]
    for part in range(1, parts):
        att, more = attend_next(me, part, parts, projected, slots)
        more, att_parts[-1], gain_one, gain_two, control = hold(
            (more, att_parts[-1], gain_one, gain_two, control)
        )
        att_parts.append(swap_slots(att, "seq"))
        kept.append(more)
    pay_parts, second_parts, middle_parts = [], [], []
    for part in range(parts):
        pay, second, middle = mix(
            me, part, att_parts[part], inputs, cotangent, packed, gain_two, control, experts
        )
        if part + 1 < parts:
            pay, second, middle, att_parts[part + 1] = together(
                (pay, second, middle, att_parts[part + 1]), halves[1]
            )
        if part == 0:
            halves[1].steps("seq")
        if part == parts - 1:
            pay, second, middle, pay_parts = together((pay, second, middle, pay_parts), halves[1])
        pay_parts.append(swap_slots(pay, "gi"))
        second_parts.append(second)
        middle_parts.append(middle)
    halves = [half.value.reshape(-1, *half.value.shape[-2:]) for half in halves]
    halves = [(half, partner(half, "seq", slots, 1)) for half in halves]
    ret_parts, earlier = [], []
    for part in range(parts):
        back, more = expert(me, seq_me % 2, part, parts, pay_parts[part], halves, earlier)
        earlier = earlier + list(more)
        if part + 1 < parts:
            pay_parts[part + 1][1], back = hold((pay_parts[part + 1][1], back))
        elif part:
            back, more, ret_parts = hold((back, more, ret_parts))
        ret_parts.append(swap_slots([back] * members, "gi"))

    kept_grad, send = more
    received = partner(send, "seq", slots, 1)
    bits = [2] * len(bits_of((("gq", groups),)))
    bits += [members] + [2] * (len(bits_of((("seq", slots),))) - 1)

    def to_bits(keep, other):
        return (keep.astype(f32) + other.astype(f32)).reshape(*bits, *keep.shape[1:])

    do_parts, before = [], []
    for part in range(parts):
        last = part == parts - 1
        if last:
            sum_expert = Halving(to_bits(kept_grad, received), owners, ("seq", "gq"), 1)
            sum_expert.prepare()
            ret_parts[part], before = together((ret_parts[part], before), sum_expert)
        do, before = unmix(
            me,
            part,
            last,
            groups * members * slots,
            ret_parts[part],
            att_parts[part],
            second_parts[part],
            middle_parts[part],
            cotangent,
            packed,
            gain_two,
            control,
            before,
        )
        do_parts.append(swap_slots(do, "seq"))
    output, grad_middle, keep_out, send_out = before
    every_bit = [2] * len(bits_of(place))
    do_parts, send_out = together((do_parts, send_out), sum_expert)
    sum_expert.exchange()
    received_out = partner(send_out, "seq", slots, 1)

    gf_rows, grad_in = [], None
    for row in range(rows):
        gf_slots, grad_in = attend_back(
            me,
            row,
            rows,
            groups * members * slots,
            x_rows[row],
            do_parts,
            gain_one,
            packed,
            projected,
            kept,
            grad_in,
        )
        grad_in = grad_in[0] if row < rows - 1 else grad_in
        if row == 0:
            gf_slots, grad_in, received_out = together((gf_slots, grad_in, received_out), sum_expert)
            sum_expert.combine()
            while sum_expert.order[0][0] == "seq":
                sum_expert.step(sum_expert.order.pop(0))
            sum_expert.prepare()
            gf_slots, grad_in = together((gf_slots, grad_in), sum_expert)
            sum_expert.exchange()
        if row:
            gf_slots, grad_in, gf_rows = together((gf_slots, grad_in, gf_rows), sum_expert)
        if row < rows - 1:
            gf_rows.append(swap_slots(gf_slots, "seq"))
    gf_rows.append([gf_slots[0]])
    send_some(gf_slots, gf_rows[-1], 1, slots // 2 + 1)
    keep, send = grad_in
    received = partner(send, "seq", slots, 1)
    gf_rows, gf_slots, received = hold((gf_rows, gf_slots, received))
    send_some(gf_slots, gf_rows[-1], slots // 2 + 1, slots)
    total = keep + received.astype(f32)
    total = jnp.concatenate([total, keep_out + received_out.astype(f32)], axis=-1)
    total = total.reshape(*every_bit[1:], *total.shape[1:])
    sum_in = Halving(total, place, ("gi", "gq", "seq"))
    sum_in.at_once(("gi",))
    gf_rows = together(gf_rows, sum_in, sum_expert)
    sum_in.combine()
    sum_in.at_once(("gq", "seq"))
    sum_expert.combine()
    sums = sum_expert.finish()
    columns = [p if j == 0 else p.astype(bf16) for j, p in enumerate(member_parts(sums))]
    columns = swap_slots(columns, "gi")
    grad_inputs = finish(me, gf_rows, inputs, grad_middle, gain_one)
    grad_inputs, columns = together((grad_inputs, columns), sum_in)
    sum_in.combine()
    columns = natural(columns, member)
    columns = jnp.stack([c.astype(f32) for c in columns])
    grad_expand, grad_shrink = unpack_expert(columns, width // (groups * members * slots))
    total = sum_in.finish()
    grad_in, grad_out = total[:, : 3 * width], total[:, 3 * width :]
    small = jnp.transpose(grad_out[:, width:])
    weighted = jnp.sum(grad_in * w_qkv.astype(bf16).astype(f32), axis=1)
    return (
        output,
        grad_inputs,
        weighted / gain_attn.astype(bf16).astype(f32),
        grad_in,
        grad_out[:, :width],
        small[0],
        small[1 : 1 + experts],
        grad_expand,
        grad_shrink,
    )


def solution(mesh):
    dp_count, seq_count = mesh.shape["dp"], mesh.shape["seq"]

    def run(inputs, *args):
        members = GROUP * dp_count // inputs.shape[0]
        sizes = (dp_count // members, members, seq_count)
        fine = Mesh(mesh.devices.reshape(sizes), ("gq", "gi", "seq"))
        dp, both = ("gq", "gi"), ("gq", "gi", "seq")
        return jax.shard_map(
            functools.partial(on_device, sizes),
            mesh=fine,
            in_specs=(
                P(dp, "seq", None),
                P(dp, "seq"),
                P(dp, "seq", None),
                P(both),
                P(both, None),
                P(both, None),
                P(both),
                P(None, both),
                P(None, both, None),
                P(None, both, None),
            ),
            out_specs=(
                P(dp, "seq", None),
                P(dp, "seq", None),
                P(both),
                P(both, None),
                P(both, None),
                P(both),
                P(None, both),
                P(None, both, None),
                P(None, both, None),
            ),
            check_vma=False,
        )(inputs, *args)

    return run
```

```python
import functools
import math

import jax
import jax.numpy as jnp
from jax import lax
from jax.experimental import pallas as pl
from jax.experimental.pallas import tpu as pltpu
from jax.sharding import Mesh
from jax.sharding import PartitionSpec as P

HEADS = 8
GROUP = 32
BLOCK = 256
LANES = 128
MARKS = 16

LOG2E = math.log2(math.e)
LN2 = math.log(2.0)
BIG = 1e30

bf16 = jnp.bfloat16
f32 = jnp.float32

NN = (((1,), (0,)), ((), ()))
NT = (((1,), (1,)), ((), ()))
TN = (((0,), (0,)), ((), ()))


def dot(a, b, dims=NN):
    return lax.dot_general(a, b, dims, preferred_element_type=f32)


def normalize(values):
    center = values - jnp.mean(values, axis=-1, keepdims=True)
    scaled = lax.rsqrt(jnp.mean(center * center, axis=-1, keepdims=True) + 1e-05)
    return center * scaled, scaled


def norm_back(incoming, normed, scaled):
    return scaled * (
        incoming
        - jnp.mean(incoming, axis=-1, keepdims=True)
        - normed * jnp.mean(incoming * normed, axis=-1, keepdims=True)
    )


def split3(value):
    high = value.astype(bf16).astype(f32)
    rest = value - high
    mid = rest.astype(bf16).astype(f32)
    low = (rest - mid).astype(bf16).astype(f32)
    return high, mid, low


def partner(value, axis, size, mask):
    return lax.ppermute(value, axis, [(i, i ^ mask) for i in range(size)])


def swap_slots(slots, axis):
    size = len(slots)
    return [slots[0]] + [partner(slots[j], axis, size, j) for j in range(1, size)]


def natural(slots, me):
    out = list(slots)
    bit = 1
    while bit < len(out):
        flip = (me & bit) != 0
        out = [jnp.where(flip, out[k ^ bit], out[k]) for k in range(len(out))]
        bit *= 2
    return out


def bits_of(sizes):
    bits = []
    for axis, size in sizes:
        mask = size // 2
        while mask:
            bits.append((axis, size, mask))
            mask //= 2
    return bits


def named(bit):
    axis, _, mask = bit
    return "core" if axis == "seq" and mask == 1 else axis


class Steps:
    def __init__(self, value, sizes, order):
        self.order = [bit for axis in order for bit in reversed(bits_of(sizes)) if named(bit) == axis]
        self.value = value

    def steps(self, axis):
        while self.order and named(self.order[0]) == axis:
            self.step(self.order.pop(0))
        return self

    def finish(self):
        while self.order:
            self.step(self.order.pop(0))
        return self.value


class Doubling(Steps):
    def __init__(self, value, sizes, order, inner=0):
        super().__init__(value, sizes, order)
        self.inner = inner
        self.place = bits_of(sizes)
        self.have = []

    def step(self, bit):
        axis, size, mask = bit
        depth = sum(self.place.index(other) < self.place.index(bit) for other in self.have)
        depth += self.inner if axis == "seq" else 0
        other = partner(self.value, axis, size, mask)
        high = (lax.axis_index(axis) & mask) != 0
        first = jnp.where(high, other, self.value)
        second = jnp.where(high, self.value, other)
        self.value = jnp.stack([first, second], axis=depth)
        self.have.append(bit)

    def at_once(self, axis):
        bits = [bit for bit in self.place if bit[0] == axis]
        self.order = [bit for bit in self.order if bit[0] != axis]
        depth = sum(self.place.index(other) < self.place.index(bits[0]) for other in self.have)
        depth += self.inner if axis == "seq" else 0
        slots = natural(swap_slots([self.value] * 2 ** len(bits), axis), lax.axis_index(axis))
        shape = self.value.shape
        value = jnp.stack(slots, axis=depth)
        self.value = value.reshape(shape[:depth] + (2,) * len(bits) + shape[depth:])
        self.have += bits


class Halving(Steps):
    def __init__(self, value, sizes, order, inner=0):
        super().__init__(value, sizes, order)
        self.sizes = sizes
        self.left = [bit for bit in bits_of(sizes) if bit in self.order]
        self.inner = inner

    def prepare(self):
        bit = self.order.pop(0)
        depth = self.left.index(bit)
        self.left.pop(depth)
        axis, size, mask = bit
        depth += self.inner if axis == "seq" else 0
        high = ((lax.axis_index(axis) & mask) != 0).astype(jnp.int32)
        keep = lax.dynamic_index_in_dim(self.value, high, depth, keepdims=False)
        send = lax.dynamic_index_in_dim(self.value, 1 - high, depth, keepdims=False)
        self.value = (keep, send.astype(bf16))
        self.link = bit

    def exchange(self):
        axis, size, mask = self.link
        keep, send = self.value
        self.value = (keep, partner(send, axis, size, mask))

    def combine(self):
        self.value = functools.reduce(jnp.add, [part.astype(f32) for part in self.value])

    def step(self, bit):
        self.order.insert(0, bit)
        self.prepare()
        self.exchange()
        self.combine()

    def cut(self, axes):
        bits = [bit for bit in self.left if bit[0] in axes]
        self.order = [bit for bit in self.order if bit not in bits]
        depth = self.left.index(bits[0])
        if self.inner or bits != self.left[depth : depth + len(bits)]:
            raise NotImplementedError
        self.left = [bit for bit in self.left if bit not in bits]
        shape = self.value.shape
        value = self.value.reshape(shape[:depth] + (2 ** len(bits),) + shape[depth + len(bits) :])
        place = 0
        for axis, size, mask in bits:
            place = 2 * place + ((lax.axis_index(axis) & mask) != 0).astype(jnp.int32)
        parts = [
            lax.dynamic_index_in_dim(value, place ^ j, depth, keepdims=False)
            for j in range(2 ** len(bits))
        ]
        self.value = [parts[0]] + [part.astype(bf16) for part in parts[1:]]
        self.link = bits

    def send(self):
        bits = self.link
        sizes = [(axis, size) for axis, size in self.sizes if axis in [bit[0] for bit in bits]]
        names = tuple(axis for axis, _ in sizes)
        for j in range(1, 2 ** len(bits)):
            masks = {axis: 0 for axis in names}
            for i, (axis, _, mask) in enumerate(bits):
                if j >> (len(bits) - 1 - i) & 1:
                    masks[axis] |= mask
            pairs = []
            for source in range(math.prod(size for _, size in sizes)):
                target, rest, unit = 0, source, 1
                for axis, size in reversed(sizes):
                    target += ((rest % size) ^ masks[axis]) * unit
                    rest, unit = rest // size, unit * size
                pairs.append((source, target))
            self.value[j] = lax.ppermute(self.value[j], names, pairs)


hold = lax.optimization_barrier


def together(values, *sums):
    values, held = lax.optimization_barrier((values, [item.value for item in sums]))
    for item, value in zip(sums, held):
        item.value = value
    return values


def call(kernel, name, grid, in_specs, outs, scratch, args, micros, aliases=None, room=10):
    def full(shape):
        return pl.BlockSpec(shape, lambda *_: (0,) * len(shape))

    in_specs = [spec or full(arg.shape) for spec, arg in zip(in_specs, args[1:], strict=True)]
    outs = [(spec or full(shape), shape, dtype) for spec, shape, dtype in outs]
    return pl.pallas_call(
        kernel,
        grid_spec=pltpu.PrefetchScalarGridSpec(
            num_scalar_prefetch=1,
            grid=grid,
            in_specs=in_specs,
            out_specs=[spec for spec, _, _ in outs],
            scratch_shapes=[pltpu.VMEM(shape, dtype) for shape, dtype in scratch],
        ),
        out_shape=[jax.ShapeDtypeStruct(shape, dtype) for _, shape, dtype in outs],
        input_output_aliases=aliases or {},
        compiler_params=pltpu.CompilerParams(vmem_limit_bytes=room << 20),
        cost_estimate=pl.CostEstimate(
            flops=int(micros * 1e9), bytes_accessed=1 << 20, transcendentals=0
        ),
        name=name,
    )(*args)


def per_row(*shape):
    return pl.BlockSpec((1,) + shape, lambda r, me: (r,) + (0,) * len(shape))


def whole(*shape):
    return pl.BlockSpec(shape, lambda r, me: (0,) * len(shape))


def fourth(width):
    return pl.BlockSpec((width, width), lambda b, me: (0, 3))


def by_core(me, pairs):
    odd = me % 2 == 1
    first, second = pairs[:, 0], pairs[:, 1]
    return jnp.where(odd, second, first), jnp.where(odd, first, second)


def causal_bias(step=LANES):
    rows = LANES + step * (BLOCK // LANES - 1)
    key = lax.broadcasted_iota(jnp.int32, (rows, BLOCK), 0)
    query = lax.broadcasted_iota(jnp.int32, (rows, BLOCK), 1)
    query = query + (query // LANES) * (step - LANES)
    return jnp.where(key <= query, 0.0, -BIG).astype(f32)


def key_features(segment_row, length):
    row = lax.broadcasted_iota(jnp.int32, (LANES, length), 0)
    marks = (row == segment_row) | ((row >= 7) & (row < 10))
    return jnp.where(marks, 1.0, 0.0).astype(f32).T.astype(bf16)


def query_features(segment_row, length):
    row = lax.broadcasted_iota(jnp.int32, (16, length), 0)
    return jnp.where((row < 7) & (row != segment_row), -BIG, 0.0).astype(f32)


def padded_head(head, features, odd):
    blank = jnp.zeros_like(head)
    rest = jnp.zeros((LANES - 16, head.shape[1]), bf16)
    both = [blank, head] if odd else [head, blank]
    return jnp.concatenate(both + [features, rest], axis=0)


def attend_queries(part, parts, slots, me, seg_ref, q_t, k_ref, v_t, att_refs, ot_ref, lse_ref, aux):
    k_aux, q_aux, causal = aux
    length = k_ref.shape[1]
    piece = length // slots
    some = piece // parts
    step = piece if parts > 1 else LANES
    segment_row = seg_ref[0]
    q_aux[...] = query_features(segment_row, length)
    k_aux[...] = key_features(segment_row, length)
    blocks = slots * some // BLOCK
    count = BLOCK // some if parts > 1 else 1

    def head_pair(pair, carry):
        base = pl.multiple_of(pair * LANES, LANES)
        for odd in range(2):
            rows = pl.ds(pl.multiple_of(pair * LANES + odd * 64, 64), 64)
            for block in range(blocks):
                if parts > 1:
                    first = block * count * piece + part * some
                    places = [pl.ds(first + i * piece, some) for i in range(count)]
                else:
                    first = block * BLOCK
                    places = [pl.ds(first, BLOCK)]
                feats = jnp.concatenate([q_aux[:, p] for p in places], axis=1).astype(bf16)
                head = jnp.concatenate([q_t[0, rows, p] for p in places], axis=1)
                query = padded_head(head, feats, odd)
                chunks = [(k, min(BLOCK, first - k)) for k in range(0, first, BLOCK)]
                chunks.append((first, causal.shape[0]))
                scores = []
                for start, size in chunks:
                    keys = pl.ds(start, size)
                    key = jnp.concatenate([k_ref[0, keys, pl.ds(base, LANES)], k_aux[keys]], axis=1)
                    score = dot(key, query)
                    scores.append(score + causal[...] if start == first else score)
                top = functools.reduce(
                    jnp.maximum, [jnp.max(score, axis=0, keepdims=True) for score in scores]
                )
                total = jnp.zeros((1, BLOCK), f32)
                out = jnp.zeros((64, BLOCK), f32)
                for (start, size), score in zip(chunks, scores):
                    prob = jnp.exp2(score - top)
                    total = total + jnp.sum(prob, axis=0, keepdims=True)
                    out = out + dot(v_t[0, rows, pl.ds(start, size)], prob.astype(bf16))
                held = pl.ds(block * BLOCK, BLOCK)
                ot_ref[0, rows, held] = (out / total).astype(bf16)
                lse_ref[0, pl.ds(pair * 2 + odd, 1), held] = top + jnp.log2(total)
        return carry

    lax.fori_loop(0, HEADS // 2, head_pair, 0)
    for j in range(slots):
        place = pl.ds(pl.multiple_of((me ^ j) * some, some), some)
        att_refs[j][0] = ot_ref[0, :, place].T


def attend_first_kernel(parts, slots, old, *refs):
    me_ref = refs[0]
    x_refs = refs[1 : 1 + slots]
    vector_ref, w_ref = refs[1 + slots : 3 + slots]
    rest = refs[3 + slots + old :]
    att_refs = rest[:slots]
    seg_ref, qt_ref, k_ref, v_ref, q_ref, vt_ref, ot_ref, lse_ref = rest[slots : slots + 8]
    w_t, *aux = rest[slots + 8 :]
    width = w_ref.shape[0]
    piece = x_refs[0].shape[1] - MARKS
    me = me_ref[0]
    score_scale = LOG2E / math.sqrt(width // HEADS)

    w_t[:width] = w_ref[:, :width].T
    w_t[width:] = w_ref[:, 2 * width :].T
    aux[2][...] = causal_bias(piece if parts > 1 else LANES)
    gain = vector_ref[...].astype(f32).T[0:1]
    for j in range(slots):
        place = pl.ds(pl.multiple_of((me ^ j) * piece, piece), piece)
        marks = x_refs[j][0, piece:].astype(f32)
        seg_ref[0, :, place] = marks[0:1, :piece].astype(jnp.int32)
        normed, _ = normalize(x_refs[j][0, :piece].astype(f32))
        first_in = (normed * gain).astype(bf16)
        projected = dot(first_in, w_ref[...])
        q_ref[0, place] = (projected[:, :width] * score_scale).astype(bf16)
        k_ref[0, place] = projected[:, width : 2 * width].astype(bf16)
        v_ref[0, place] = projected[:, 2 * width :].astype(bf16)
        turned = dot(w_t[...], first_in, NT)
        qt_ref[0, :, place] = (turned[:width] * score_scale).astype(bf16)
        vt_ref[0, :, place] = turned[width:].astype(bf16)
    attend_queries(
        0, parts, slots, me, seg_ref, qt_ref, k_ref, vt_ref, att_refs, ot_ref, lse_ref, aux
    )


def attend_next_kernel(part, parts, slots, *refs):
    me_ref, seg_ref, qt_ref, k_ref, vt_ref = refs[:5]
    att_refs = refs[5 : 5 + slots]
    ot_ref, lse_ref, *aux = refs[5 + slots :]

    @pl.when(pl.program_id(0) == 0)
    def _():
        aux[2][...] = causal_bias(k_ref.shape[1] // slots if parts > 1 else LANES)

    attend_queries(
        part, parts, slots, me_ref[0], seg_ref, qt_ref, k_ref, vt_ref, att_refs, ot_ref, lse_ref, aux
    )


def attend_outs(rows, slots, some, width):
    return [(per_row(some, width), (rows, some, width), bf16)] * slots, [
        (per_row(width, slots * some), (rows, width, slots * some), bf16),
        (per_row(HEADS, slots * some), (rows, HEADS, slots * some), f32),
    ]


def attend_scratch(length, piece, parts):
    span = LANES + (piece if parts > 1 else LANES) * (BLOCK // LANES - 1)
    return [((length, LANES), bf16), ((16, length), f32), ((span, BLOCK), f32)]


def attend_first(me, row, rows, x_slots, weights, parts, old):
    slots = len(x_slots)
    _, packed, width = x_slots[0].shape
    piece = packed - MARKS
    length = piece * slots

    def this(*shape):
        return pl.BlockSpec((1,) + shape, lambda r, me: (row,) + (0,) * len(shape))

    some = piece // parts
    turned = (this(width, length), (rows, width, length), bf16)
    plain = (this(length, width), (rows, length, width), bf16)
    outs = (
        [(this(some, width), (rows, some, width), bf16)] * slots
        + [(this(1, length), (rows, 1, length), jnp.int32)]
        + [turned, plain, plain, plain, turned]
        + [
            (this(width, slots * some), (rows, width, slots * some), bf16),
            (this(HEADS, slots * some), (rows, HEADS, slots * some), f32),
        ]
    )
    result = call(
        functools.partial(attend_first_kernel, parts, slots, len(old)),
        "attend_first",
        (1,),
        [per_row(packed, width)] * slots
        + [
            pl.BlockSpec((width, LANES), lambda r, me: (0, 4 * width // LANES)),
            whole(width, 3 * width),
        ]
        + [pl.BlockSpec(memory_space=pl.ANY)] * len(old),
        outs,
        [((2 * width, width), bf16)] + attend_scratch(length, piece, parts),
        (me, *x_slots, weights, weights, *old),
        12,
        {3 + slots + i: i for i in range(len(old))},
        room=26,
    )
    return result


def attend_next(me, part, parts, projected, slots):
    segment_rows, q_t, k, _, _, v_t = projected
    rows, length, width = k.shape
    piece = length // slots
    att, more = attend_outs(rows, slots, piece // parts, width)
    result = call(
        functools.partial(attend_next_kernel, part, parts, slots),
        "attend_next",
        (rows,),
        [
            per_row(1, length),
            per_row(width, length),
            per_row(length, width),
            per_row(width, length),
        ],
        att + more,
        attend_scratch(length, piece, parts),
        (me, segment_rows, q_t, k, v_t),
        28 / parts,
        room=16,
    )
    return result[:slots], result[slots:]


def attend_back_kernel(row, last, parts, slot_count, *refs):
    me_ref = refs[0]
    x_refs = refs[1 : 1 + slot_count]
    rest = refs[1 + slot_count :]
    do_refs, rest = rest[: parts * slot_count], rest[parts * slot_count :]
    seg_ref, gain_ref, w_ref, qt_ref, k_ref, v_ref, q_ref = rest[:7]
    ot_refs, lse_refs = rest[7 : 7 + parts], rest[7 + parts : 7 + 2 * parts]
    rest = rest[7 + 2 * parts :]
    if row:
        before_ref, rest = rest[0], rest[1:]
    gf_refs, rest = rest[:slot_count], rest[slot_count:]
    dw_refs, rest = rest[: 1 + last], rest[1 + last :]
    (
        k_aux, q_aux, v_aux, causal, do, first_t, work_t, k_t, grads, prob, grad_score, delta, lse
    ) = rest
    width = w_ref.shape[0]
    piece = x_refs[0].shape[1] - MARKS
    some = piece // parts
    length = piece * slot_count
    me = me_ref[0]
    score_scale = 1.0 / math.sqrt(width // HEADS)
    causal[...] = causal_bias()
    lane = lax.broadcasted_iota(jnp.int32, (length, LANES), 1)
    v_aux[...] = jnp.where(lane < 3, 1.0, 0.0).astype(bf16)
    for part in range(parts):
        for i in range(slot_count):
            held = pl.ds(i * some, some)
            lse[:, pl.ds(i * piece + part * some, some)] = lse_refs[part][0, :, held]

    segment_row = seg_ref[0]
    q_aux[...] = query_features(segment_row, length)
    k_aux[...] = key_features(segment_row, length)
    gain = gain_ref[...]
    for j in range(slot_count):
        place = pl.ds(pl.multiple_of((me ^ j) * piece, piece), piece)
        normed, _ = normalize(x_refs[j][0, :piece].astype(f32))
        first_t[:, place] = (normed * gain).astype(bf16).T
        k_t[:, place] = k_ref[0, place].T
        for part in range(parts):
            start = (me ^ j) * piece + part * some
            place = pl.ds(pl.multiple_of(start, some), some)
            held = pl.ds(pl.multiple_of((me ^ j) * some, some), some)
            grad = do_refs[part * slot_count + j][0]
            do[place] = grad
            turned = grad.T
            work_t[:, place] = turned
            product = turned.astype(f32) * ot_refs[part][0, :, held].astype(f32)
            delta[:, place] = jnp.sum(product.reshape(HEADS, width // HEADS, some), axis=1)
    lane = lax.broadcasted_iota(jnp.int32, (1, LANES), 1)
    feature = lax.broadcasted_iota(jnp.int32, (16, BLOCK), 0)
    blocks = length // BLOCK

    def head_pair(pair, carry):
        base = pl.multiple_of(pair * LANES, LANES)
        for odd in range(2):
            rows = pl.ds(pl.multiple_of(pair * LANES + odd * 64, 64), 64)
            head = pl.ds(pair * 2 + odd, 1)
            for qb in range(blocks):
                queries = pl.ds(qb * BLOCK, BLOCK)
                a, b, c = split3(lse[head, queries])
                feats = jnp.where(feature == 7, -a, q_aux[:, queries])
                feats = jnp.where(feature == 8, -b, jnp.where(feature == 9, -c, feats))
                query = padded_head(qt_ref[0, rows, queries], feats.astype(bf16), odd)
                a, b, c = split3(delta[head, queries])
                feats = jnp.where(feature == 0, -a, jnp.where(feature == 1, -b, 0.0))
                feats = jnp.where(feature == 2, -c, feats)
                grad = padded_head(work_t[rows, queries], feats.astype(bf16), odd)
                held = pl.ds(odd * length + qb * BLOCK, BLOCK)
                for kb in range(qb + 1):
                    keys = pl.ds(kb * BLOCK, BLOCK)
                    key = jnp.concatenate([k_ref[0, keys, pl.ds(base, LANES)], k_aux[keys]], axis=1)
                    score = dot(key, query)
                    if kb == qb:
                        score = score + causal[...]
                    value = jnp.concatenate(
                        [v_ref[0, keys, pl.ds(base, LANES)], v_aux[keys]], axis=1
                    )
                    grad_prob = dot(value, grad)
                    weight = jnp.exp2(score)
                    prob[keys, held] = weight.astype(bf16)
                    grad_score[keys, held] = (weight * grad_prob).astype(bf16)
                end = (qb + 1) * BLOCK
                grad_q = dot(k_t[rows, 0:end], grad_score[0:end, held])
                work_t[rows, queries] = (grad_q * score_scale).astype(bf16)
        for kb in range(blocks):
            keys = pl.ds(kb * BLOCK, BLOCK)
            later = pl.ds(kb * BLOCK, length - kb * BLOCK)
            grad_v = jnp.zeros((BLOCK, LANES), f32)
            grad_k = jnp.zeros((BLOCK, LANES), f32)
            for odd in range(2):
                mine = (lane >= 64) if odd else (lane < 64)
                held = pl.ds(odd * length + kb * BLOCK, length - kb * BLOCK)
                zero = jnp.zeros((), bf16)
                grad = jnp.where(mine, do[later, pl.ds(base, LANES)], zero)
                query = jnp.where(mine, q_ref[0, later, pl.ds(base, LANES)], zero)
                grad_v = grad_v + dot(prob[keys, held], grad)
                grad_k = grad_k + dot(grad_score[keys, held], query)
            grads[keys, pl.ds(pl.multiple_of(width + pair * LANES, LANES), LANES)] = (
                grad_k * LN2
            ).astype(bf16)
            grads[keys, pl.ds(pl.multiple_of(2 * width + pair * LANES, LANES), LANES)] = (
                grad_v.astype(bf16)
            )
        return carry

    lax.fori_loop(0, HEADS // 2, head_pair, 0)
    for j in range(slot_count):
        place = pl.ds(pl.multiple_of((me ^ j) * piece, piece), piece)
        grads[place, :width] = work_t[:, place].T
        gf_refs[j][0] = dot(grads[place], w_ref[...], NT).astype(bf16)
    update = dot(first_t[...], grads[...])
    if row:
        update = before_ref[...] + update
    if last:
        keep, send = by_core(me, update.reshape(-1, 2, *dw_refs[0].shape[1:]))
        dw_refs[0][...] = keep
        dw_refs[1][...] = send.astype(bf16)
    else:
        dw_refs[0][...] = update


def attend_back(me, row, rows, shards, x_slots, do_parts, gain, w_qkv, projected, kept, before):
    slot_count, parts = len(x_slots), len(do_parts)
    _, packed, width = x_slots[0].shape
    piece = packed - MARKS
    length = piece * slot_count
    some = piece // parts
    last = row == rows - 1

    def this(*shape):
        return pl.BlockSpec((1,) + shape, lambda r, me: (row,) + (0,) * len(shape))

    half = (shards // 2, width // shards, 3 * width)
    outs = [(per_row(piece, width), (1, piece, width), bf16)] * slot_count
    if last:
        outs += [(whole(*half), half, f32), (whole(*half), half, bf16)]
    else:
        outs += [(whole(width, 3 * width), (width, 3 * width), f32)]
    segment_rows, q_t, k, v, q, _ = projected
    result = call(
        functools.partial(attend_back_kernel, row, last, parts, slot_count),
        "attend_back",
        (1,),
        [per_row(packed, width)] * slot_count
        + [this(some, width)] * (parts * slot_count)
        + [this(1, length), whole(1, width), whole(width, 3 * width)]
        + [this(width, length)]
        + [this(length, width)] * 3
        + [this(width, some * slot_count)] * parts
        + [this(HEADS, some * slot_count)] * parts
        + ([whole(width, 3 * width)] if row else []),
        outs,
        [
            ((length, LANES), bf16),
            ((16, length), f32),
            ((length, LANES), bf16),
            ((BLOCK, BLOCK), f32),
            ((length, width), bf16),
            ((width, length), bf16),
            ((width, length), bf16),
            ((width, length), bf16),
            ((length, 3 * width), bf16),
            ((length, 2 * length), bf16),
            ((length, 2 * length), bf16),
            ((HEADS, length), f32),
            ((HEADS, length), f32),
        ],
        (
            me,
            *x_slots,
            *[do for part in do_parts for do in part],
            segment_rows,
            gain,
            w_qkv,
            q_t,
            k,
            v,
            q,
            *[o for o, _ in kept],
            *[l for _, l in kept],
            *([before] if row else []),
        ),
        28,
        room=60,
    )
    return result[:slot_count], result[slot_count:]


def tokens_of(refs, span):
    return jnp.concatenate([ref[:, span] for ref in refs], axis=0).reshape(-1, refs[0].shape[-1])


def rows_of(ref, me, rows, slot_count, span):
    parts = [ref[pl.ds((me ^ j) * rows, rows), span] for j in range(slot_count)]
    return jnp.concatenate(parts, axis=0).reshape(-1, ref.shape[-1])


def diagonal(piece):
    place = lax.broadcasted_iota(jnp.int32, (piece, LANES), 0)
    lane = lax.broadcasted_iota(jnp.int32, (piece, LANES), 1)
    return place == lane % piece, lane // piece, lane


def mix_kernel(slot_count, experts, piece, *refs):
    me_ref = refs[0]
    att_refs = refs[1 : 1 + slot_count]
    inputs_ref, cot_ref, w_out_ref, gain_ref, control_ref = refs[1 + slot_count : 6 + slot_count]
    pay_refs = refs[6 + slot_count :]
    rows, positions, width = att_refs[0].shape
    tokens = rows * slot_count
    me = me_ref[0]
    own, _, lane = diagonal(piece)
    w_out = w_out_ref[...]
    for sub in range(positions // piece):
        span = slice(sub * piece, (sub + 1) * piece)
        added = dot(tokens_of(att_refs, span), w_out)
        second = []
        for token in range(tokens):
            row = (me ^ (token // rows)) * rows + token % rows
            middle = inputs_ref[row, span].astype(f32) + added[token * piece : (token + 1) * piece]
            normed, _ = normalize(middle)
            second.append((normed * gain_ref[...]).astype(bf16))
        second = jnp.concatenate(second, axis=0)
        grad = rows_of(cot_ref, me, rows, slot_count, span)
        logits = dot(second, control_ref[...], NT).reshape(tokens, piece, LANES)
        top = jnp.max(logits, axis=0)
        weights = jnp.exp(logits - top)
        total = jnp.sum(weights, axis=0)
        log_total = top + jnp.log(total)
        weights = jnp.where(own, weights * (1.0 / total), 0.0)
        spread_out = weights.reshape(-1, LANES).astype(bf16)
        mixed = dot(spread_out, second, TN).astype(bf16)
        grad_results = dot(spread_out, grad, TN).astype(bf16)
        a, b, c = split3(log_total)
        for e in range(experts):
            mine = slice(e * piece, (e + 1) * piece)
            first = slice(e * piece, e * piece + 1)
            stats = jnp.where(lane == 0, a[:, first], jnp.where(lane == 1, b[:, first], c[:, first]))
            pay_refs[e][span, :width] = mixed[mine]
            pay_refs[e][span, width : 2 * width] = grad_results[mine]
            pay_refs[e][span, 2 * width :] = stats.astype(bf16)


def mix(me, part, att_slots, inputs, cotangent, w_out, gain, control, experts):
    slot_count = len(att_slots)
    rows, positions, width = att_slots[0].shape
    tokens = rows * slot_count
    half = pl.BlockSpec((tokens, positions, width), lambda b, me: (0, part, 0))
    pay = (None, (positions, 2 * width + LANES), bf16)
    return call(
        functools.partial(mix_kernel, slot_count, experts, LANES // experts),
        "mix",
        (1,),
        [None] * slot_count + [half, half, fourth(width), None, None],
        [pay] * experts,
        [],
        (me, *att_slots, inputs, cotangent, w_out, gain, control),
        positions * 8 / 256,
    )


def expert_kernel(part, parts, tiled, slot_count, *refs):
    me_ref = refs[0]
    pay_refs = refs[1 : 1 + slot_count]
    rest = refs[1 + slot_count :]
    count = 4 if tiled else 2
    weight_refs, rest = rest[:count], rest[count:]
    expand_ref = weight_refs[0]
    last = part == parts - 1
    earlier, rest = rest[: 4 * part], rest[4 * part :]
    if last:
        back_ref, keep_ref, send_ref = rest[:3]
        mixed_acc, grad_acc, result_acc, back_acc, stat, *more, mixed_low, grad_low = rest[3:]
    else:
        back_ref, mixed_low, grad_low, hidden_ref, pre_ref = rest[:5]
        mixed_acc, grad_acc, result_acc, back_acc, stat, *more = rest[5:]
    me = me_ref[0]
    width = expand_ref.shape[-1]
    step = pl.program_id(0)

    @pl.when(step == 0)
    def _():
        logs = []
        for j in range(slot_count):
            stats = pay_refs[j][:, 2 * width :].astype(f32)
            logs.append(stats[:, 0:1] + stats[:, 1:2] + stats[:, 2:3])
        top = functools.reduce(jnp.maximum, logs)
        total = functools.reduce(jnp.add, [jnp.exp(log - top) for log in logs])
        log_total = top + jnp.log(total)
        mixed, grad = 0.0, 0.0
        for j in range(slot_count):
            share = jnp.exp(logs[j] - log_total)
            mixed = mixed + share * pay_refs[j][:, :width].astype(f32)
            grad = grad + share * pay_refs[j][:, width : 2 * width].astype(f32)
        mixed_acc[...] = mixed
        grad_acc[...] = grad
        mixed_low[...] = mixed.astype(bf16)
        grad_low[...] = grad.astype(bf16)
        result_acc[...] = jnp.zeros_like(result_acc)
        back_acc[...] = jnp.zeros_like(back_acc)
        stat[...] = jnp.broadcast_to(log_total, stat.shape)

    mixed, grad = mixed_low[...], grad_low[...]
    if tiled:
        for i in range(2):
            own, other = weight_refs[2 * i][...], weight_refs[2 * i + 1][...]
            odd = me % 2 == 1
            more[i][:, 0] = jnp.where(odd, other, own)
            more[i][:, 1] = jnp.where(odd, own, other)
        expand, shrink = [ref[...].reshape(-1, width) for ref in more]
    else:
        expand, shrink = [ref[...].reshape(-1, width) for ref in weight_refs]
    value = dot(mixed, expand)
    coeff = math.sqrt(2.0 / math.pi)
    square = value * value
    turn = jnp.tanh(coeff * (value + 0.044715 * (square * value)))
    half = 0.5 * (1.0 + turn)
    hidden = (value * half).astype(bf16)
    slope = half + (0.5 * coeff) * value * (1.0 - turn * turn) * (1.0 + (3 * 0.044715) * square)
    result_acc[...] += dot(hidden, shrink)
    grad_pre = (dot(grad, shrink, NT) * slope).astype(bf16)
    back_acc[...] += dot(grad_pre, expand, NT)
    if last:
        sets = [earlier[4 * i : 4 * i + 4] for i in range(part)]
        mixed = jnp.concatenate([m[...] for m, _, _, _ in sets] + [mixed], axis=0)
        grad = jnp.concatenate([g[...] for _, g, _, _ in sets] + [grad], axis=0)
        hidden = jnp.concatenate([h[...] for _, _, h, _ in sets] + [hidden], axis=0)
        grad_pre = jnp.concatenate([p[...] for _, _, _, p in sets] + [grad_pre], axis=0)
        grad_expand = dot(mixed, grad_pre, TN).astype(bf16)
        grad_shrink = dot(hidden, grad, TN).astype(bf16)
        if tiled:
            shards = 2 * keep_ref.shape[0]
            lines = width // shards
            both = keep_ref.shape[1]
            keep, send = by_core(me, grad_expand.reshape(shards // 2, 2, lines, width))
            place = pl.ds(pl.multiple_of(step * lines, lines), lines)
            keep_ref[:, place] = keep
            send_ref[:, place] = send
            count = 2 * width // both // 2
            keep, send = by_core(me, grad_shrink.reshape(count, 2, both // 2, width))
            place = pl.ds(step * count, count)
            keep_ref[place, both // 2 :] = keep
            send_ref[place, both // 2 :] = send
        else:
            keep_ref[...] = grad_expand.reshape(keep_ref.shape)
            send_ref[...] = grad_shrink.reshape(send_ref.shape)
    else:
        hidden_ref[...] = hidden
        pre_ref[...] = grad_pre

    @pl.when(step == pl.num_programs(0) - 1)
    def _():
        results = result_acc[...].astype(bf16)
        back = back_acc[...].astype(bf16)
        back_ref[:, :width] = results
        back_ref[:, width : 2 * width] = back
        inner = jnp.sum(
            results.astype(f32) * grad_acc[...] + back.astype(f32) * mixed_acc[...],
            axis=-1,
            keepdims=True,
        )
        lane = lax.broadcasted_iota(jnp.int32, stat.shape, 1)
        a, b, c = split3(stat[...])
        d, e, f = split3(inner)
        stats = jnp.where(lane == 0, a, jnp.where(lane == 1, b, c))
        stats = jnp.where(lane < 3, stats, jnp.where(lane == 3, d, jnp.where(lane == 4, e, f)))
        back_ref[:, 2 * width :] = stats.astype(bf16)


def pack_expert(expand, shrink):
    experts, lines, hidden = expand.shape
    width = shrink.shape[-1]
    expand = expand.reshape(experts, lines, hidden // width, width)
    expand = jnp.swapaxes(expand, 1, 2).reshape(experts, -1, width)
    return jnp.concatenate([expand, shrink], axis=1)


def unpack_expert(packed, lines):
    experts, both, width = packed.shape
    expand = packed[:, : both // 2].reshape(experts, -1, lines, width)
    expand = jnp.swapaxes(expand, 1, 2).reshape(experts, lines, -1)
    return expand, packed[:, both // 2 :]


def expert(me, core, part, parts, pay_slots, halves, earlier):
    slot_count = len(pay_slots)
    groups, packed = pay_slots[0].shape
    shards = 2 * halves[0][0].shape[0]
    tail, width = halves[0][0].shape[1:]
    hidden = shards * tail
    chunks = hidden // width
    lines = width // shards
    acc = ((groups, width), f32)
    low = ((groups, width), bf16)
    tiled = lines % 16 == 0
    group = shards // chunks // 2
    if tiled:
        columns = pl.BlockSpec((shards // 2, lines, width), lambda f, me: (0, f, 0))
        lower = pl.BlockSpec((group, tail, width), lambda f, me: (f, 0, 0))
        weights = [*halves[0], *halves[1]]
        specs = [columns, columns, lower, lower]
        built = [((shards // 2, 2, lines, width), bf16), ((group, 2, tail, width), bf16)]
        both = (shards // 2, 2 * tail, width)
        grads = [(whole(*both), both, bf16)] * 2
    else:
        odd = core == 1
        weights = [
            jnp.stack([jnp.where(odd, b, a), jnp.where(odd, a, b)], axis=1) for a, b in halves
        ]
        expand = weights[0].reshape(shards, chunks, lines, width)
        expand = jnp.swapaxes(expand, 0, 1).reshape(chunks, width, width)
        weights = [expand, weights[1].reshape(chunks, width, width)]
        specs = [pl.BlockSpec((1, width, width), lambda f, me: (f, 0, 0))] * 2
        built = []
        grads = [(specs[0], (chunks, width, width), bf16)] * 2
    token = whole(groups, width)
    inner = pl.BlockSpec((groups, width), lambda f, me: (0, f))
    last = part == parts - 1
    outs = [(whole(groups, packed), (groups, packed), bf16)]
    scratch = [acc, acc, acc, acc, ((groups, LANES), f32)] + built
    if last:
        outs += grads
        scratch += [low, low]
    else:
        outs += [(token, (groups, width), bf16)] * 2 + [(inner, (groups, hidden), bf16)] * 2
    result = call(
        functools.partial(expert_kernel, part, parts, tiled, slot_count),
        "expert",
        (chunks,),
        [whole(groups, packed)] * slot_count + specs + [token, token, inner, inner] * part,
        outs,
        scratch,
        (me, *pay_slots, *weights, *earlier),
        7,
        room=18,
    )
    more = list(result[1:])
    if last and not tiled:
        grad = jnp.swapaxes(more[0].reshape(chunks, shards, lines, width), 0, 1)
        more = [grad.reshape(shards, tail, width), more[1].reshape(shards, tail, width)]
        more = jnp.concatenate(more, axis=1).reshape(shards // 2, 2, 2 * tail, width)
        odd = core == 1
        more = [
            jnp.where(odd, more[:, 1], more[:, 0]),
            jnp.where(odd, more[:, 0], more[:, 1]),
        ]
    return result[0], more


def unmix_kernel(slot_count, experts, piece, part, last, *refs):
    me_ref = refs[0]
    ret_refs = refs[1 : 1 + experts]
    att_refs = refs[1 + experts : 1 + experts + slot_count]
    rest = refs[1 + experts + slot_count :]
    inputs_ref, cot_ref, w_out_ref, gain_ref, control_ref = rest[:5]
    rest = rest[5:]
    if part:
        old_out_ref, old_control_ref, old_gain_ref = rest[1:4]
        rest = rest[4:]
    out_ref, grad_middle_ref = rest[:2]
    back_refs = rest[2 : 2 + slot_count]
    rest = rest[2 + slot_count :]
    if last:
        keep_ref, send_ref, middle_scratch, small = rest
    else:
        grad_out_ref, grad_control_ref, grad_gain_ref, middle_scratch = rest
    rows, positions, width = att_refs[0].shape
    tokens = rows * slot_count
    me = me_ref[0]

    own, group, _ = diagonal(piece)
    control = control_ref[...]
    w_out = w_out_ref[...]
    grad_out, grad_control, grad_gain = 0.0, 0.0, 0.0
    if part:
        grad_out, grad_control = old_out_ref[...], old_control_ref[...]
        grad_gain = old_gain_ref[...]
    for sub in range(positions // piece):
        span = slice(sub * piece, (sub + 1) * piece)
        attended = tokens_of(att_refs, span)
        added = dot(attended, w_out)
        second = []
        for token in range(tokens):
            row = (me ^ (token // rows)) * rows + token % rows
            middle = inputs_ref[row, span].astype(f32) + added[token * piece : (token + 1) * piece]
            middle_scratch[token] = middle
            normed, _ = normalize(middle)
            second.append((normed * gain_ref[...]).astype(bf16))
        second = jnp.concatenate(second, axis=0)
        cot = rows_of(cot_ref, me, rows, slot_count, span)
        log_total = jnp.zeros((piece, LANES), f32)
        inner = jnp.zeros((piece, LANES), f32)
        for e in range(experts):
            stats = ret_refs[e][span, 2 * width :].astype(f32)
            mine = group == e
            log_total = jnp.where(mine, stats[:, 0:1] + stats[:, 1:2] + stats[:, 2:3], log_total)
            inner = jnp.where(mine, stats[:, 3:4] + stats[:, 4:5] + stats[:, 5:6], inner)
        results = jnp.concatenate([ref[span, :width] for ref in ret_refs], axis=0)
        back = jnp.concatenate([ref[span, width : 2 * width] for ref in ret_refs], axis=0)
        logits = dot(second, control, NT).reshape(tokens, piece, LANES)
        weights = jnp.where(own, jnp.exp(logits - log_total), 0.0)
        low = weights.reshape(-1, LANES).astype(bf16)
        spread = dot(low, results)
        grad_weights = (dot(cot, results, NT) + dot(second, back, NT)).reshape(tokens, piece, LANES)
        grad_logits = (weights * (grad_weights - inner)).reshape(-1, LANES).astype(bf16)
        grad_second = dot(low, back) + dot(grad_logits, control)
        grad_control = grad_control + dot(grad_logits, second, TN)
        grad_middles = []
        for token in range(tokens):
            row = (me ^ (token // rows)) * rows + token % rows
            mine = slice(token * piece, (token + 1) * piece)
            middle = middle_scratch[token]
            out_ref[row, span] = (middle + spread[mine].astype(bf16).astype(f32)).astype(bf16)
            grad = grad_second[mine].astype(bf16).astype(f32)
            normed, scaled = normalize(middle)
            grad_gain = grad_gain + jnp.sum((grad * normed).reshape(-1, 8, width), axis=0)
            grad_middle = norm_back(grad * gain_ref[...], normed, scaled)
            grad_middle = (cot_ref[row, span].astype(f32) + grad_middle).astype(bf16)
            grad_middle_ref[token, span] = grad_middle
            grad_middles.append(grad_middle)
        grad_middle = jnp.concatenate(grad_middles, axis=0)
        grad_attended = dot(grad_middle, w_out, NT).astype(bf16)
        grad_attended = grad_attended.reshape(tokens, piece, width)
        for j in range(slot_count):
            back_refs[j][:, span] = grad_attended[j * rows : (j + 1) * rows]
        grad_out = grad_out + dot(attended, grad_middle, TN)
    if last:
        small[...] = jnp.zeros_like(small)
        small[0:1] = jnp.sum(grad_gain, axis=0, keepdims=True)
        for e in range(experts):
            total = grad_control[e * piece : (e + 1) * piece]
            small[pl.ds(1 + (me_ref[1] ^ e), 1)] = jnp.sum(total, axis=0, keepdims=True)
        blocks, lines = keep_ref.shape[:2]
        for columns, value in (
            (slice(0, width), grad_out),
            (slice(width, width + LANES), small[...].T),
        ):
            keep, send = by_core(me, value.reshape(blocks, 2, lines, -1))
            keep_ref[:, :, columns] = keep
            send_ref[:, :, columns] = send.astype(bf16)
    else:
        grad_control_ref[...] = grad_control
        grad_gain_ref[...] = grad_gain
        grad_out_ref[...] = grad_out


def unmix(
    me, part, last, shards, ret_slots, att_slots, inputs, cotangent, w_out, gain, control, before
):
    slot_count, experts = len(att_slots), len(ret_slots)
    rows, positions, width = att_slots[0].shape
    tokens = rows * slot_count
    half = pl.BlockSpec((tokens, positions, width), lambda b, me: (0, part, 0))
    count = 1 + experts + slot_count + 5
    if last:
        kept = (shards // 2, width // shards, width + LANES)
        made = [(None, kept, f32), (None, kept, bf16)]
    else:
        made = [
            (None, (width, width), f32),
            (None, (LANES, width), f32),
            (None, (8, width), f32),
        ]
    result = call(
        functools.partial(unmix_kernel, slot_count, experts, LANES // experts, part, last),
        "unmix",
        (1,),
        [None] * (experts + slot_count)
        + [half, half, fourth(width), None, None]
        + ([pl.BlockSpec(memory_space=pl.ANY)] + [None] * 3 if part else []),
        [(half, cotangent.shape, bf16), (None, (tokens, positions, width), bf16)]
        + [(None, (rows, positions, width), bf16)] * slot_count
        + made,
        [((tokens, LANES // experts, width), f32)] + ([((LANES, width), f32)] if last else []),
        (me, *ret_slots, *att_slots, inputs, cotangent, w_out, gain, control, *before),
        positions * 12 / 256,
        {count: 0} if part else None,
        room=10 if part else 58,
    )
    do_slots = result[2 : 2 + slot_count]
    return do_slots, result[1], [result[0], *result[2 + slot_count :]]


def finish_kernel(slot_count, row_count, parts, *refs):
    me_ref = refs[0]
    gf_refs = refs[1 : 1 + slot_count * row_count]
    rest = refs[1 + slot_count * row_count :]
    inputs_ref, grad_middle_refs, (gain_ref, out_ref) = rest[0], rest[1 : 1 + parts], rest[1 + parts :]
    me = me_ref[0]
    piece = 64
    positions = out_ref.shape[1]
    some = positions // parts
    for start in range(0, positions, piece):
        span = slice(start, start + piece)
        inner = slice(start % some, start % some + piece)
        for j in range(slot_count):
            for row in range(row_count):
                place = (me ^ j) * row_count + row
                normed, scaled = normalize(inputs_ref[place, span].astype(f32))
                incoming = gf_refs[row * slot_count + j][0, span].astype(f32) * gain_ref[...]
                grad = norm_back(incoming, normed, scaled)
                middle = grad_middle_refs[start // some][j * row_count + row, inner]
                out_ref[place, span] = (grad + middle.astype(f32)).astype(bf16)


def finish(me, gf_rows, inputs, grad_middles, gain):
    slot_count, row_count, parts = len(gf_rows[0]), len(gf_rows), len(grad_middles)
    return call(
        functools.partial(finish_kernel, slot_count, row_count, parts),
        "finish",
        (1,),
        [None] * (slot_count * row_count + 2 + parts),
        [(None, inputs.shape, bf16)],
        [],
        (me, *[gf for row in gf_rows for gf in row], inputs, *grad_middles, gain),
        4,
    )[0]


def on_device(
    sizes,
    inputs,
    segments,
    cotangent,
    gain_attn,
    w_qkv,
    w_out,
    gain_mix,
    w_control,
    w_expand,
    w_shrink,
):
    groups, members, slots = sizes
    local_rows, positions, width = inputs.shape
    experts = w_expand.shape[0]
    rows = local_rows // slots
    place = (("gq", groups), ("gi", members), ("seq", slots))
    owners = (("gq", groups), ("seq", slots))
    seq_me = lax.axis_index("seq")
    member = lax.axis_index("gi")
    me = jnp.stack([seq_me, member]).astype(jnp.int32)

    parts = 2 if positions % BLOCK == 0 else 1

    marks = segments.astype(bf16)[:, None, :]
    marks = jnp.pad(marks, ((0, 0), (0, MARKS - 1), (0, width - positions)))

    def row_part(row, j):
        index = (seq_me ^ j) * rows + row
        parts = [lax.dynamic_slice_in_dim(array, index, 1, axis=0) for array in (inputs, marks)]
        return jnp.concatenate(parts, axis=1)

    x_parts = [[row_part(row, j) for j in range(slots)] for row in range(rows)]
    x_rows = [[x_parts[0][0]]]

    def send_some(slots_of, done, first, last):
        for j in range(first, last):
            done.append(partner(slots_of[j], "seq", slots, j))

    small = jnp.concatenate([gain_attn[None], gain_mix[None], w_control], axis=0)
    small = jnp.pad(jnp.transpose(small), ((0, 0), (0, LANES - 2 - experts)))
    packed = jnp.concatenate([w_qkv, w_out, small], axis=1).astype(bf16)
    packed = Doubling(packed, place, ("seq", "gq", "core"))
    send_some(x_parts[0], x_rows[0], 1, slots // 2 + 1)
    packed.steps("seq")
    x_rows, x_parts, w_expand, w_shrink = together((x_rows, x_parts, w_expand, w_shrink), packed)

    def member_parts(array):
        return [
            lax.dynamic_index_in_dim(array, member ^ j, 0, keepdims=False) for j in range(members)
        ]

    send_some(x_parts[0], x_rows[0], slots // 2 + 1, slots)
    weights = member_parts(pack_expert(w_expand.astype(bf16), w_shrink.astype(bf16)))
    weights = swap_slots(weights, "gi")
    packed.steps("gq")
    x_rows, x_parts, weights = together((x_rows, x_parts, weights), packed)
    packed.at_once("gi")
    weights = jnp.stack(natural(weights, member))
    x_rows, x_parts, weights = together((x_rows, x_parts, weights), packed)
    packed.steps("core")
    x_rows, x_parts, weights = together((x_rows, x_parts, weights), packed)
    tail = weights.shape[1] // 2
    halves = [
        Doubling(half, owners, ("gq", "seq"), 1) for half in (weights[:, :tail], weights[:, tail:])
    ]
    halves[0].steps("gq")
    packed = packed.value.reshape(width, -1)

    old = []
    for row in range(rows):
        old = attend_first(me, row, rows, x_rows[row], packed, parts, old)
        if row + 1 < rows:
            x_rows.append(swap_slots(x_parts[row + 1], "seq"))
            old, x_rows[row + 1] = together((old, x_rows[row + 1]), *halves)
        if row == max(0, rows - 2):
            halves[0].steps("seq")
            halves[1].steps("gq")
        if row == rows - 1:
            old = together(old, *halves)
    vectors = jnp.transpose(packed[:, 4 * width :])
    gain_one = vectors[0:1].astype(f32)
    gain_two = vectors[1:2].astype(f32)
    control = natural([vectors[2 + e : 3 + e] for e in range(experts)], member)
    control = jnp.concatenate(
        [jnp.broadcast_to(c, (LANES // experts, width)) for c in control], axis=0
    )
    att, projected, kept = old[:slots], old[slots : slots + 6], old[slots + 6 :]
    att_parts, kept = [swap_slots(att, "seq")], [kept]
    for part in range(1, parts):
        att, more = attend_next(me, part, parts, projected, slots)
        more, att_parts[-1], gain_one, gain_two, control = hold(
            (more, att_parts[-1], gain_one, gain_two, control)
        )
        att_parts.append(swap_slots(att, "seq"))
        kept.append(more)
    pay_parts = []
    for part in range(parts):
        pay = mix(
            me, part, att_parts[part], inputs, cotangent, packed, gain_two, control, experts
        )
        if part + 1 < parts:
            pay, att_parts[part + 1] = together((pay, att_parts[part + 1]), halves[1])
        if part == 0:
            halves[1].steps("seq")
        if part == parts - 1:
            pay, pay_parts = together((pay, pay_parts), halves[1])
        pay_parts.append(swap_slots(pay, "gi"))
    halves = [half.value.reshape(-1, *half.value.shape[-2:]) for half in halves]
    halves = [(half, partner(half, "seq", slots, 1)) for half in halves]
    ret_parts, earlier = [], []
    for part in range(parts):
        back, more = expert(me, seq_me % 2, part, parts, pay_parts[part], halves, earlier)
        earlier = earlier + list(more)
        if part + 1 < parts:
            pay_parts[part + 1][1], back = hold((pay_parts[part + 1][1], back))
        elif part:
            back, more, ret_parts = hold((back, more, ret_parts))
        ret_parts.append(swap_slots([back] * members, "gi"))

    kept_grad, send = more
    received = partner(send, "seq", slots, 1)
    bits = [2] * len(bits_of((("gq", groups),)))
    bits += [members] + [2] * (len(bits_of((("seq", slots),))) - 1)

    def to_bits(keep, other):
        return (keep.astype(f32) + other.astype(f32)).reshape(*bits, *keep.shape[1:])

    do_parts, grad_middles, before = [], [], []
    for part in range(parts):
        last = part == parts - 1
        if last:
            sum_expert = Halving(to_bits(kept_grad, received), owners, ("seq", "gq"), 1)
            sum_expert.prepare()
            ret_parts[part], before = together((ret_parts[part], before), sum_expert)
        do, grad_middle, before = unmix(
            me,
            part,
            last,
            groups * members * slots,
            ret_parts[part],
            att_parts[part],
            inputs,
            cotangent,
            packed,
            gain_two,
            control,
            before,
        )
        grad_middles.append(grad_middle)
        do_parts.append(swap_slots(do, "seq"))
    output, keep_out, send_out = before
    every_bit = [2] * len(bits_of(place))
    do_parts, send_out = together((do_parts, send_out), sum_expert)
    sum_expert.exchange()
    received_out = partner(send_out, "seq", slots, 1)

    gf_rows, grad_in = [], None
    for row in range(rows):
        gf_slots, grad_in = attend_back(
            me,
            row,
            rows,
            groups * members * slots,
            x_rows[row],
            do_parts,
            gain_one,
            packed,
            projected,
            kept,
            grad_in,
        )
        grad_in = grad_in[0] if row < rows - 1 else grad_in
        if row == 0:
            gf_slots, grad_in, received_out = together((gf_slots, grad_in, received_out), sum_expert)
            sum_expert.combine()
            while sum_expert.order[0][0] == "seq":
                sum_expert.step(sum_expert.order.pop(0))
            sum_expert.prepare()
            gf_slots, grad_in = together((gf_slots, grad_in), sum_expert)
            sum_expert.exchange()
        if row:
            gf_slots, grad_in, gf_rows = together((gf_slots, grad_in, gf_rows), sum_expert)
        if row < rows - 1:
            gf_rows.append(swap_slots(gf_slots, "seq"))
    gf_rows.append([gf_slots[0]])
    send_some(gf_slots, gf_rows[-1], 1, slots // 2 + 1)
    keep, send = grad_in
    received = partner(send, "seq", slots, 1)
    sum_expert.combine()
    sums = sum_expert.finish()
    columns = [p if j == 0 else p.astype(bf16) for j, p in enumerate(member_parts(sums))]
    columns = swap_slots(columns, "gi")
    gf_rows, gf_slots, received, columns = hold((gf_rows, gf_slots, received, columns))
    send_some(gf_slots, gf_rows[-1], slots // 2 + 1, slots)
    total = keep + received.astype(f32)
    total = jnp.concatenate([total, keep_out + received_out.astype(f32)], axis=-1)
    total = total.reshape(*every_bit[1:], *total.shape[1:])
    sum_in = Halving(total, place, ("gi", "gq", "seq"))
    sum_in.cut(("gi",))
    sum_in.send()
    gf_rows = together(gf_rows, sum_in)
    sum_in.combine()
    sum_in.cut(("gq", "seq"))
    gf_rows = together(gf_rows, sum_in)
    sum_in.send()
    grad_inputs = finish(me, gf_rows, inputs, grad_middles, gain_one)
    grad_inputs = together(grad_inputs, sum_in)
    sum_in.combine()
    columns = natural(columns, member)
    columns = jnp.stack([c.astype(f32) for c in columns])
    grad_expand, grad_shrink = unpack_expert(columns, width // (groups * members * slots))
    total = sum_in.finish()
    grad_in, grad_out = total[:, : 3 * width], total[:, 3 * width :]
    small = jnp.transpose(grad_out[:, width:])
    weighted = jnp.sum(grad_in * w_qkv.astype(bf16).astype(f32), axis=1)
    return (
        output,
        grad_inputs,
        weighted / gain_attn.astype(bf16).astype(f32),
        grad_in,
        grad_out[:, :width],
        small[0],
        small[1 : 1 + experts],
        grad_expand,
        grad_shrink,
    )


def solution(mesh):
    dp_count, seq_count = mesh.shape["dp"], mesh.shape["seq"]

    def run(inputs, *args):
        members = GROUP * dp_count // inputs.shape[0]
        sizes = (dp_count // members, members, seq_count)
        fine = Mesh(mesh.devices.reshape(sizes), ("gq", "gi", "seq"))
        dp, both = ("gq", "gi"), ("gq", "gi", "seq")
        return jax.shard_map(
            functools.partial(on_device, sizes),
            mesh=fine,
            in_specs=(
                P(dp, "seq", None),
                P(dp, "seq"),
                P(dp, "seq", None),
                P(both),
                P(both, None),
                P(both, None),
                P(both),
                P(None, both),
                P(None, both, None),
                P(None, both, None),
            ),
            out_specs=(
                P(dp, "seq", None),
                P(dp, "seq", None),
                P(both),
                P(both, None),
                P(both, None),
                P(both),
                P(None, both),
                P(None, both, None),
                P(None, both, None),
            ),
            check_vma=False,
        )(inputs, *args)

    return run
```

```python
import functools
import math

import jax
import jax.numpy as jnp
from jax import lax
from jax.experimental import pallas as pl
from jax.experimental.pallas import tpu as pltpu
from jax.sharding import Mesh
from jax.sharding import PartitionSpec as P

HEADS = 8
GROUP = 32
BLOCK = 256
LANES = 128
MARKS = 16

LOG2E = math.log2(math.e)
LN2 = math.log(2.0)
BIG = 1e30

bf16 = jnp.bfloat16
f32 = jnp.float32

NN = (((1,), (0,)), ((), ()))
NT = (((1,), (1,)), ((), ()))
TN = (((0,), (0,)), ((), ()))


def dot(a, b, dims=NN):
    return lax.dot_general(a, b, dims, preferred_element_type=f32)


def normalize(values):
    center = values - jnp.mean(values, axis=-1, keepdims=True)
    scaled = lax.rsqrt(jnp.mean(center * center, axis=-1, keepdims=True) + 1e-05)
    return center * scaled, scaled


def norm_back(incoming, normed, scaled):
    return scaled * (
        incoming
        - jnp.mean(incoming, axis=-1, keepdims=True)
        - normed * jnp.mean(incoming * normed, axis=-1, keepdims=True)
    )


def split3(value):
    high = value.astype(bf16).astype(f32)
    rest = value - high
    mid = rest.astype(bf16).astype(f32)
    low = (rest - mid).astype(bf16).astype(f32)
    return high, mid, low


def partner(value, axis, size, mask):
    return lax.ppermute(value, axis, [(i, i ^ mask) for i in range(size)])


def swap_slots(slots, axis):
    size = len(slots)
    return [slots[0]] + [partner(slots[j], axis, size, j) for j in range(1, size)]


def natural(slots, me):
    out = list(slots)
    bit = 1
    while bit < len(out):
        flip = (me & bit) != 0
        out = [jnp.where(flip, out[k ^ bit], out[k]) for k in range(len(out))]
        bit *= 2
    return out


def bits_of(sizes):
    bits = []
    for axis, size in sizes:
        mask = size // 2
        while mask:
            bits.append((axis, size, mask))
            mask //= 2
    return bits


def named(bit):
    axis, _, mask = bit
    return "core" if axis == "seq" and mask == 1 else axis


class Steps:
    def __init__(self, value, sizes, order):
        self.order = [bit for axis in order for bit in reversed(bits_of(sizes)) if named(bit) == axis]
        self.value = value

    def steps(self, axis):
        while self.order and named(self.order[0]) == axis:
            self.step(self.order.pop(0))
        return self

    def finish(self):
        while self.order:
            self.step(self.order.pop(0))
        return self.value


class Doubling(Steps):
    def __init__(self, value, sizes, order, inner=0):
        super().__init__(value, sizes, order)
        self.inner = inner
        self.place = bits_of(sizes)
        self.have = []

    def step(self, bit):
        axis, size, mask = bit
        depth = sum(self.place.index(other) < self.place.index(bit) for other in self.have)
        depth += self.inner if axis == "seq" else 0
        other = partner(self.value, axis, size, mask)
        high = (lax.axis_index(axis) & mask) != 0
        first = jnp.where(high, other, self.value)
        second = jnp.where(high, self.value, other)
        self.value = jnp.stack([first, second], axis=depth)
        self.have.append(bit)

    def at_once(self, axis):
        bits = [bit for bit in self.place if bit[0] == axis]
        self.order = [bit for bit in self.order if bit[0] != axis]
        depth = sum(self.place.index(other) < self.place.index(bits[0]) for other in self.have)
        depth += self.inner if axis == "seq" else 0
        slots = natural(swap_slots([self.value] * 2 ** len(bits), axis), lax.axis_index(axis))
        shape = self.value.shape
        value = jnp.stack(slots, axis=depth)
        self.value = value.reshape(shape[:depth] + (2,) * len(bits) + shape[depth:])
        self.have += bits


def total_of(terms):
    return functools.reduce(jnp.add, [term.astype(f32) for term in terms])


class Halving(Steps):
    def __init__(self, value, sizes, order, inner=0):
        super().__init__(None, sizes, order)
        self.terms = value if isinstance(value, list) else [value]
        self.sizes = sizes
        self.left = [bit for bit in bits_of(sizes) if bit in self.order]
        self.inner = inner

    def prepare(self):
        bit = self.order.pop(0)
        depth = self.left.index(bit)
        self.left.pop(depth)
        axis, size, mask = bit
        depth += self.inner if axis == "seq" else 0
        high = ((lax.axis_index(axis) & mask) != 0).astype(jnp.int32)
        keep, send = [
            [lax.dynamic_index_in_dim(term, at, depth, keepdims=False) for term in self.terms]
            for at in (high, 1 - high)
        ]
        self.terms = keep
        self.value = total_of(send).astype(bf16)
        self.link = bit

    def exchange(self):
        axis, size, mask = self.link
        self.value = partner(self.value, axis, size, mask)

    def combine(self):
        if isinstance(self.value, list):
            self.terms = self.value
        else:
            self.terms = self.terms + [self.value]
        self.value = None

    def finish(self):
        super().finish()
        return total_of(self.terms)

    def step(self, bit):
        self.order.insert(0, bit)
        self.prepare()
        self.exchange()
        self.combine()

    def cut(self, axes):
        bits = [bit for bit in self.left if bit[0] in axes]
        self.order = [bit for bit in self.order if bit not in bits]
        depth = self.left.index(bits[0])
        if self.inner or bits != self.left[depth : depth + len(bits)]:
            raise NotImplementedError
        self.left = [bit for bit in self.left if bit not in bits]
        value = total_of(self.terms)
        shape = value.shape
        value = value.reshape(shape[:depth] + (2 ** len(bits),) + shape[depth + len(bits) :])
        place = 0
        for axis, size, mask in bits:
            place = 2 * place + ((lax.axis_index(axis) & mask) != 0).astype(jnp.int32)
        parts = [
            lax.dynamic_index_in_dim(value, place ^ j, depth, keepdims=False)
            for j in range(2 ** len(bits))
        ]
        self.value = [parts[0]] + [part.astype(bf16) for part in parts[1:]]
        self.link = bits

    def send(self):
        bits = self.link
        sizes = [(axis, size) for axis, size in self.sizes if axis in [bit[0] for bit in bits]]
        names = tuple(axis for axis, _ in sizes)
        for j in range(1, 2 ** len(bits)):
            masks = {axis: 0 for axis in names}
            for i, (axis, _, mask) in enumerate(bits):
                if j >> (len(bits) - 1 - i) & 1:
                    masks[axis] |= mask
            pairs = []
            for source in range(math.prod(size for _, size in sizes)):
                target, rest, unit = 0, source, 1
                for axis, size in reversed(sizes):
                    target += ((rest % size) ^ masks[axis]) * unit
                    rest, unit = rest // size, unit * size
                pairs.append((source, target))
            self.value[j] = lax.ppermute(self.value[j], names, pairs)


hold = lax.optimization_barrier


def together(values, *sums):
    values, held = lax.optimization_barrier((values, [item.value for item in sums]))
    for item, value in zip(sums, held):
        item.value = value
    return values


def call(kernel, name, grid, in_specs, outs, scratch, args, micros, aliases=None, room=10):
    def full(shape):
        return pl.BlockSpec(shape, lambda *_: (0,) * len(shape))

    in_specs = [spec or full(arg.shape) for spec, arg in zip(in_specs, args[1:], strict=True)]
    outs = [(spec or full(shape), shape, dtype) for spec, shape, dtype in outs]
    return pl.pallas_call(
        kernel,
        grid_spec=pltpu.PrefetchScalarGridSpec(
            num_scalar_prefetch=1,
            grid=grid,
            in_specs=in_specs,
            out_specs=[spec for spec, _, _ in outs],
            scratch_shapes=[pltpu.VMEM(shape, dtype) for shape, dtype in scratch],
        ),
        out_shape=[jax.ShapeDtypeStruct(shape, dtype) for _, shape, dtype in outs],
        input_output_aliases=aliases or {},
        compiler_params=pltpu.CompilerParams(vmem_limit_bytes=room << 20),
        cost_estimate=pl.CostEstimate(
            flops=int(micros * 1e9), bytes_accessed=1 << 20, transcendentals=0
        ),
        name=name,
    )(*args)


def per_row(*shape):
    return pl.BlockSpec((1,) + shape, lambda r, me: (r,) + (0,) * len(shape))


def whole(*shape):
    return pl.BlockSpec(shape, lambda r, me: (0,) * len(shape))


def fourth(width):
    return pl.BlockSpec((width, width), lambda b, me: (0, 3))


def by_core(me, pairs):
    odd = me % 2 == 1
    first, second = pairs[:, 0], pairs[:, 1]
    return jnp.where(odd, second, first), jnp.where(odd, first, second)


def causal_bias(step=LANES):
    rows = LANES + step * (BLOCK // LANES - 1)
    key = lax.broadcasted_iota(jnp.int32, (rows, BLOCK), 0)
    query = lax.broadcasted_iota(jnp.int32, (rows, BLOCK), 1)
    query = query + (query // LANES) * (step - LANES)
    return jnp.where(key <= query, 0.0, -BIG).astype(f32)


def key_features(segment_row, length):
    row = lax.broadcasted_iota(jnp.int32, (LANES, length), 0)
    marks = (row == segment_row) | ((row >= 7) & (row < 10))
    return jnp.where(marks, 1.0, 0.0).astype(f32).T.astype(bf16)


def query_features(segment_row, length):
    row = lax.broadcasted_iota(jnp.int32, (16, length), 0)
    return jnp.where((row < 7) & (row != segment_row), -BIG, 0.0).astype(f32)


def padded_head(head, features, odd):
    blank = jnp.zeros_like(head)
    rest = jnp.zeros((LANES - 16, head.shape[1]), bf16)
    both = [blank, head] if odd else [head, blank]
    return jnp.concatenate(both + [features, rest], axis=0)


def attend_queries(part, parts, slots, me, seg_ref, q_t, k_ref, v_t, att_refs, ot_ref, lse_ref, aux):
    k_aux, q_aux, causal = aux
    length = k_ref.shape[1]
    piece = length // slots
    some = piece // parts
    step = piece if parts > 1 else LANES
    segment_row = seg_ref[0]
    q_aux[...] = query_features(segment_row, length)
    k_aux[...] = key_features(segment_row, length)
    blocks = slots * some // BLOCK
    count = BLOCK // some if parts > 1 else 1

    def head_pair(pair, carry):
        base = pl.multiple_of(pair * LANES, LANES)
        for odd in range(2):
            rows = pl.ds(pl.multiple_of(pair * LANES + odd * 64, 64), 64)
            for block in range(blocks):
                if parts > 1:
                    first = block * count * piece + part * some
                    places = [pl.ds(first + i * piece, some) for i in range(count)]
                else:
                    first = block * BLOCK
                    places = [pl.ds(first, BLOCK)]
                feats = jnp.concatenate([q_aux[:, p] for p in places], axis=1).astype(bf16)
                head = jnp.concatenate([q_t[0, rows, p] for p in places], axis=1)
                query = padded_head(head, feats, odd)
                chunks = [(k, min(BLOCK, first - k)) for k in range(0, first, BLOCK)]
                chunks.append((first, causal.shape[0]))
                scores = []
                for start, size in chunks:
                    keys = pl.ds(start, size)
                    key = jnp.concatenate([k_ref[0, keys, pl.ds(base, LANES)], k_aux[keys]], axis=1)
                    score = dot(key, query)
                    scores.append(score + causal[...] if start == first else score)
                top = functools.reduce(
                    jnp.maximum, [jnp.max(score, axis=0, keepdims=True) for score in scores]
                )
                total = jnp.zeros((1, BLOCK), f32)
                out = jnp.zeros((64, BLOCK), f32)
                for (start, size), score in zip(chunks, scores):
                    prob = jnp.exp2(score - top)
                    total = total + jnp.sum(prob, axis=0, keepdims=True)
                    out = out + dot(v_t[0, rows, pl.ds(start, size)], prob.astype(bf16))
                held = pl.ds(block * BLOCK, BLOCK)
                ot_ref[0, rows, held] = (out / total).astype(bf16)
                lse_ref[0, pl.ds(pair * 2 + odd, 1), held] = top + jnp.log2(total)
        return carry

    lax.fori_loop(0, HEADS // 2, head_pair, 0)
    for j in range(slots):
        place = pl.ds(pl.multiple_of((me ^ j) * some, some), some)
        att_refs[j][0] = ot_ref[0, :, place].T


def attend_first_kernel(parts, slots, old, *refs):
    me_ref = refs[0]
    x_refs = refs[1 : 1 + slots]
    vector_ref, w_ref = refs[1 + slots : 3 + slots]
    rest = refs[3 + slots + old :]
    att_refs = rest[:slots]
    seg_ref, qt_ref, k_ref, v_ref, q_ref, vt_ref, ot_ref, lse_ref, rows_ref = rest[slots : slots + 9]
    w_t, *aux = rest[slots + 9 :]
    width = w_ref.shape[0]
    piece = x_refs[0].shape[1] - MARKS
    me = me_ref[0]
    score_scale = LOG2E / math.sqrt(width // HEADS)

    w_t[:width] = w_ref[:, :width].T
    w_t[width:] = w_ref[:, 2 * width :].T
    aux[2][...] = causal_bias(piece if parts > 1 else LANES)
    rows_ref[...] = vector_ref[...].astype(f32).T
    gain = rows_ref[0:1]
    for j in range(slots):
        place = pl.ds(pl.multiple_of((me ^ j) * piece, piece), piece)
        marks = x_refs[j][0, piece:].astype(f32)
        seg_ref[0, :, place] = marks[0:1, :piece].astype(jnp.int32)
        normed, _ = normalize(x_refs[j][0, :piece].astype(f32))
        first_in = (normed * gain).astype(bf16)
        projected = dot(first_in, w_ref[...])
        q_ref[0, place] = (projected[:, :width] * score_scale).astype(bf16)
        k_ref[0, place] = projected[:, width : 2 * width].astype(bf16)
        v_ref[0, place] = projected[:, 2 * width :].astype(bf16)
        turned = dot(w_t[...], first_in, NT)
        qt_ref[0, :, place] = (turned[:width] * score_scale).astype(bf16)
        vt_ref[0, :, place] = turned[width:].astype(bf16)
    attend_queries(
        0, parts, slots, me, seg_ref, qt_ref, k_ref, vt_ref, att_refs, ot_ref, lse_ref, aux
    )


def attend_next_kernel(part, parts, slots, *refs):
    me_ref, seg_ref, qt_ref, k_ref, vt_ref = refs[:5]
    att_refs = refs[5 : 5 + slots]
    ot_ref, lse_ref, *aux = refs[5 + slots :]

    @pl.when(pl.program_id(0) == 0)
    def _():
        aux[2][...] = causal_bias(k_ref.shape[1] // slots if parts > 1 else LANES)

    attend_queries(
        part, parts, slots, me_ref[0], seg_ref, qt_ref, k_ref, vt_ref, att_refs, ot_ref, lse_ref, aux
    )


def attend_outs(rows, slots, some, width):
    return [(per_row(some, width), (rows, some, width), bf16)] * slots, [
        (per_row(width, slots * some), (rows, width, slots * some), bf16),
        (per_row(HEADS, slots * some), (rows, HEADS, slots * some), f32),
    ]


def attend_scratch(length, piece, parts):
    span = LANES + (piece if parts > 1 else LANES) * (BLOCK // LANES - 1)
    return [((length, LANES), bf16), ((16, length), f32), ((span, BLOCK), f32)]


def attend_first(me, row, rows, x_slots, weights, parts, old):
    slots = len(x_slots)
    _, packed, width = x_slots[0].shape
    piece = packed - MARKS
    length = piece * slots

    def this(*shape):
        return pl.BlockSpec((1,) + shape, lambda r, me: (row,) + (0,) * len(shape))

    some = piece // parts
    turned = (this(width, length), (rows, width, length), bf16)
    plain = (this(length, width), (rows, length, width), bf16)
    outs = (
        [(this(some, width), (rows, some, width), bf16)] * slots
        + [(this(1, length), (rows, 1, length), jnp.int32)]
        + [turned, plain, plain, plain, turned]
        + [
            (this(width, slots * some), (rows, width, slots * some), bf16),
            (this(HEADS, slots * some), (rows, HEADS, slots * some), f32),
            (whole(LANES, width), (LANES, width), f32),
        ]
    )
    result = call(
        functools.partial(attend_first_kernel, parts, slots, len(old)),
        "attend_first",
        (1,),
        [per_row(packed, width)] * slots
        + [
            pl.BlockSpec((width, LANES), lambda r, me: (0, 4 * width // LANES)),
            whole(width, 3 * width),
        ]
        + [pl.BlockSpec(memory_space=pl.ANY)] * len(old),
        outs,
        [((2 * width, width), bf16)] + attend_scratch(length, piece, parts),
        (me, *x_slots, weights, weights, *old),
        12,
        {3 + slots + i: i for i in range(len(old))},
        room=26,
    )
    return result


def attend_next(me, part, parts, projected, slots):
    segment_rows, q_t, k, _, _, v_t = projected
    rows, length, width = k.shape
    piece = length // slots
    att, more = attend_outs(rows, slots, piece // parts, width)
    result = call(
        functools.partial(attend_next_kernel, part, parts, slots),
        "attend_next",
        (rows,),
        [
            per_row(1, length),
            per_row(width, length),
            per_row(length, width),
            per_row(width, length),
        ],
        att + more,
        attend_scratch(length, piece, parts),
        (me, segment_rows, q_t, k, v_t),
        28 / parts,
        room=16,
    )
    return result[:slots], result[slots:]


def attend_back_kernel(row, last, parts, slot_count, *refs):
    me_ref = refs[0]
    x_refs = refs[1 : 1 + slot_count]
    rest = refs[1 + slot_count :]
    do_refs, rest = rest[: parts * slot_count], rest[parts * slot_count :]
    seg_ref, gain_ref, w_ref, qt_ref, k_ref, v_ref, q_ref = rest[:7]
    ot_refs, lse_refs = rest[7 : 7 + parts], rest[7 + parts : 7 + 2 * parts]
    rest = rest[7 + 2 * parts :]
    if row:
        before_ref, rest = rest[0], rest[1:]
    gf_refs, rest = rest[:slot_count], rest[slot_count:]
    dw_refs, rest = rest[: 1 + last], rest[1 + last :]
    (
        k_aux, q_aux, v_aux, causal, do, first_t, work_t, k_t, grads, prob, grad_score, delta, lse
    ) = rest
    width = w_ref.shape[0]
    piece = x_refs[0].shape[1] - MARKS
    some = piece // parts
    length = piece * slot_count
    me = me_ref[0]
    score_scale = 1.0 / math.sqrt(width // HEADS)
    causal[...] = causal_bias()
    lane = lax.broadcasted_iota(jnp.int32, (length, LANES), 1)
    v_aux[...] = jnp.where(lane < 3, 1.0, 0.0).astype(bf16)
    for part in range(parts):
        for i in range(slot_count):
            held = pl.ds(i * some, some)
            lse[:, pl.ds(i * piece + part * some, some)] = lse_refs[part][0, :, held]

    segment_row = seg_ref[0]
    q_aux[...] = query_features(segment_row, length)
    k_aux[...] = key_features(segment_row, length)
    gain = gain_ref[...]
    for j in range(slot_count):
        place = pl.ds(pl.multiple_of((me ^ j) * piece, piece), piece)
        normed, _ = normalize(x_refs[j][0, :piece].astype(f32))
        first_t[:, place] = (normed * gain).astype(bf16).T
        k_t[:, place] = k_ref[0, place].T
        for part in range(parts):
            start = (me ^ j) * piece + part * some
            place = pl.ds(pl.multiple_of(start, some), some)
            held = pl.ds(pl.multiple_of((me ^ j) * some, some), some)
            grad = do_refs[part * slot_count + j][0]
            do[place] = grad
            turned = grad.T
            work_t[:, place] = turned
            product = turned.astype(f32) * ot_refs[part][0, :, held].astype(f32)
            delta[:, place] = jnp.sum(product.reshape(HEADS, width // HEADS, some), axis=1)
    lane = lax.broadcasted_iota(jnp.int32, (1, LANES), 1)
    feature = lax.broadcasted_iota(jnp.int32, (16, BLOCK), 0)
    blocks = length // BLOCK

    def head_pair(pair, carry):
        base = pl.multiple_of(pair * LANES, LANES)
        for odd in range(2):
            rows = pl.ds(pl.multiple_of(pair * LANES + odd * 64, 64), 64)
            head = pl.ds(pair * 2 + odd, 1)
            for qb in range(blocks):
                queries = pl.ds(qb * BLOCK, BLOCK)
                a, b, c = split3(lse[head, queries])
                feats = jnp.where(feature == 7, -a, q_aux[:, queries])
                feats = jnp.where(feature == 8, -b, jnp.where(feature == 9, -c, feats))
                query = padded_head(qt_ref[0, rows, queries], feats.astype(bf16), odd)
                a, b, c = split3(delta[head, queries])
                feats = jnp.where(feature == 0, -a, jnp.where(feature == 1, -b, 0.0))
                feats = jnp.where(feature == 2, -c, feats)
                grad = padded_head(work_t[rows, queries], feats.astype(bf16), odd)
                held = pl.ds(odd * length + qb * BLOCK, BLOCK)
                for kb in range(qb + 1):
                    keys = pl.ds(kb * BLOCK, BLOCK)
                    key = jnp.concatenate([k_ref[0, keys, pl.ds(base, LANES)], k_aux[keys]], axis=1)
                    score = dot(key, query)
                    if kb == qb:
                        score = score + causal[...]
                    value = jnp.concatenate(
                        [v_ref[0, keys, pl.ds(base, LANES)], v_aux[keys]], axis=1
                    )
                    grad_prob = dot(value, grad)
                    weight = jnp.exp2(score)
                    prob[keys, held] = weight.astype(bf16)
                    grad_score[keys, held] = (weight * grad_prob).astype(bf16)
                end = (qb + 1) * BLOCK
                grad_q = dot(k_t[rows, 0:end], grad_score[0:end, held])
                work_t[rows, queries] = (grad_q * score_scale).astype(bf16)
        for kb in range(blocks):
            keys = pl.ds(kb * BLOCK, BLOCK)
            later = pl.ds(kb * BLOCK, length - kb * BLOCK)
            grad_v = jnp.zeros((BLOCK, LANES), f32)
            grad_k = jnp.zeros((BLOCK, LANES), f32)
            for odd in range(2):
                mine = (lane >= 64) if odd else (lane < 64)
                held = pl.ds(odd * length + kb * BLOCK, length - kb * BLOCK)
                zero = jnp.zeros((), bf16)
                grad = jnp.where(mine, do[later, pl.ds(base, LANES)], zero)
                query = jnp.where(mine, q_ref[0, later, pl.ds(base, LANES)], zero)
                grad_v = grad_v + dot(prob[keys, held], grad)
                grad_k = grad_k + dot(grad_score[keys, held], query)
            grads[keys, pl.ds(pl.multiple_of(width + pair * LANES, LANES), LANES)] = (
                grad_k * LN2
            ).astype(bf16)
            grads[keys, pl.ds(pl.multiple_of(2 * width + pair * LANES, LANES), LANES)] = (
                grad_v.astype(bf16)
            )
        return carry

    lax.fori_loop(0, HEADS // 2, head_pair, 0)
    for j in range(slot_count):
        place = pl.ds(pl.multiple_of((me ^ j) * piece, piece), piece)
        grads[place, :width] = work_t[:, place].T
        gf_refs[j][0] = dot(grads[place], w_ref[...], NT).astype(bf16)
    update = dot(first_t[...], grads[...])
    if row:
        update = before_ref[...] + update
    if last:
        keep, send = by_core(me, update.reshape(-1, 2, *dw_refs[0].shape[1:]))
        dw_refs[0][...] = keep
        dw_refs[1][...] = send.astype(bf16)
    else:
        dw_refs[0][...] = update


def attend_back(me, row, rows, shards, x_slots, do_parts, gain, w_qkv, projected, kept, before):
    slot_count, parts = len(x_slots), len(do_parts)
    _, packed, width = x_slots[0].shape
    piece = packed - MARKS
    length = piece * slot_count
    some = piece // parts
    last = row == rows - 1

    def this(*shape):
        return pl.BlockSpec((1,) + shape, lambda r, me: (row,) + (0,) * len(shape))

    half = (shards // 2, width // shards, 3 * width)
    outs = [(per_row(piece, width), (1, piece, width), bf16)] * slot_count
    if last:
        outs += [(whole(*half), half, f32), (whole(*half), half, bf16)]
    else:
        outs += [(whole(width, 3 * width), (width, 3 * width), f32)]
    segment_rows, q_t, k, v, q, _ = projected
    result = call(
        functools.partial(attend_back_kernel, row, last, parts, slot_count),
        "attend_back",
        (1,),
        [per_row(packed, width)] * slot_count
        + [this(some, width)] * (parts * slot_count)
        + [this(1, length), whole(1, width), whole(width, 3 * width)]
        + [this(width, length)]
        + [this(length, width)] * 3
        + [this(width, some * slot_count)] * parts
        + [this(HEADS, some * slot_count)] * parts
        + ([whole(width, 3 * width)] if row else []),
        outs,
        [
            ((length, LANES), bf16),
            ((16, length), f32),
            ((length, LANES), bf16),
            ((BLOCK, BLOCK), f32),
            ((length, width), bf16),
            ((width, length), bf16),
            ((width, length), bf16),
            ((width, length), bf16),
            ((length, 3 * width), bf16),
            ((length, 2 * length), bf16),
            ((length, 2 * length), bf16),
            ((HEADS, length), f32),
            ((HEADS, length), f32),
        ],
        (
            me,
            *x_slots,
            *[do for part in do_parts for do in part],
            segment_rows,
            gain,
            w_qkv,
            q_t,
            k,
            v,
            q,
            *[o for o, _ in kept],
            *[l for _, l in kept],
            *([before] if row else []),
        ),
        28,
        room=60,
    )
    return result[:slot_count], result[slot_count:]


def tokens_of(refs, span):
    return jnp.concatenate([ref[:, span] for ref in refs], axis=0).reshape(-1, refs[0].shape[-1])


def rows_of(ref, me, rows, slot_count, span):
    parts = [ref[pl.ds((me ^ j) * rows, rows), span] for j in range(slot_count)]
    return jnp.concatenate(parts, axis=0).reshape(-1, ref.shape[-1])


def diagonal(piece):
    place = lax.broadcasted_iota(jnp.int32, (piece, LANES), 0)
    lane = lax.broadcasted_iota(jnp.int32, (piece, LANES), 1)
    return place == lane % piece, lane // piece, lane


def mix_kernel(slot_count, experts, piece, *refs):
    me_ref = refs[0]
    att_refs = refs[1 : 1 + slot_count]
    inputs_ref, cot_ref, w_out_ref, gain_ref, control_ref = refs[1 + slot_count : 6 + slot_count]
    pay_refs = refs[6 + slot_count :]
    rows, positions, width = att_refs[0].shape
    tokens = rows * slot_count
    me = me_ref[0]
    own, _, lane = diagonal(piece)
    w_out = w_out_ref[...]
    for sub in range(positions // piece):
        span = slice(sub * piece, (sub + 1) * piece)
        added = dot(tokens_of(att_refs, span), w_out)
        second = []
        for token in range(tokens):
            row = (me ^ (token // rows)) * rows + token % rows
            middle = inputs_ref[row, span].astype(f32) + added[token * piece : (token + 1) * piece]
            normed, _ = normalize(middle)
            second.append((normed * gain_ref[...]).astype(bf16))
        second = jnp.concatenate(second, axis=0)
        grad = rows_of(cot_ref, me, rows, slot_count, span)
        logits = dot(second, control_ref[...], NT).reshape(tokens, piece, LANES)
        top = jnp.max(logits, axis=0)
        weights = jnp.exp(logits - top)
        total = jnp.sum(weights, axis=0)
        log_total = top + jnp.log(total)
        weights = jnp.where(own, weights * (1.0 / total), 0.0)
        spread_out = weights.reshape(-1, LANES).astype(bf16)
        mixed = dot(spread_out, second, TN).astype(bf16)
        grad_results = dot(spread_out, grad, TN).astype(bf16)
        a, b, c = split3(log_total)
        for e in range(experts):
            mine = slice(e * piece, (e + 1) * piece)
            first = slice(e * piece, e * piece + 1)
            stats = jnp.where(lane == 0, a[:, first], jnp.where(lane == 1, b[:, first], c[:, first]))
            pay_refs[e][span, :width] = mixed[mine]
            pay_refs[e][span, width : 2 * width] = grad_results[mine]
            pay_refs[e][span, 2 * width :] = stats.astype(bf16)


def mix(me, part, att_slots, inputs, cotangent, w_out, gain, control, experts):
    slot_count = len(att_slots)
    rows, positions, width = att_slots[0].shape
    tokens = rows * slot_count
    half = pl.BlockSpec((tokens, positions, width), lambda b, me: (0, part, 0))
    pay = (None, (positions, 2 * width + LANES), bf16)
    return call(
        functools.partial(mix_kernel, slot_count, experts, LANES // experts),
        "mix",
        (1,),
        [None] * slot_count + [half, half, fourth(width), None, None],
        [pay] * experts,
        [],
        (me, *att_slots, inputs, cotangent, w_out, gain, control),
        positions * 8 / 256,
    )


def expert_kernel(part, parts, tiled, slot_count, *refs):
    me_ref = refs[0]
    pay_refs = refs[1 : 1 + slot_count]
    rest = refs[1 + slot_count :]
    count = 4 if tiled else 2
    weight_refs, rest = rest[:count], rest[count:]
    expand_ref = weight_refs[0]
    last = part == parts - 1
    earlier, rest = rest[: 4 * part], rest[4 * part :]
    if last:
        back_ref, keep_ref, send_ref = rest[:3]
        mixed_acc, grad_acc, result_acc, back_acc, stat, *more, mixed_low, grad_low = rest[3:]
    else:
        back_ref, mixed_low, grad_low, hidden_ref, pre_ref = rest[:5]
        mixed_acc, grad_acc, result_acc, back_acc, stat, *more = rest[5:]
    me = me_ref[0]
    width = expand_ref.shape[-1]
    step = pl.program_id(0)

    @pl.when(step == 0)
    def _():
        logs = []
        for j in range(slot_count):
            stats = pay_refs[j][:, 2 * width :].astype(f32)
            logs.append(stats[:, 0:1] + stats[:, 1:2] + stats[:, 2:3])
        top = functools.reduce(jnp.maximum, logs)
        total = functools.reduce(jnp.add, [jnp.exp(log - top) for log in logs])
        log_total = top + jnp.log(total)
        mixed, grad = 0.0, 0.0
        for j in range(slot_count):
            share = jnp.exp(logs[j] - log_total)
            mixed = mixed + share * pay_refs[j][:, :width].astype(f32)
            grad = grad + share * pay_refs[j][:, width : 2 * width].astype(f32)
        mixed_acc[...] = mixed
        grad_acc[...] = grad
        mixed_low[...] = mixed.astype(bf16)
        grad_low[...] = grad.astype(bf16)
        result_acc[...] = jnp.zeros_like(result_acc)
        back_acc[...] = jnp.zeros_like(back_acc)
        stat[...] = jnp.broadcast_to(log_total, stat.shape)

    mixed, grad = mixed_low[...], grad_low[...]
    if tiled:
        for i in range(2):
            own, other = weight_refs[2 * i][...], weight_refs[2 * i + 1][...]
            odd = me % 2 == 1
            more[i][:, 0] = jnp.where(odd, other, own)
            more[i][:, 1] = jnp.where(odd, own, other)
        expand, shrink = [ref[...].reshape(-1, width) for ref in more]
    else:
        expand, shrink = [ref[...].reshape(-1, width) for ref in weight_refs]
    value = dot(mixed, expand)
    coeff = math.sqrt(2.0 / math.pi)
    square = value * value
    turn = jnp.tanh(coeff * (value + 0.044715 * (square * value)))
    half = 0.5 * (1.0 + turn)
    hidden = (value * half).astype(bf16)
    slope = half + (0.5 * coeff) * value * (1.0 - turn * turn) * (1.0 + (3 * 0.044715) * square)
    result_acc[...] += dot(hidden, shrink)
    grad_pre = (dot(grad, shrink, NT) * slope).astype(bf16)
    back_acc[...] += dot(grad_pre, expand, NT)
    if last:
        sets = [earlier[4 * i : 4 * i + 4] for i in range(part)]
        mixed = jnp.concatenate([m[...] for m, _, _, _ in sets] + [mixed], axis=0)
        grad = jnp.concatenate([g[...] for _, g, _, _ in sets] + [grad], axis=0)
        hidden = jnp.concatenate([h[...] for _, _, h, _ in sets] + [hidden], axis=0)
        grad_pre = jnp.concatenate([p[...] for _, _, _, p in sets] + [grad_pre], axis=0)
        grad_expand = dot(mixed, grad_pre, TN).astype(bf16)
        grad_shrink = dot(hidden, grad, TN).astype(bf16)
        if tiled:
            shards = 2 * keep_ref.shape[0]
            lines = width // shards
            both = keep_ref.shape[1]
            keep, send = by_core(me, grad_expand.reshape(shards // 2, 2, lines, width))
            place = pl.ds(pl.multiple_of(step * lines, lines), lines)
            keep_ref[:, place] = keep
            send_ref[:, place] = send
            count = 2 * width // both // 2
            keep, send = by_core(me, grad_shrink.reshape(count, 2, both // 2, width))
            place = pl.ds(step * count, count)
            keep_ref[place, both // 2 :] = keep
            send_ref[place, both // 2 :] = send
        else:
            keep_ref[...] = grad_expand.reshape(keep_ref.shape)
            send_ref[...] = grad_shrink.reshape(send_ref.shape)
    else:
        hidden_ref[...] = hidden
        pre_ref[...] = grad_pre

    @pl.when(step == pl.num_programs(0) - 1)
    def _():
        results = result_acc[...].astype(bf16)
        back = back_acc[...].astype(bf16)
        back_ref[:, :width] = results
        back_ref[:, width : 2 * width] = back
        inner = jnp.sum(
            results.astype(f32) * grad_acc[...] + back.astype(f32) * mixed_acc[...],
            axis=-1,
            keepdims=True,
        )
        lane = lax.broadcasted_iota(jnp.int32, stat.shape, 1)
        a, b, c = split3(stat[...])
        d, e, f = split3(inner)
        stats = jnp.where(lane == 0, a, jnp.where(lane == 1, b, c))
        stats = jnp.where(lane < 3, stats, jnp.where(lane == 3, d, jnp.where(lane == 4, e, f)))
        back_ref[:, 2 * width :] = stats.astype(bf16)


def pack_expert(expand, shrink):
    experts, lines, hidden = expand.shape
    width = shrink.shape[-1]
    expand = expand.reshape(experts, lines, hidden // width, width)
    expand = jnp.swapaxes(expand, 1, 2).reshape(experts, -1, width)
    return jnp.concatenate([expand, shrink], axis=1)


def unpack_expert(packed, lines):
    experts, both, width = packed.shape
    expand = packed[:, : both // 2].reshape(experts, -1, lines, width)
    expand = jnp.swapaxes(expand, 1, 2).reshape(experts, lines, -1)
    return expand, packed[:, both // 2 :]


def expert(me, core, part, parts, pay_slots, halves, earlier):
    slot_count = len(pay_slots)
    groups, packed = pay_slots[0].shape
    shards = 2 * halves[0][0].shape[0]
    tail, width = halves[0][0].shape[1:]
    hidden = shards * tail
    chunks = hidden // width
    lines = width // shards
    acc = ((groups, width), f32)
    low = ((groups, width), bf16)
    tiled = lines % 16 == 0
    group = shards // chunks // 2
    if tiled:
        columns = pl.BlockSpec((shards // 2, lines, width), lambda f, me: (0, f, 0))
        lower = pl.BlockSpec((group, tail, width), lambda f, me: (f, 0, 0))
        weights = [*halves[0], *halves[1]]
        specs = [columns, columns, lower, lower]
        built = [((shards // 2, 2, lines, width), bf16), ((group, 2, tail, width), bf16)]
        both = (shards // 2, 2 * tail, width)
        grads = [(whole(*both), both, bf16)] * 2
    else:
        odd = core == 1
        weights = [
            jnp.stack([jnp.where(odd, b, a), jnp.where(odd, a, b)], axis=1) for a, b in halves
        ]
        expand = weights[0].reshape(shards, chunks, lines, width)
        expand = jnp.swapaxes(expand, 0, 1).reshape(chunks, width, width)
        weights = [expand, weights[1].reshape(chunks, width, width)]
        specs = [pl.BlockSpec((1, width, width), lambda f, me: (f, 0, 0))] * 2
        built = []
        grads = [(specs[0], (chunks, width, width), bf16)] * 2
    token = whole(groups, width)
    inner = pl.BlockSpec((groups, width), lambda f, me: (0, f))
    last = part == parts - 1
    outs = [(whole(groups, packed), (groups, packed), bf16)]
    scratch = [acc, acc, acc, acc, ((groups, LANES), f32)] + built
    if last:
        outs += grads
        scratch += [low, low]
    else:
        outs += [(token, (groups, width), bf16)] * 2 + [(inner, (groups, hidden), bf16)] * 2
    result = call(
        functools.partial(expert_kernel, part, parts, tiled, slot_count),
        "expert",
        (chunks,),
        [whole(groups, packed)] * slot_count + specs + [token, token, inner, inner] * part,
        outs,
        scratch,
        (me, *pay_slots, *weights, *earlier),
        7,
        room=18,
    )
    more = list(result[1:])
    if last and not tiled:
        grad = jnp.swapaxes(more[0].reshape(chunks, shards, lines, width), 0, 1)
        more = [grad.reshape(shards, tail, width), more[1].reshape(shards, tail, width)]
        more = jnp.concatenate(more, axis=1).reshape(shards // 2, 2, 2 * tail, width)
        odd = core == 1
        more = [
            jnp.where(odd, more[:, 1], more[:, 0]),
            jnp.where(odd, more[:, 0], more[:, 1]),
        ]
    return result[0], more


def unmix_kernel(slot_count, experts, piece, part, last, *refs):
    me_ref = refs[0]
    ret_refs = refs[1 : 1 + experts]
    att_refs = refs[1 + experts : 1 + experts + slot_count]
    rest = refs[1 + experts + slot_count :]
    inputs_ref, cot_ref, w_out_ref, gain_ref, control_ref = rest[:5]
    rest = rest[5:]
    if part:
        old_out_ref, old_control_ref, old_gain_ref = rest[1:4]
        rest = rest[4:]
    out_ref, grad_middle_ref = rest[:2]
    back_refs = rest[2 : 2 + slot_count]
    rest = rest[2 + slot_count :]
    if last:
        keep_ref, send_ref, middle_scratch, small = rest
    else:
        grad_out_ref, grad_control_ref, grad_gain_ref, middle_scratch = rest
    rows, positions, width = att_refs[0].shape
    tokens = rows * slot_count
    me = me_ref[0]

    own, group, _ = diagonal(piece)
    control = control_ref[...]
    w_out = w_out_ref[...]
    grad_out, grad_control, grad_gain = 0.0, 0.0, 0.0
    if part:
        grad_out, grad_control = old_out_ref[...], old_control_ref[...]
        grad_gain = old_gain_ref[...]
    for sub in range(positions // piece):
        span = slice(sub * piece, (sub + 1) * piece)
        attended = tokens_of(att_refs, span)
        added = dot(attended, w_out)
        second = []
        for token in range(tokens):
            row = (me ^ (token // rows)) * rows + token % rows
            middle = inputs_ref[row, span].astype(f32) + added[token * piece : (token + 1) * piece]
            middle_scratch[token] = middle
            normed, _ = normalize(middle)
            second.append((normed * gain_ref[...]).astype(bf16))
        second = jnp.concatenate(second, axis=0)
        cot = rows_of(cot_ref, me, rows, slot_count, span)
        log_total = jnp.zeros((piece, LANES), f32)
        inner = jnp.zeros((piece, LANES), f32)
        for e in range(experts):
            stats = ret_refs[e][span, 2 * width :].astype(f32)
            mine = group == e
            log_total = jnp.where(mine, stats[:, 0:1] + stats[:, 1:2] + stats[:, 2:3], log_total)
            inner = jnp.where(mine, stats[:, 3:4] + stats[:, 4:5] + stats[:, 5:6], inner)
        results = jnp.concatenate([ref[span, :width] for ref in ret_refs], axis=0)
        back = jnp.concatenate([ref[span, width : 2 * width] for ref in ret_refs], axis=0)
        logits = dot(second, control, NT).reshape(tokens, piece, LANES)
        weights = jnp.where(own, jnp.exp(logits - log_total), 0.0)
        low = weights.reshape(-1, LANES).astype(bf16)
        spread = dot(low, results)
        grad_weights = (dot(cot, results, NT) + dot(second, back, NT)).reshape(tokens, piece, LANES)
        grad_logits = (weights * (grad_weights - inner)).reshape(-1, LANES).astype(bf16)
        grad_second = dot(low, back) + dot(grad_logits, control)
        grad_control = grad_control + dot(grad_logits, second, TN)
        grad_middles = []
        for token in range(tokens):
            row = (me ^ (token // rows)) * rows + token % rows
            mine = slice(token * piece, (token + 1) * piece)
            middle = middle_scratch[token]
            out_ref[row, span] = (middle + spread[mine].astype(bf16).astype(f32)).astype(bf16)
            grad = grad_second[mine].astype(bf16).astype(f32)
            normed, scaled = normalize(middle)
            grad_gain = grad_gain + jnp.sum((grad * normed).reshape(-1, 8, width), axis=0)
            grad_middle = norm_back(grad * gain_ref[...], normed, scaled)
            grad_middle = (cot_ref[row, span].astype(f32) + grad_middle).astype(bf16)
            grad_middle_ref[token, span] = grad_middle
            grad_middles.append(grad_middle)
        grad_middle = jnp.concatenate(grad_middles, axis=0)
        grad_attended = dot(grad_middle, w_out, NT).astype(bf16)
        grad_attended = grad_attended.reshape(tokens, piece, width)
        for j in range(slot_count):
            back_refs[j][:, span] = grad_attended[j * rows : (j + 1) * rows]
        grad_out = grad_out + dot(attended, grad_middle, TN)
    if last:
        small[...] = jnp.zeros_like(small)
        small[0:1] = jnp.sum(grad_gain, axis=0, keepdims=True)
        for e in range(experts):
            total = grad_control[e * piece : (e + 1) * piece]
            small[pl.ds(1 + (me_ref[1] ^ e), 1)] = jnp.sum(total, axis=0, keepdims=True)
        blocks, lines = keep_ref.shape[:2]
        for columns, value in (
            (slice(0, width), grad_out),
            (slice(width, width + LANES), small[...].T),
        ):
            keep, send = by_core(me, value.reshape(blocks, 2, lines, -1))
            keep_ref[:, :, columns] = keep
            send_ref[:, :, columns] = send.astype(bf16)
    else:
        grad_control_ref[...] = grad_control
        grad_gain_ref[...] = grad_gain
        grad_out_ref[...] = grad_out


def unmix(
    me, part, last, shards, ret_slots, att_slots, inputs, cotangent, w_out, gain, control, before
):
    slot_count, experts = len(att_slots), len(ret_slots)
    rows, positions, width = att_slots[0].shape
    tokens = rows * slot_count
    half = pl.BlockSpec((tokens, positions, width), lambda b, me: (0, part, 0))
    count = 1 + experts + slot_count + 5
    if last:
        kept = (shards // 2, width // shards, width + LANES)
        made = [(None, kept, f32), (None, kept, bf16)]
    else:
        made = [
            (None, (width, width), f32),
            (None, (LANES, width), f32),
            (None, (8, width), f32),
        ]
    result = call(
        functools.partial(unmix_kernel, slot_count, experts, LANES // experts, part, last),
        "unmix",
        (1,),
        [None] * (experts + slot_count)
        + [half, half, fourth(width), None, None]
        + ([pl.BlockSpec(memory_space=pl.ANY)] + [None] * 3 if part else []),
        [(half, cotangent.shape, bf16), (None, (tokens, positions, width), bf16)]
        + [(None, (rows, positions, width), bf16)] * slot_count
        + made,
        [((tokens, LANES // experts, width), f32)] + ([((LANES, width), f32)] if last else []),
        (me, *ret_slots, *att_slots, inputs, cotangent, w_out, gain, control, *before),
        positions * 12 / 256,
        {count: 0} if part else None,
        room=58,
    )
    do_slots = result[2 : 2 + slot_count]
    return do_slots, result[1], [result[0], *result[2 + slot_count :]]


def finish_kernel(slot_count, row_count, parts, *refs):
    me_ref = refs[0]
    gf_refs = refs[1 : 1 + slot_count * row_count]
    rest = refs[1 + slot_count * row_count :]
    inputs_ref, grad_middle_refs, (gain_ref, out_ref) = rest[0], rest[1 : 1 + parts], rest[1 + parts :]
    me = me_ref[0]
    piece = 64
    positions = out_ref.shape[1]
    some = positions // parts
    for start in range(0, positions, piece):
        span = slice(start, start + piece)
        inner = slice(start % some, start % some + piece)
        for j in range(slot_count):
            for row in range(row_count):
                place = (me ^ j) * row_count + row
                normed, scaled = normalize(inputs_ref[place, span].astype(f32))
                incoming = gf_refs[row * slot_count + j][0, span].astype(f32) * gain_ref[...]
                grad = norm_back(incoming, normed, scaled)
                middle = grad_middle_refs[start // some][j * row_count + row, inner]
                out_ref[place, span] = (grad + middle.astype(f32)).astype(bf16)


def finish(me, gf_rows, inputs, grad_middles, gain):
    slot_count, row_count, parts = len(gf_rows[0]), len(gf_rows), len(grad_middles)
    return call(
        functools.partial(finish_kernel, slot_count, row_count, parts),
        "finish",
        (1,),
        [None] * (slot_count * row_count + 2 + parts),
        [(None, inputs.shape, bf16)],
        [],
        (me, *[gf for row in gf_rows for gf in row], inputs, *grad_middles, gain),
        4,
    )[0]


def on_device(
    sizes,
    inputs,
    segments,
    cotangent,
    gain_attn,
    w_qkv,
    w_out,
    gain_mix,
    w_control,
    w_expand,
    w_shrink,
):
    groups, members, slots = sizes
    local_rows, positions, width = inputs.shape
    experts = w_expand.shape[0]
    rows = local_rows // slots
    place = (("gq", groups), ("gi", members), ("seq", slots))
    owners = (("gq", groups), ("seq", slots))
    seq_me = lax.axis_index("seq")
    member = lax.axis_index("gi")
    me = jnp.stack([seq_me, member]).astype(jnp.int32)

    parts = 2 if positions % BLOCK == 0 else 1

    marks = segments.astype(bf16)[:, None, :]
    marks = jnp.pad(marks, ((0, 0), (0, MARKS - 1), (0, width - positions)))

    def row_part(row, j):
        index = (seq_me ^ j) * rows + row
        parts = [lax.dynamic_slice_in_dim(array, index, 1, axis=0) for array in (inputs, marks)]
        return jnp.concatenate(parts, axis=1)

    x_parts = [[row_part(row, j) for j in range(slots)] for row in range(rows)]
    x_rows = [[x_parts[0][0]]]

    def send_some(slots_of, done, first, last):
        for j in range(first, last):
            done.append(partner(slots_of[j], "seq", slots, j))

    small = jnp.concatenate([gain_attn[None], gain_mix[None], w_control], axis=0)
    small = jnp.pad(jnp.transpose(small), ((0, 0), (0, LANES - 2 - experts)))
    packed = jnp.concatenate([w_qkv, w_out, small], axis=1).astype(bf16)
    packed = Doubling(packed, place, ("seq", "gq", "core"))
    packed.steps("seq")
    x_rows, x_parts, w_expand, w_shrink = together((x_rows, x_parts, w_expand, w_shrink), packed)

    def member_parts(array):
        return [
            lax.dynamic_index_in_dim(array, member ^ j, 0, keepdims=False) for j in range(members)
        ]

    send_some(x_parts[0], x_rows[0], 1, slots // 2 + 1)
    weights = member_parts(pack_expert(w_expand.astype(bf16), w_shrink.astype(bf16)))
    weights = swap_slots(weights, "gi")
    packed.steps("gq")
    x_rows, x_parts, weights = together((x_rows, x_parts, weights), packed)
    send_some(x_parts[0], x_rows[0], slots // 2 + 1, slots)
    packed.at_once("gi")
    weights = jnp.stack(natural(weights, member))
    x_rows, x_parts, weights = together((x_rows, x_parts, weights), packed)
    packed.steps("core")
    x_rows, x_parts, weights = together((x_rows, x_parts, weights), packed)
    tail = weights.shape[1] // 2
    halves = [
        Doubling(half, owners, ("gq", "seq"), 1) for half in (weights[:, :tail], weights[:, tail:])
    ]
    halves[0].steps("gq")
    packed = packed.value.reshape(width, -1)

    old = []
    for row in range(rows):
        old = attend_first(me, row, rows, x_rows[row], packed, parts, old)
        if row == 0:
            vectors = old[-1]
            gains = [vectors[0:1], vectors[1:2]]
            control = natural([vectors[2 + e : 3 + e] for e in range(experts)], member)
            control = jnp.concatenate(
                [jnp.broadcast_to(c, (LANES // experts, width)) for c in control], axis=0
            ).astype(bf16)
        if row + 1 < rows:
            x_rows.append(swap_slots(x_parts[row + 1], "seq"))
            old, x_rows[row + 1] = together((old, x_rows[row + 1]), *halves)
        if row == max(0, rows - 2):
            halves[0].steps("seq")
            halves[1].steps("gq")
        if row == rows - 1:
            old, (gain_one, gain_two), control = together((old, gains, control), *halves)
    att, projected, kept = old[:slots], old[slots : slots + 6], old[slots + 6 : slots + 8]
    att_parts, kept = [swap_slots(att, "seq")], [kept]
    for part in range(1, parts):
        att, more = attend_next(me, part, parts, projected, slots)
        more, att_parts[-1] = hold((more, att_parts[-1]))
        att_parts.append(swap_slots(att, "seq"))
        kept.append(more)
    pay_parts = []
    for part in range(parts):
        pay = mix(
            me, part, att_parts[part], inputs, cotangent, packed, gain_two, control, experts
        )
        if part + 1 < parts:
            pay, att_parts[part + 1] = together((pay, att_parts[part + 1]), halves[1])
        if part == 0:
            halves[1].steps("seq")
        if part == parts - 1:
            pay, pay_parts = together((pay, pay_parts), halves[1])
        pay_parts.append(swap_slots(pay, "gi"))
    halves = [half.value.reshape(-1, *half.value.shape[-2:]) for half in halves]
    halves = [(half, partner(half, "seq", slots, 1)) for half in halves]
    ret_parts, earlier = [], []
    for part in range(parts):
        back, more = expert(me, seq_me % 2, part, parts, pay_parts[part], halves, earlier)
        earlier = earlier + list(more)
        if part + 1 < parts:
            pay_parts[part + 1][1], back = hold((pay_parts[part + 1][1], back))
        elif part:
            back, more, ret_parts = hold((back, more, ret_parts))
        ret_parts.append(swap_slots([back] * members, "gi"))

    kept_grad, send = more
    received = partner(send, "seq", slots, 1)
    bits = [2] * len(bits_of((("gq", groups),)))
    bits += [members] + [2] * (len(bits_of((("seq", slots),))) - 1)

    def to_bits(*terms):
        return [term.reshape(*bits, *term.shape[1:]) for term in terms]

    do_parts, grad_middles, before = [], [], []
    for part in range(parts):
        last = part == parts - 1
        if last:
            sum_expert = Halving(to_bits(kept_grad, received), owners, ("seq", "gq"), 1)
            sum_expert.prepare()
            ret_parts[part], before = together((ret_parts[part], before), sum_expert)
        do, grad_middle, before = unmix(
            me,
            part,
            last,
            groups * members * slots,
            ret_parts[part],
            att_parts[part],
            inputs,
            cotangent,
            packed,
            gain_two,
            control,
            before,
        )
        grad_middles.append(grad_middle)
        do_parts.append(swap_slots(do, "seq"))
    output, keep_out, send_out = before
    every_bit = [2] * len(bits_of(place))
    do_parts, send_out = together((do_parts, send_out), sum_expert)
    sum_expert.exchange()
    received_out = partner(send_out, "seq", slots, 1)

    gf_rows, grad_in = [], None
    for row in range(rows):
        gf_slots, grad_in = attend_back(
            me,
            row,
            rows,
            groups * members * slots,
            x_rows[row],
            do_parts,
            gain_one,
            packed,
            projected,
            kept,
            grad_in,
        )
        grad_in = grad_in[0] if row < rows - 1 else grad_in
        if row == 0:
            gf_slots, grad_in, received_out = together((gf_slots, grad_in, received_out), sum_expert)
            sum_expert.combine()
            while sum_expert.order[0][0] == "seq":
                sum_expert.step(sum_expert.order.pop(0))
            sum_expert.prepare()
            gf_slots, grad_in = together((gf_slots, grad_in), sum_expert)
            sum_expert.exchange()
        if row:
            gf_slots, grad_in, gf_rows = together((gf_slots, grad_in, gf_rows), sum_expert)
        if row < rows - 1:
            gf_rows.append(swap_slots(gf_slots, "seq"))
    gf_rows.append([gf_slots[0]])
    send_some(gf_slots, gf_rows[-1], 1, slots // 2 + 1)
    keep, send = grad_in
    received = partner(send, "seq", slots, 1)
    sum_expert.combine()
    sums = sum_expert.finish()
    columns = [p if j == 0 else p.astype(bf16) for j, p in enumerate(member_parts(sums))]
    columns = swap_slots(columns, "gi")
    gf_rows, gf_slots, received, columns = hold((gf_rows, gf_slots, received, columns))
    send_some(gf_slots, gf_rows[-1], slots // 2 + 1, slots)
    total = keep + received.astype(f32)
    total = jnp.concatenate([total, keep_out + received_out.astype(f32)], axis=-1)
    total = total.reshape(*every_bit[1:], *total.shape[1:])
    sum_in = Halving(total, place, ("gi", "gq", "seq"))
    sum_in.cut(("gi",))
    sum_in.send()
    gf_rows = together(gf_rows, sum_in)
    sum_in.combine()
    sum_in.cut(("gq", "seq"))
    gf_rows = together(gf_rows, sum_in)
    sum_in.send()
    grad_inputs = finish(me, gf_rows, inputs, grad_middles, gain_one)
    grad_inputs = together(grad_inputs, sum_in)
    sum_in.combine()
    columns = natural(columns, member)
    columns = jnp.stack([c.astype(f32) for c in columns])
    grad_expand, grad_shrink = unpack_expert(columns, width // (groups * members * slots))
    total = sum_in.finish()
    grad_in, grad_out = total[:, : 3 * width], total[:, 3 * width :]
    small = jnp.transpose(grad_out[:, width:])
    weighted = jnp.sum(grad_in * w_qkv.astype(bf16).astype(f32), axis=1)
    return (
        output,
        grad_inputs,
        weighted / gain_attn.astype(bf16).astype(f32),
        grad_in,
        grad_out[:, :width],
        small[0],
        small[1 : 1 + experts],
        grad_expand,
        grad_shrink,
    )


def solution(mesh):
    dp_count, seq_count = mesh.shape["dp"], mesh.shape["seq"]

    def run(inputs, *args):
        members = GROUP * dp_count // inputs.shape[0]
        sizes = (dp_count // members, members, seq_count)
        fine = Mesh(mesh.devices.reshape(sizes), ("gq", "gi", "seq"))
        dp, both = ("gq", "gi"), ("gq", "gi", "seq")
        return jax.shard_map(
            functools.partial(on_device, sizes),
            mesh=fine,
            in_specs=(
                P(dp, "seq", None),
                P(dp, "seq"),
                P(dp, "seq", None),
                P(both),
                P(both, None),
                P(both, None),
                P(both),
                P(None, both),
                P(None, both, None),
                P(None, both, None),
            ),
            out_specs=(
                P(dp, "seq", None),
                P(dp, "seq", None),
                P(both),
                P(both, None),
                P(both, None),
                P(both),
                P(None, both),
                P(None, both, None),
                P(None, both, None),
            ),
            check_vma=False,
        )(inputs, *args)

    return run
```

```python
import functools
import math

import jax
import jax.numpy as jnp
from jax import lax
from jax.experimental import pallas as pl
from jax.experimental.pallas import tpu as pltpu
from jax.sharding import Mesh
from jax.sharding import PartitionSpec as P

HEADS = 8
GROUP = 32
BLOCK = 256
LANES = 128
MARKS = 16

LOG2E = math.log2(math.e)
LN2 = math.log(2.0)
BIG = 1e30

bf16 = jnp.bfloat16
f32 = jnp.float32

NN = (((1,), (0,)), ((), ()))
NT = (((1,), (1,)), ((), ()))
TN = (((0,), (0,)), ((), ()))


def dot(a, b, dims=NN):
    return lax.dot_general(a, b, dims, preferred_element_type=f32)


def normalize(values):
    center = values - jnp.mean(values, axis=-1, keepdims=True)
    scaled = lax.rsqrt(jnp.mean(center * center, axis=-1, keepdims=True) + 1e-05)
    return center * scaled, scaled


def norm_back(incoming, normed, scaled):
    return scaled * (
        incoming
        - jnp.mean(incoming, axis=-1, keepdims=True)
        - normed * jnp.mean(incoming * normed, axis=-1, keepdims=True)
    )


def split3(value):
    high = value.astype(bf16).astype(f32)
    rest = value - high
    mid = rest.astype(bf16).astype(f32)
    low = (rest - mid).astype(bf16).astype(f32)
    return high, mid, low


def partner(value, axis, size, mask):
    return lax.ppermute(value, axis, [(i, i ^ mask) for i in range(size)])


def swap_slots(slots, axis):
    size = len(slots)
    return [slots[0]] + [partner(slots[j], axis, size, j) for j in range(1, size)]


def natural(slots, me):
    out = list(slots)
    bit = 1
    while bit < len(out):
        flip = (me & bit) != 0
        out = [jnp.where(flip, out[k ^ bit], out[k]) for k in range(len(out))]
        bit *= 2
    return out


def bits_of(sizes):
    bits = []
    for axis, size in sizes:
        mask = size // 2
        while mask:
            bits.append((axis, size, mask))
            mask //= 2
    return bits


def named(bit):
    axis, _, mask = bit
    return "core" if axis == "seq" and mask == 1 else axis


class Steps:
    def __init__(self, value, sizes, order):
        self.order = [bit for axis in order for bit in reversed(bits_of(sizes)) if named(bit) == axis]
        self.value = value

    def steps(self, axis):
        while self.order and named(self.order[0]) == axis:
            self.step(self.order.pop(0))
        return self

    def finish(self):
        while self.order:
            self.step(self.order.pop(0))
        return self.value


class Doubling(Steps):
    def __init__(self, value, sizes, order, inner=0):
        super().__init__(value, sizes, order)
        self.inner = inner
        self.place = bits_of(sizes)
        self.have = []

    def step(self, bit):
        axis, size, mask = bit
        depth = sum(self.place.index(other) < self.place.index(bit) for other in self.have)
        depth += self.inner if axis == "seq" else 0
        other = partner(self.value, axis, size, mask)
        high = (lax.axis_index(axis) & mask) != 0
        first = jnp.where(high, other, self.value)
        second = jnp.where(high, self.value, other)
        self.value = jnp.stack([first, second], axis=depth)
        self.have.append(bit)

    def at_once(self, axis):
        bits = [bit for bit in self.place if bit[0] == axis]
        self.order = [bit for bit in self.order if bit[0] != axis]
        depth = sum(self.place.index(other) < self.place.index(bits[0]) for other in self.have)
        depth += self.inner if axis == "seq" else 0
        slots = natural(swap_slots([self.value] * 2 ** len(bits), axis), lax.axis_index(axis))
        shape = self.value.shape
        value = jnp.stack(slots, axis=depth)
        self.value = value.reshape(shape[:depth] + (2,) * len(bits) + shape[depth:])
        self.have += bits


def total_of(terms):
    return functools.reduce(jnp.add, [term.astype(f32) for term in terms])


class Halving(Steps):
    def __init__(self, value, sizes, order, inner=0):
        super().__init__(None, sizes, order)
        self.terms = value if isinstance(value, list) else [value]
        self.sizes = sizes
        self.left = [bit for bit in bits_of(sizes) if bit in self.order]
        self.inner = inner

    def prepare(self):
        bit = self.order.pop(0)
        depth = self.left.index(bit)
        self.left.pop(depth)
        axis, size, mask = bit
        depth += self.inner if axis == "seq" else 0
        high = ((lax.axis_index(axis) & mask) != 0).astype(jnp.int32)
        keep, send = [
            [lax.dynamic_index_in_dim(term, at, depth, keepdims=False) for term in self.terms]
            for at in (high, 1 - high)
        ]
        self.terms = keep
        self.value = total_of(send).astype(bf16)
        self.link = bit

    def exchange(self):
        axis, size, mask = self.link
        self.value = partner(self.value, axis, size, mask)

    def combine(self):
        if isinstance(self.value, list):
            self.terms = self.value
        else:
            self.terms = self.terms + [self.value]
        self.value = None

    def finish(self):
        super().finish()
        return total_of(self.terms)

    def step(self, bit):
        self.order.insert(0, bit)
        self.prepare()
        self.exchange()
        self.combine()

    def cut(self, axes):
        bits = [bit for bit in self.left if bit[0] in axes]
        self.order = [bit for bit in self.order if bit not in bits]
        depth = self.left.index(bits[0])
        if self.inner or bits != self.left[depth : depth + len(bits)]:
            raise NotImplementedError
        self.left = [bit for bit in self.left if bit not in bits]
        value = total_of(self.terms)
        shape = value.shape
        value = value.reshape(shape[:depth] + (2 ** len(bits),) + shape[depth + len(bits) :])
        place = 0
        for axis, size, mask in bits:
            place = 2 * place + ((lax.axis_index(axis) & mask) != 0).astype(jnp.int32)
        parts = [
            lax.dynamic_index_in_dim(value, place ^ j, depth, keepdims=False)
            for j in range(2 ** len(bits))
        ]
        self.value = [parts[0]] + [part.astype(bf16) for part in parts[1:]]
        self.link = bits

    def send(self):
        bits = self.link
        sizes = [(axis, size) for axis, size in self.sizes if axis in [bit[0] for bit in bits]]
        names = tuple(axis for axis, _ in sizes)
        for j in range(1, 2 ** len(bits)):
            masks = {axis: 0 for axis in names}
            for i, (axis, _, mask) in enumerate(bits):
                if j >> (len(bits) - 1 - i) & 1:
                    masks[axis] |= mask
            pairs = []
            for source in range(math.prod(size for _, size in sizes)):
                target, rest, unit = 0, source, 1
                for axis, size in reversed(sizes):
                    target += ((rest % size) ^ masks[axis]) * unit
                    rest, unit = rest // size, unit * size
                pairs.append((source, target))
            self.value[j] = lax.ppermute(self.value[j], names, pairs)


hold = lax.optimization_barrier


def together(values, *sums):
    values, held = lax.optimization_barrier((values, [item.value for item in sums]))
    for item, value in zip(sums, held):
        item.value = value
    return values


def call(kernel, name, grid, in_specs, outs, scratch, args, micros, aliases=None, room=10):
    def full(shape):
        return pl.BlockSpec(shape, lambda *_: (0,) * len(shape))

    in_specs = [spec or full(arg.shape) for spec, arg in zip(in_specs, args[1:], strict=True)]
    outs = [(spec or full(shape), shape, dtype) for spec, shape, dtype in outs]
    return pl.pallas_call(
        kernel,
        grid_spec=pltpu.PrefetchScalarGridSpec(
            num_scalar_prefetch=1,
            grid=grid,
            in_specs=in_specs,
            out_specs=[spec for spec, _, _ in outs],
            scratch_shapes=[pltpu.VMEM(shape, dtype) for shape, dtype in scratch],
        ),
        out_shape=[jax.ShapeDtypeStruct(shape, dtype) for _, shape, dtype in outs],
        input_output_aliases=aliases or {},
        compiler_params=pltpu.CompilerParams(vmem_limit_bytes=room << 20),
        cost_estimate=pl.CostEstimate(
            flops=int(micros * 1e9), bytes_accessed=1 << 20, transcendentals=0
        ),
        name=name,
    )(*args)


def per_row(*shape):
    return pl.BlockSpec((1,) + shape, lambda r, me: (r,) + (0,) * len(shape))


def whole(*shape):
    return pl.BlockSpec(shape, lambda r, me: (0,) * len(shape))


def fourth(width):
    return pl.BlockSpec((width, width), lambda b, me: (0, 3))


def by_core(me, pairs):
    odd = me % 2 == 1
    first, second = pairs[:, 0], pairs[:, 1]
    return jnp.where(odd, second, first), jnp.where(odd, first, second)


def causal_bias(step=LANES):
    rows = LANES + step * (BLOCK // LANES - 1)
    key = lax.broadcasted_iota(jnp.int32, (rows, BLOCK), 0)
    query = lax.broadcasted_iota(jnp.int32, (rows, BLOCK), 1)
    query = query + (query // LANES) * (step - LANES)
    return jnp.where(key <= query, 0.0, -BIG).astype(f32)


def key_features(segment_row, length):
    row = lax.broadcasted_iota(jnp.int32, (LANES, length), 0)
    marks = (row == segment_row) | ((row >= 7) & (row < 10))
    return jnp.where(marks, 1.0, 0.0).astype(f32).T.astype(bf16)


def query_features(segment_row, length):
    row = lax.broadcasted_iota(jnp.int32, (16, length), 0)
    return jnp.where((row < 7) & (row != segment_row), -BIG, 0.0).astype(f32)


def padded_head(head, features, odd):
    blank = jnp.zeros_like(head)
    rest = jnp.zeros((LANES - 16, head.shape[1]), bf16)
    both = [blank, head] if odd else [head, blank]
    return jnp.concatenate(both + [features, rest], axis=0)


def attend_queries(part, parts, slots, me, seg_ref, q_t, k_ref, v_t, att_refs, ot_ref, lse_ref, aux):
    k_aux, q_aux, causal = aux
    length = k_ref.shape[1]
    piece = length // slots
    some = piece // parts
    step = piece if parts > 1 else LANES
    segment_row = seg_ref[0]
    q_aux[...] = query_features(segment_row, length)
    k_aux[...] = key_features(segment_row, length)
    blocks = slots * some // BLOCK
    count = BLOCK // some if parts > 1 else 1

    def head_pair(pair, carry):
        base = pl.multiple_of(pair * LANES, LANES)
        for odd in range(2):
            rows = pl.ds(pl.multiple_of(pair * LANES + odd * 64, 64), 64)
            for block in range(blocks):
                if parts > 1:
                    first = block * count * piece + part * some
                    places = [pl.ds(first + i * piece, some) for i in range(count)]
                else:
                    first = block * BLOCK
                    places = [pl.ds(first, BLOCK)]
                feats = jnp.concatenate([q_aux[:, p] for p in places], axis=1).astype(bf16)
                head = jnp.concatenate([q_t[0, rows, p] for p in places], axis=1)
                query = padded_head(head, feats, odd)
                chunks = [(k, min(BLOCK, first - k)) for k in range(0, first, BLOCK)]
                chunks.append((first, causal.shape[0]))
                scores = []
                for start, size in chunks:
                    keys = pl.ds(start, size)
                    key = jnp.concatenate([k_ref[0, keys, pl.ds(base, LANES)], k_aux[keys]], axis=1)
                    score = dot(key, query)
                    scores.append(score + causal[...] if start == first else score)
                top = functools.reduce(
                    jnp.maximum, [jnp.max(score, axis=0, keepdims=True) for score in scores]
                )
                total = jnp.zeros((1, BLOCK), f32)
                out = jnp.zeros((64, BLOCK), f32)
                for (start, size), score in zip(chunks, scores):
                    prob = jnp.exp2(score - top)
                    total = total + jnp.sum(prob, axis=0, keepdims=True)
                    out = out + dot(v_t[0, rows, pl.ds(start, size)], prob.astype(bf16))
                held = pl.ds(block * BLOCK, BLOCK)
                ot_ref[0, rows, held] = (out / total).astype(bf16)
                lse_ref[0, pl.ds(pair * 2 + odd, 1), held] = top + jnp.log2(total)
        return carry

    lax.fori_loop(0, HEADS // 2, head_pair, 0)
    for j in range(slots):
        place = pl.ds(pl.multiple_of((me ^ j) * some, some), some)
        att_refs[j][0] = ot_ref[0, :, place].T


def attend_first_kernel(parts, slots, old, *refs):
    me_ref = refs[0]
    x_refs = refs[1 : 1 + slots]
    vector_ref, w_ref = refs[1 + slots : 3 + slots]
    rest = refs[3 + slots + old :]
    att_refs = rest[:slots]
    seg_ref, qt_ref, k_ref, v_ref, q_ref, vt_ref, ot_ref, lse_ref, rows_ref = rest[slots : slots + 9]
    w_t, *aux = rest[slots + 9 :]
    width = w_ref.shape[0]
    piece = x_refs[0].shape[1] - MARKS
    me = me_ref[0]
    score_scale = LOG2E / math.sqrt(width // HEADS)

    w_t[:width] = w_ref[:, :width].T
    w_t[width:] = w_ref[:, 2 * width :].T
    aux[2][...] = causal_bias(piece if parts > 1 else LANES)
    rows_ref[...] = vector_ref[...].astype(f32).T
    gain = rows_ref[0:1]
    for j in range(slots):
        place = pl.ds(pl.multiple_of((me ^ j) * piece, piece), piece)
        marks = x_refs[j][0, piece:].astype(f32)
        seg_ref[0, :, place] = marks[0:1, :piece].astype(jnp.int32)
        normed, _ = normalize(x_refs[j][0, :piece].astype(f32))
        first_in = (normed * gain).astype(bf16)
        projected = dot(first_in, w_ref[...])
        q_ref[0, place] = (projected[:, :width] * score_scale).astype(bf16)
        k_ref[0, place] = projected[:, width : 2 * width].astype(bf16)
        v_ref[0, place] = projected[:, 2 * width :].astype(bf16)
        turned = dot(w_t[...], first_in, NT)
        qt_ref[0, :, place] = (turned[:width] * score_scale).astype(bf16)
        vt_ref[0, :, place] = turned[width:].astype(bf16)
    attend_queries(
        0, parts, slots, me, seg_ref, qt_ref, k_ref, vt_ref, att_refs, ot_ref, lse_ref, aux
    )


def attend_next_kernel(part, parts, slots, *refs):
    me_ref, seg_ref, qt_ref, k_ref, vt_ref = refs[:5]
    att_refs = refs[5 : 5 + slots]
    ot_ref, lse_ref, *aux = refs[5 + slots :]

    @pl.when(pl.program_id(0) == 0)
    def _():
        aux[2][...] = causal_bias(k_ref.shape[1] // slots if parts > 1 else LANES)

    attend_queries(
        part, parts, slots, me_ref[0], seg_ref, qt_ref, k_ref, vt_ref, att_refs, ot_ref, lse_ref, aux
    )


def attend_outs(rows, slots, some, width):
    return [(per_row(some, width), (rows, some, width), bf16)] * slots, [
        (per_row(width, slots * some), (rows, width, slots * some), bf16),
        (per_row(HEADS, slots * some), (rows, HEADS, slots * some), f32),
    ]


def attend_scratch(length, piece, parts):
    span = LANES + (piece if parts > 1 else LANES) * (BLOCK // LANES - 1)
    return [((length, LANES), bf16), ((16, length), f32), ((span, BLOCK), f32)]


def attend_first(me, row, rows, x_slots, weights, parts, old):
    slots = len(x_slots)
    _, packed, width = x_slots[0].shape
    piece = packed - MARKS
    length = piece * slots

    def this(*shape):
        return pl.BlockSpec((1,) + shape, lambda r, me: (row,) + (0,) * len(shape))

    some = piece // parts
    turned = (this(width, length), (rows, width, length), bf16)
    plain = (this(length, width), (rows, length, width), bf16)
    outs = (
        [(this(some, width), (rows, some, width), bf16)] * slots
        + [(this(1, length), (rows, 1, length), jnp.int32)]
        + [turned, plain, plain, plain, turned]
        + [
            (this(width, slots * some), (rows, width, slots * some), bf16),
            (this(HEADS, slots * some), (rows, HEADS, slots * some), f32),
            (whole(LANES, width), (LANES, width), f32),
        ]
    )
    result = call(
        functools.partial(attend_first_kernel, parts, slots, len(old)),
        "attend_first",
        (1,),
        [per_row(packed, width)] * slots
        + [
            pl.BlockSpec((width, LANES), lambda r, me: (0, 4 * width // LANES)),
            whole(width, 3 * width),
        ]
        + [pl.BlockSpec(memory_space=pl.ANY)] * len(old),
        outs,
        [((2 * width, width), bf16)] + attend_scratch(length, piece, parts),
        (me, *x_slots, weights, weights, *old),
        12,
        {3 + slots + i: i for i in range(len(old))},
        room=26,
    )
    return result


def attend_next(me, part, parts, projected, slots):
    segment_rows, q_t, k, _, _, v_t = projected
    rows, length, width = k.shape
    piece = length // slots
    att, more = attend_outs(rows, slots, piece // parts, width)
    result = call(
        functools.partial(attend_next_kernel, part, parts, slots),
        "attend_next",
        (rows,),
        [
            per_row(1, length),
            per_row(width, length),
            per_row(length, width),
            per_row(width, length),
        ],
        att + more,
        attend_scratch(length, piece, parts),
        (me, segment_rows, q_t, k, v_t),
        28 / parts,
        room=16,
    )
    return result[:slots], result[slots:]


def attend_back_kernel(row, last, parts, slot_count, *refs):
    me_ref = refs[0]
    x_refs = refs[1 : 1 + slot_count]
    rest = refs[1 + slot_count :]
    do_refs, rest = rest[: parts * slot_count], rest[parts * slot_count :]
    seg_ref, gain_ref, w_ref, qt_ref, k_ref, v_ref, q_ref = rest[:7]
    ot_refs, lse_refs = rest[7 : 7 + parts], rest[7 + parts : 7 + 2 * parts]
    rest = rest[7 + 2 * parts :]
    if row:
        before_ref, rest = rest[0], rest[1:]
    gf_refs, rest = rest[:slot_count], rest[slot_count:]
    dw_refs, rest = rest[: 1 + last], rest[1 + last :]
    (
        k_aux, q_aux, v_aux, causal, do, first_t, work_t, k_t, grads, prob, grad_score, delta, lse
    ) = rest
    width = w_ref.shape[0]
    piece = x_refs[0].shape[1] - MARKS
    some = piece // parts
    length = piece * slot_count
    me = me_ref[0]
    score_scale = 1.0 / math.sqrt(width // HEADS)
    causal[...] = causal_bias()
    lane = lax.broadcasted_iota(jnp.int32, (length, LANES), 1)
    v_aux[...] = jnp.where(lane < 3, 1.0, 0.0).astype(bf16)
    for part in range(parts):
        for i in range(slot_count):
            held = pl.ds(i * some, some)
            lse[:, pl.ds(i * piece + part * some, some)] = lse_refs[part][0, :, held]

    segment_row = seg_ref[0]
    q_aux[...] = query_features(segment_row, length)
    k_aux[...] = key_features(segment_row, length)
    gain = gain_ref[...]
    for j in range(slot_count):
        place = pl.ds(pl.multiple_of((me ^ j) * piece, piece), piece)
        normed, _ = normalize(x_refs[j][0, :piece].astype(f32))
        first_t[:, place] = (normed * gain).astype(bf16).T
        k_t[:, place] = k_ref[0, place].T
        for part in range(parts):
            start = (me ^ j) * piece + part * some
            place = pl.ds(pl.multiple_of(start, some), some)
            held = pl.ds(pl.multiple_of((me ^ j) * some, some), some)
            grad = do_refs[part * slot_count + j][0]
            do[place] = grad
            turned = grad.T
            work_t[:, place] = turned
            product = turned.astype(f32) * ot_refs[part][0, :, held].astype(f32)
            delta[:, place] = jnp.sum(product.reshape(HEADS, width // HEADS, some), axis=1)
    lane = lax.broadcasted_iota(jnp.int32, (1, LANES), 1)
    feature = lax.broadcasted_iota(jnp.int32, (16, BLOCK), 0)
    blocks = length // BLOCK

    def head_pair(pair, carry):
        base = pl.multiple_of(pair * LANES, LANES)
        for odd in range(2):
            rows = pl.ds(pl.multiple_of(pair * LANES + odd * 64, 64), 64)
            head = pl.ds(pair * 2 + odd, 1)
            for qb in range(blocks):
                queries = pl.ds(qb * BLOCK, BLOCK)
                a, b, c = split3(lse[head, queries])
                feats = jnp.where(feature == 7, -a, q_aux[:, queries])
                feats = jnp.where(feature == 8, -b, jnp.where(feature == 9, -c, feats))
                query = padded_head(qt_ref[0, rows, queries], feats.astype(bf16), odd)
                a, b, c = split3(delta[head, queries])
                feats = jnp.where(feature == 0, -a, jnp.where(feature == 1, -b, 0.0))
                feats = jnp.where(feature == 2, -c, feats)
                grad = padded_head(work_t[rows, queries], feats.astype(bf16), odd)
                held = pl.ds(odd * length + qb * BLOCK, BLOCK)
                for kb in range(qb + 1):
                    keys = pl.ds(kb * BLOCK, BLOCK)
                    key = jnp.concatenate([k_ref[0, keys, pl.ds(base, LANES)], k_aux[keys]], axis=1)
                    score = dot(key, query)
                    if kb == qb:
                        score = score + causal[...]
                    value = jnp.concatenate(
                        [v_ref[0, keys, pl.ds(base, LANES)], v_aux[keys]], axis=1
                    )
                    grad_prob = dot(value, grad)
                    weight = jnp.exp2(score)
                    prob[keys, held] = weight.astype(bf16)
                    grad_score[keys, held] = (weight * grad_prob).astype(bf16)
                end = (qb + 1) * BLOCK
                grad_q = dot(k_t[rows, 0:end], grad_score[0:end, held])
                work_t[rows, queries] = (grad_q * score_scale).astype(bf16)
        for kb in range(blocks):
            keys = pl.ds(kb * BLOCK, BLOCK)
            later = pl.ds(kb * BLOCK, length - kb * BLOCK)
            grad_v = jnp.zeros((BLOCK, LANES), f32)
            grad_k = jnp.zeros((BLOCK, LANES), f32)
            for odd in range(2):
                mine = (lane >= 64) if odd else (lane < 64)
                held = pl.ds(odd * length + kb * BLOCK, length - kb * BLOCK)
                zero = jnp.zeros((), bf16)
                grad = jnp.where(mine, do[later, pl.ds(base, LANES)], zero)
                query = jnp.where(mine, q_ref[0, later, pl.ds(base, LANES)], zero)
                grad_v = grad_v + dot(prob[keys, held], grad)
                grad_k = grad_k + dot(grad_score[keys, held], query)
            grads[keys, pl.ds(pl.multiple_of(width + pair * LANES, LANES), LANES)] = (
                grad_k * LN2
            ).astype(bf16)
            grads[keys, pl.ds(pl.multiple_of(2 * width + pair * LANES, LANES), LANES)] = (
                grad_v.astype(bf16)
            )
        return carry

    lax.fori_loop(0, HEADS // 2, head_pair, 0)
    for j in range(slot_count):
        place = pl.ds(pl.multiple_of((me ^ j) * piece, piece), piece)
        grads[place, :width] = work_t[:, place].T
        gf_refs[j][0] = dot(grads[place], w_ref[...], NT).astype(bf16)
    update = dot(first_t[...], grads[...])
    if row:
        update = before_ref[...] + update
    if last:
        keep, send = by_core(me, update.reshape(-1, 2, *dw_refs[0].shape[1:]))
        dw_refs[0][...] = keep
        dw_refs[1][...] = send.astype(bf16)
    else:
        dw_refs[0][...] = update


def attend_back(me, row, rows, shards, x_slots, do_parts, gain, w_qkv, projected, kept, before):
    slot_count, parts = len(x_slots), len(do_parts)
    _, packed, width = x_slots[0].shape
    piece = packed - MARKS
    length = piece * slot_count
    some = piece // parts
    last = row == rows - 1

    def this(*shape):
        return pl.BlockSpec((1,) + shape, lambda r, me: (row,) + (0,) * len(shape))

    half = (shards // 2, width // shards, 3 * width)
    outs = [(per_row(piece, width), (1, piece, width), bf16)] * slot_count
    if last:
        outs += [(whole(*half), half, f32), (whole(*half), half, bf16)]
    else:
        outs += [(whole(width, 3 * width), (width, 3 * width), f32)]
    segment_rows, q_t, k, v, q, _ = projected
    result = call(
        functools.partial(attend_back_kernel, row, last, parts, slot_count),
        "attend_back",
        (1,),
        [per_row(packed, width)] * slot_count
        + [this(some, width)] * (parts * slot_count)
        + [this(1, length), whole(1, width), whole(width, 3 * width)]
        + [this(width, length)]
        + [this(length, width)] * 3
        + [this(width, some * slot_count)] * parts
        + [this(HEADS, some * slot_count)] * parts
        + ([whole(width, 3 * width)] if row else []),
        outs,
        [
            ((length, LANES), bf16),
            ((16, length), f32),
            ((length, LANES), bf16),
            ((BLOCK, BLOCK), f32),
            ((length, width), bf16),
            ((width, length), bf16),
            ((width, length), bf16),
            ((width, length), bf16),
            ((length, 3 * width), bf16),
            ((length, 2 * length), bf16),
            ((length, 2 * length), bf16),
            ((HEADS, length), f32),
            ((HEADS, length), f32),
        ],
        (
            me,
            *x_slots,
            *[do for part in do_parts for do in part],
            segment_rows,
            gain,
            w_qkv,
            q_t,
            k,
            v,
            q,
            *[o for o, _ in kept],
            *[l for _, l in kept],
            *([before] if row else []),
        ),
        28,
        room=60,
    )
    return result[:slot_count], result[slot_count:]


def tokens_of(refs, span):
    return jnp.concatenate([ref[:, span] for ref in refs], axis=0).reshape(-1, refs[0].shape[-1])


def rows_of(ref, me, rows, slot_count, span):
    parts = [ref[pl.ds((me ^ j) * rows, rows), span] for j in range(slot_count)]
    return jnp.concatenate(parts, axis=0).reshape(-1, ref.shape[-1])


def diagonal(piece):
    place = lax.broadcasted_iota(jnp.int32, (piece, LANES), 0)
    lane = lax.broadcasted_iota(jnp.int32, (piece, LANES), 1)
    return place == lane % piece, lane // piece, lane


def mix_kernel(slot_count, experts, piece, *refs):
    me_ref = refs[0]
    att_refs = refs[1 : 1 + slot_count]
    inputs_ref, cot_ref, w_out_ref, gain_ref, control_ref = refs[1 + slot_count : 6 + slot_count]
    pay_refs = refs[6 + slot_count :]
    rows, positions, width = att_refs[0].shape
    tokens = rows * slot_count
    me = me_ref[0]
    own, _, lane = diagonal(piece)
    w_out = w_out_ref[...]
    for sub in range(positions // piece):
        span = slice(sub * piece, (sub + 1) * piece)
        added = dot(tokens_of(att_refs, span), w_out)
        second = []
        for token in range(tokens):
            row = (me ^ (token // rows)) * rows + token % rows
            middle = inputs_ref[row, span].astype(f32) + added[token * piece : (token + 1) * piece]
            normed, _ = normalize(middle)
            second.append((normed * gain_ref[...]).astype(bf16))
        second = jnp.concatenate(second, axis=0)
        grad = rows_of(cot_ref, me, rows, slot_count, span)
        logits = dot(second, control_ref[...], NT).reshape(tokens, piece, LANES)
        top = jnp.max(logits, axis=0)
        weights = jnp.exp(logits - top)
        total = jnp.sum(weights, axis=0)
        log_total = top + jnp.log(total)
        weights = jnp.where(own, weights * (1.0 / total), 0.0)
        spread_out = weights.reshape(-1, LANES).astype(bf16)
        mixed = dot(spread_out, second, TN).astype(bf16)
        grad_results = dot(spread_out, grad, TN).astype(bf16)
        a, b, c = split3(log_total)
        for e in range(experts):
            mine = slice(e * piece, (e + 1) * piece)
            first = slice(e * piece, e * piece + 1)
            stats = jnp.where(lane == 0, a[:, first], jnp.where(lane == 1, b[:, first], c[:, first]))
            pay_refs[e][span, :width] = mixed[mine]
            pay_refs[e][span, width : 2 * width] = grad_results[mine]
            pay_refs[e][span, 2 * width :] = stats.astype(bf16)


def mix(me, part, att_slots, inputs, cotangent, w_out, gain, control, experts):
    slot_count = len(att_slots)
    rows, positions, width = att_slots[0].shape
    tokens = rows * slot_count
    half = pl.BlockSpec((tokens, positions, width), lambda b, me: (0, part, 0))
    pay = (None, (positions, 2 * width + LANES), bf16)
    return call(
        functools.partial(mix_kernel, slot_count, experts, LANES // experts),
        "mix",
        (1,),
        [None] * slot_count + [half, half, fourth(width), None, None],
        [pay] * experts,
        [],
        (me, *att_slots, inputs, cotangent, w_out, gain, control),
        positions * 8 / 256,
    )


def expert_kernel(part, parts, tiled, slot_count, *refs):
    me_ref = refs[0]
    pay_refs = refs[1 : 1 + slot_count]
    rest = refs[1 + slot_count :]
    count = 4 if tiled else 2
    weight_refs, rest = rest[:count], rest[count:]
    expand_ref = weight_refs[0]
    last = part == parts - 1
    earlier, rest = rest[: 4 * part], rest[4 * part :]
    if last:
        back_ref, keep_ref, send_ref = rest[:3]
        mixed_acc, grad_acc, result_acc, back_acc, stat, *more, mixed_low, grad_low = rest[3:]
    else:
        back_ref, mixed_low, grad_low, hidden_ref, pre_ref = rest[:5]
        mixed_acc, grad_acc, result_acc, back_acc, stat, *more = rest[5:]
    me = me_ref[0]
    width = expand_ref.shape[-1]
    step = pl.program_id(0)

    @pl.when(step == 0)
    def _():
        logs = []
        for j in range(slot_count):
            stats = pay_refs[j][:, 2 * width :].astype(f32)
            logs.append(stats[:, 0:1] + stats[:, 1:2] + stats[:, 2:3])
        top = functools.reduce(jnp.maximum, logs)
        total = functools.reduce(jnp.add, [jnp.exp(log - top) for log in logs])
        log_total = top + jnp.log(total)
        mixed, grad = 0.0, 0.0
        for j in range(slot_count):
            share = jnp.exp(logs[j] - log_total)
            mixed = mixed + share * pay_refs[j][:, :width].astype(f32)
            grad = grad + share * pay_refs[j][:, width : 2 * width].astype(f32)
        mixed_acc[...] = mixed
        grad_acc[...] = grad
        mixed_low[...] = mixed.astype(bf16)
        grad_low[...] = grad.astype(bf16)
        result_acc[...] = jnp.zeros_like(result_acc)
        back_acc[...] = jnp.zeros_like(back_acc)
        stat[...] = jnp.broadcast_to(log_total, stat.shape)

    mixed, grad = mixed_low[...], grad_low[...]
    if tiled:
        for i in range(2):
            own, other = weight_refs[2 * i][...], weight_refs[2 * i + 1][...]
            odd = me % 2 == 1
            more[i][:, 0] = jnp.where(odd, other, own)
            more[i][:, 1] = jnp.where(odd, own, other)
        expand, shrink = [ref[...].reshape(-1, width) for ref in more]
    else:
        expand, shrink = [ref[...].reshape(-1, width) for ref in weight_refs]
    value = dot(mixed, expand)
    coeff = math.sqrt(2.0 / math.pi)
    square = value * value
    turn = jnp.tanh(coeff * (value + 0.044715 * (square * value)))
    half = 0.5 * (1.0 + turn)
    hidden = (value * half).astype(bf16)
    slope = half + (0.5 * coeff) * value * (1.0 - turn * turn) * (1.0 + (3 * 0.044715) * square)
    result_acc[...] += dot(hidden, shrink)
    grad_pre = (dot(grad, shrink, NT) * slope).astype(bf16)
    back_acc[...] += dot(grad_pre, expand, NT)
    if last:
        sets = [earlier[4 * i : 4 * i + 4] for i in range(part)]
        mixed = jnp.concatenate([m[...] for m, _, _, _ in sets] + [mixed], axis=0)
        grad = jnp.concatenate([g[...] for _, g, _, _ in sets] + [grad], axis=0)
        hidden = jnp.concatenate([h[...] for _, _, h, _ in sets] + [hidden], axis=0)
        grad_pre = jnp.concatenate([p[...] for _, _, _, p in sets] + [grad_pre], axis=0)
        grad_expand = dot(mixed, grad_pre, TN).astype(bf16)
        grad_shrink = dot(hidden, grad, TN).astype(bf16)
        if tiled:
            shards = 2 * keep_ref.shape[0]
            lines = width // shards
            both = keep_ref.shape[1]
            keep, send = by_core(me, grad_expand.reshape(shards // 2, 2, lines, width))
            place = pl.ds(pl.multiple_of(step * lines, lines), lines)
            keep_ref[:, place] = keep
            send_ref[:, place] = send
            count = 2 * width // both // 2
            keep, send = by_core(me, grad_shrink.reshape(count, 2, both // 2, width))
            place = pl.ds(step * count, count)
            keep_ref[place, both // 2 :] = keep
            send_ref[place, both // 2 :] = send
        else:
            keep_ref[...] = grad_expand.reshape(keep_ref.shape)
            send_ref[...] = grad_shrink.reshape(send_ref.shape)
    else:
        hidden_ref[...] = hidden
        pre_ref[...] = grad_pre

    @pl.when(step == pl.num_programs(0) - 1)
    def _():
        results = result_acc[...].astype(bf16)
        back = back_acc[...].astype(bf16)
        back_ref[:, :width] = results
        back_ref[:, width : 2 * width] = back
        inner = jnp.sum(
            results.astype(f32) * grad_acc[...] + back.astype(f32) * mixed_acc[...],
            axis=-1,
            keepdims=True,
        )
        lane = lax.broadcasted_iota(jnp.int32, stat.shape, 1)
        a, b, c = split3(stat[...])
        d, e, f = split3(inner)
        stats = jnp.where(lane == 0, a, jnp.where(lane == 1, b, c))
        stats = jnp.where(lane < 3, stats, jnp.where(lane == 3, d, jnp.where(lane == 4, e, f)))
        back_ref[:, 2 * width :] = stats.astype(bf16)


def pack_expert(expand, shrink):
    experts, lines, hidden = expand.shape
    width = shrink.shape[-1]
    expand = expand.reshape(experts, lines, hidden // width, width)
    expand = jnp.swapaxes(expand, 1, 2).reshape(experts, -1, width)
    return jnp.concatenate([expand, shrink], axis=1)


def unpack_expert(packed, lines):
    experts, both, width = packed.shape
    expand = packed[:, : both // 2].reshape(experts, -1, lines, width)
    expand = jnp.swapaxes(expand, 1, 2).reshape(experts, lines, -1)
    return expand, packed[:, both // 2 :]


def expert(me, core, part, parts, pay_slots, halves, earlier):
    slot_count = len(pay_slots)
    groups, packed = pay_slots[0].shape
    shards = 2 * halves[0][0].shape[0]
    tail, width = halves[0][0].shape[1:]
    hidden = shards * tail
    chunks = hidden // width
    lines = width // shards
    acc = ((groups, width), f32)
    low = ((groups, width), bf16)
    tiled = lines % 16 == 0
    group = shards // chunks // 2
    if tiled:
        columns = pl.BlockSpec((shards // 2, lines, width), lambda f, me: (0, f, 0))
        lower = pl.BlockSpec((group, tail, width), lambda f, me: (f, 0, 0))
        weights = [*halves[0], *halves[1]]
        specs = [columns, columns, lower, lower]
        built = [((shards // 2, 2, lines, width), bf16), ((group, 2, tail, width), bf16)]
        both = (shards // 2, 2 * tail, width)
        grads = [(whole(*both), both, bf16)] * 2
    else:
        odd = core == 1
        weights = [
            jnp.stack([jnp.where(odd, b, a), jnp.where(odd, a, b)], axis=1) for a, b in halves
        ]
        expand = weights[0].reshape(shards, chunks, lines, width)
        expand = jnp.swapaxes(expand, 0, 1).reshape(chunks, width, width)
        weights = [expand, weights[1].reshape(chunks, width, width)]
        specs = [pl.BlockSpec((1, width, width), lambda f, me: (f, 0, 0))] * 2
        built = []
        grads = [(specs[0], (chunks, width, width), bf16)] * 2
    token = whole(groups, width)
    inner = pl.BlockSpec((groups, width), lambda f, me: (0, f))
    last = part == parts - 1
    outs = [(whole(groups, packed), (groups, packed), bf16)]
    scratch = [acc, acc, acc, acc, ((groups, LANES), f32)] + built
    if last:
        outs += grads
        scratch += [low, low]
    else:
        outs += [(token, (groups, width), bf16)] * 2 + [(inner, (groups, hidden), bf16)] * 2
    result = call(
        functools.partial(expert_kernel, part, parts, tiled, slot_count),
        "expert",
        (chunks,),
        [whole(groups, packed)] * slot_count + specs + [token, token, inner, inner] * part,
        outs,
        scratch,
        (me, *pay_slots, *weights, *earlier),
        7,
        room=18,
    )
    more = list(result[1:])
    if last and not tiled:
        grad = jnp.swapaxes(more[0].reshape(chunks, shards, lines, width), 0, 1)
        more = [grad.reshape(shards, tail, width), more[1].reshape(shards, tail, width)]
        more = jnp.concatenate(more, axis=1).reshape(shards // 2, 2, 2 * tail, width)
        odd = core == 1
        more = [
            jnp.where(odd, more[:, 1], more[:, 0]),
            jnp.where(odd, more[:, 0], more[:, 1]),
        ]
    return result[0], more


def unmix_kernel(slot_count, experts, piece, part, last, *refs):
    me_ref = refs[0]
    ret_refs = refs[1 : 1 + experts]
    att_refs = refs[1 + experts : 1 + experts + slot_count]
    rest = refs[1 + experts + slot_count :]
    inputs_ref, cot_ref, w_out_ref, gain_ref, control_ref = rest[:5]
    rest = rest[5:]
    if part:
        old_out_ref, old_control_ref, old_gain_ref = rest[1:4]
        rest = rest[4:]
    out_ref, grad_middle_ref = rest[:2]
    back_refs = rest[2 : 2 + slot_count]
    rest = rest[2 + slot_count :]
    if last:
        keep_ref, send_ref, middle_scratch, small = rest
    else:
        grad_out_ref, grad_control_ref, grad_gain_ref, middle_scratch = rest
    rows, positions, width = att_refs[0].shape
    tokens = rows * slot_count
    me = me_ref[0]

    own, group, _ = diagonal(piece)
    control = control_ref[...]
    w_out = w_out_ref[...]
    grad_out, grad_control, grad_gain = 0.0, 0.0, 0.0
    if part:
        grad_out, grad_control = old_out_ref[...], old_control_ref[...]
        grad_gain = old_gain_ref[...]
    for sub in range(positions // piece):
        span = slice(sub * piece, (sub + 1) * piece)
        attended = tokens_of(att_refs, span)
        added = dot(attended, w_out)
        second = []
        for token in range(tokens):
            row = (me ^ (token // rows)) * rows + token % rows
            middle = inputs_ref[row, span].astype(f32) + added[token * piece : (token + 1) * piece]
            middle_scratch[token] = middle
            normed, _ = normalize(middle)
            second.append((normed * gain_ref[...]).astype(bf16))
        second = jnp.concatenate(second, axis=0)
        cot = rows_of(cot_ref, me, rows, slot_count, span)
        log_total = jnp.zeros((piece, LANES), f32)
        inner = jnp.zeros((piece, LANES), f32)
        for e in range(experts):
            stats = ret_refs[e][span, 2 * width :].astype(f32)
            mine = group == e
            log_total = jnp.where(mine, stats[:, 0:1] + stats[:, 1:2] + stats[:, 2:3], log_total)
            inner = jnp.where(mine, stats[:, 3:4] + stats[:, 4:5] + stats[:, 5:6], inner)
        results = jnp.concatenate([ref[span, :width] for ref in ret_refs], axis=0)
        back = jnp.concatenate([ref[span, width : 2 * width] for ref in ret_refs], axis=0)
        logits = dot(second, control, NT).reshape(tokens, piece, LANES)
        weights = jnp.where(own, jnp.exp(logits - log_total), 0.0)
        low = weights.reshape(-1, LANES).astype(bf16)
        spread = dot(low, results)
        grad_weights = (dot(cot, results, NT) + dot(second, back, NT)).reshape(tokens, piece, LANES)
        grad_logits = (weights * (grad_weights - inner)).reshape(-1, LANES).astype(bf16)
        grad_second = dot(low, back) + dot(grad_logits, control)
        grad_control = grad_control + dot(grad_logits, second, TN)
        grad_middles = []
        for token in range(tokens):
            row = (me ^ (token // rows)) * rows + token % rows
            mine = slice(token * piece, (token + 1) * piece)
            middle = middle_scratch[token]
            out_ref[row, span] = (middle + spread[mine].astype(bf16).astype(f32)).astype(bf16)
            grad = grad_second[mine].astype(bf16).astype(f32)
            normed, scaled = normalize(middle)
            grad_gain = grad_gain + jnp.sum((grad * normed).reshape(-1, 8, width), axis=0)
            grad_middle = norm_back(grad * gain_ref[...], normed, scaled)
            grad_middle = (cot_ref[row, span].astype(f32) + grad_middle).astype(bf16)
            grad_middle_ref[token, span] = grad_middle
            grad_middles.append(grad_middle)
        grad_middle = jnp.concatenate(grad_middles, axis=0)
        grad_attended = dot(grad_middle, w_out, NT).astype(bf16)
        grad_attended = grad_attended.reshape(tokens, piece, width)
        for j in range(slot_count):
            back_refs[j][:, span] = grad_attended[j * rows : (j + 1) * rows]
        grad_out = grad_out + dot(attended, grad_middle, TN)
    if last:
        small[...] = jnp.zeros_like(small)
        small[0:1] = jnp.sum(grad_gain, axis=0, keepdims=True)
        for e in range(experts):
            total = grad_control[e * piece : (e + 1) * piece]
            small[pl.ds(1 + (me_ref[1] ^ e), 1)] = jnp.sum(total, axis=0, keepdims=True)
        blocks, lines = keep_ref.shape[:2]
        for columns, value in (
            (slice(0, width), grad_out),
            (slice(width, width + LANES), small[...].T),
        ):
            keep, send = by_core(me, value.reshape(blocks, 2, lines, -1))
            keep_ref[:, :, columns] = keep
            send_ref[:, :, columns] = send.astype(bf16)
    else:
        grad_control_ref[...] = grad_control
        grad_gain_ref[...] = grad_gain
        grad_out_ref[...] = grad_out


def unmix(
    me, part, last, shards, ret_slots, att_slots, inputs, cotangent, w_out, gain, control, before
):
    slot_count, experts = len(att_slots), len(ret_slots)
    rows, positions, width = att_slots[0].shape
    tokens = rows * slot_count
    half = pl.BlockSpec((tokens, positions, width), lambda b, me: (0, part, 0))
    count = 1 + experts + slot_count + 5
    if last:
        kept = (shards // 2, width // shards, width + LANES)
        made = [(None, kept, f32), (None, kept, bf16)]
    else:
        made = [
            (None, (width, width), f32),
            (None, (LANES, width), f32),
            (None, (8, width), f32),
        ]
    result = call(
        functools.partial(unmix_kernel, slot_count, experts, LANES // experts, part, last),
        "unmix",
        (1,),
        [None] * (experts + slot_count)
        + [half, half, fourth(width), None, None]
        + ([pl.BlockSpec(memory_space=pl.ANY)] + [None] * 3 if part else []),
        [(half, cotangent.shape, bf16), (None, (tokens, positions, width), bf16)]
        + [(None, (rows, positions, width), bf16)] * slot_count
        + made,
        [((tokens, LANES // experts, width), f32)] + ([((LANES, width), f32)] if last else []),
        (me, *ret_slots, *att_slots, inputs, cotangent, w_out, gain, control, *before),
        positions * 12 / 256,
        {count: 0} if part else None,
        room=58,
    )
    do_slots = result[2 : 2 + slot_count]
    return do_slots, result[1], [result[0], *result[2 + slot_count :]]


def finish_kernel(slot_count, row_count, parts, *refs):
    me_ref = refs[0]
    gf_refs = refs[1 : 1 + slot_count * row_count]
    rest = refs[1 + slot_count * row_count :]
    inputs_ref, grad_middle_refs, (gain_ref, out_ref) = rest[0], rest[1 : 1 + parts], rest[1 + parts :]
    me = me_ref[0]
    piece = 64
    positions = out_ref.shape[1]
    some = positions // parts
    for start in range(0, positions, piece):
        span = slice(start, start + piece)
        inner = slice(start % some, start % some + piece)
        for j in range(slot_count):
            for row in range(row_count):
                place = (me ^ j) * row_count + row
                normed, scaled = normalize(inputs_ref[place, span].astype(f32))
                incoming = gf_refs[row * slot_count + j][0, span].astype(f32) * gain_ref[...]
                grad = norm_back(incoming, normed, scaled)
                middle = grad_middle_refs[start // some][j * row_count + row, inner]
                out_ref[place, span] = (grad + middle.astype(f32)).astype(bf16)


def finish(me, gf_rows, inputs, grad_middles, gain):
    slot_count, row_count, parts = len(gf_rows[0]), len(gf_rows), len(grad_middles)
    return call(
        functools.partial(finish_kernel, slot_count, row_count, parts),
        "finish",
        (1,),
        [None] * (slot_count * row_count + 2 + parts),
        [(None, inputs.shape, bf16)],
        [],
        (me, *[gf for row in gf_rows for gf in row], inputs, *grad_middles, gain),
        4,
    )[0]


def on_device(
    sizes,
    inputs,
    segments,
    cotangent,
    gain_attn,
    w_qkv,
    w_out,
    gain_mix,
    w_control,
    w_expand,
    w_shrink,
):
    groups, members, slots = sizes
    local_rows, positions, width = inputs.shape
    experts = w_expand.shape[0]
    rows = local_rows // slots
    place = (("gq", groups), ("gi", members), ("seq", slots))
    owners = (("gq", groups), ("seq", slots))
    seq_me = lax.axis_index("seq")
    member = lax.axis_index("gi")
    me = jnp.stack([seq_me, member]).astype(jnp.int32)

    parts = 2 if positions % BLOCK == 0 else 1

    marks = segments.astype(bf16)[:, None, :]
    marks = jnp.pad(marks, ((0, 0), (0, MARKS - 1), (0, width - positions)))

    def row_part(row, j):
        index = (seq_me ^ j) * rows + row
        parts = [lax.dynamic_slice_in_dim(array, index, 1, axis=0) for array in (inputs, marks)]
        return jnp.concatenate(parts, axis=1)

    x_parts = [[row_part(row, j) for j in range(slots)] for row in range(rows)]
    x_rows = [[x_parts[0][0]]]

    def send_some(slots_of, done, first, last):
        for j in range(first, last):
            done.append(partner(slots_of[j], "seq", slots, j))

    small = jnp.concatenate([gain_attn[None], gain_mix[None], w_control], axis=0)
    small = jnp.pad(jnp.transpose(small), ((0, 0), (0, LANES - 2 - experts)))
    packed = jnp.concatenate([w_qkv, w_out, small], axis=1).astype(bf16)
    packed = Doubling(packed, place, ("seq", "gq", "core"))
    packed.steps("seq")
    x_rows, x_parts, w_expand, w_shrink = together((x_rows, x_parts, w_expand, w_shrink), packed)

    def member_parts(array):
        return [
            lax.dynamic_index_in_dim(array, member ^ j, 0, keepdims=False) for j in range(members)
        ]

    send_some(x_parts[0], x_rows[0], 1, slots // 2 + 1)
    weights = member_parts(pack_expert(w_expand.astype(bf16), w_shrink.astype(bf16)))
    weights = swap_slots(weights, "gi")
    packed.steps("gq")
    x_rows, x_parts, weights = together((x_rows, x_parts, weights), packed)
    send_some(x_parts[0], x_rows[0], slots // 2 + 1, slots)
    packed.at_once("gi")
    weights = jnp.stack(natural(weights, member))
    x_rows, x_parts, weights = together((x_rows, x_parts, weights), packed)
    packed.steps("core")
    x_rows, x_parts, weights = together((x_rows, x_parts, weights), packed)
    tail = weights.shape[1] // 2
    halves = [
        Doubling(half, owners, ("gq", "seq"), 1) for half in (weights[:, :tail], weights[:, tail:])
    ]
    halves[0].steps("gq")
    packed = packed.value.reshape(width, -1)

    old = []
    for row in range(rows):
        old = attend_first(me, row, rows, x_rows[row], packed, parts, old)
        if row == 0:
            vectors = old[-1]
            gains = [vectors[0:1], vectors[1:2]]
            control = natural([vectors[2 + e : 3 + e] for e in range(experts)], member)
            control = jnp.concatenate(
                [jnp.broadcast_to(c, (LANES // experts, width)) for c in control], axis=0
            ).astype(bf16)
        if row + 1 < rows:
            x_rows.append(swap_slots(x_parts[row + 1], "seq"))
            old, x_rows[row + 1] = together((old, x_rows[row + 1]), *halves)
        if row == max(0, rows - 2):
            halves[0].steps("seq")
            halves[1].steps("gq")
        if row == rows - 1:
            old, (gain_one, gain_two), control = together((old, gains, control), *halves)
    att, projected, kept = old[:slots], old[slots : slots + 6], old[slots + 6 : slots + 8]
    att_parts, kept = [swap_slots(att, "seq")], [kept]
    for part in range(1, parts):
        att, more = attend_next(me, part, parts, projected, slots)
        more, att_parts[-1] = hold((more, att_parts[-1]))
        att_parts.append(swap_slots(att, "seq"))
        kept.append(more)
    pay_parts = []
    for part in range(parts):
        pay = mix(
            me, part, att_parts[part], inputs, cotangent, packed, gain_two, control, experts
        )
        if part + 1 < parts:
            pay, att_parts[part + 1] = together((pay, att_parts[part + 1]), halves[1])
        if part == 0:
            halves[1].steps("seq")
        if part == parts - 1:
            pay, pay_parts = together((pay, pay_parts), halves[1])
        pay_parts.append(swap_slots(pay, "gi"))
    halves = [half.value.reshape(-1, *half.value.shape[-2:]) for half in halves]
    halves = [(half, partner(half, "seq", slots, 1)) for half in halves]
    ret_parts, earlier = [], []
    for part in range(parts):
        back, more = expert(me, seq_me % 2, part, parts, pay_parts[part], halves, earlier)
        earlier = earlier + list(more)
        if part + 1 < parts:
            pay_parts[part + 1][1], back = hold((pay_parts[part + 1][1], back))
        elif part:
            back, more, ret_parts = hold((back, more, ret_parts))
        ret_parts.append(swap_slots([back] * members, "gi"))

    kept_grad, send = more
    received = partner(send, "seq", slots, 1)
    bits = [2] * len(bits_of((("gq", groups),)))
    bits += [members] + [2] * (len(bits_of((("seq", slots),))) - 1)

    def to_bits(*terms):
        return [term.reshape(*bits, *term.shape[1:]) for term in terms]

    do_parts, grad_middles, before = [], [], []
    for part in range(parts):
        last = part == parts - 1
        if last:
            sum_expert = Halving(to_bits(kept_grad, received), owners, ("seq", "gq"), 1)
            sum_expert.prepare()
            ret_parts[part], before = together((ret_parts[part], before), sum_expert)
        do, grad_middle, before = unmix(
            me,
            part,
            last,
            groups * members * slots,
            ret_parts[part],
            att_parts[part],
            inputs,
            cotangent,
            packed,
            gain_two,
            control,
            before,
        )
        grad_middles.append(grad_middle)
        do_parts.append(swap_slots(do, "seq"))
    output, keep_out, send_out = before
    every_bit = [2] * len(bits_of(place))
    do_parts, send_out = together((do_parts, send_out), sum_expert)
    sum_expert.exchange()
    received_out = partner(send_out, "seq", slots, 1)

    gf_rows, grad_in = [], None
    for row in range(rows):
        gf_slots, grad_in = attend_back(
            me,
            row,
            rows,
            groups * members * slots,
            x_rows[row],
            do_parts,
            gain_one,
            packed,
            projected,
            kept,
            grad_in,
        )
        grad_in = grad_in[0] if row < rows - 1 else grad_in
        if row == 0:
            gf_slots, grad_in, received_out = together((gf_slots, grad_in, received_out), sum_expert)
            sum_expert.combine()
            while sum_expert.order[0][0] == "seq":
                sum_expert.step(sum_expert.order.pop(0))
            sum_expert.prepare()
            gf_slots, grad_in = together((gf_slots, grad_in), sum_expert)
            sum_expert.exchange()
        if row:
            gf_slots, grad_in, gf_rows = together((gf_slots, grad_in, gf_rows), sum_expert)
        if row < rows - 1:
            gf_rows.append(swap_slots(gf_slots, "seq"))
    gf_rows.append([gf_slots[0]])
    send_some(gf_slots, gf_rows[-1], 1, slots // 2 + 1)
    keep, send = grad_in
    received = partner(send, "seq", slots, 1)
    sum_expert.combine()
    sums = sum_expert.finish()
    columns = [p if j == 0 else p.astype(bf16) for j, p in enumerate(member_parts(sums))]
    columns = swap_slots(columns, "gi")
    gf_rows, gf_slots, received, columns = hold((gf_rows, gf_slots, received, columns))
    send_some(gf_slots, gf_rows[-1], slots // 2 + 1, slots)
    total = keep + received.astype(f32)
    total = jnp.concatenate([total, keep_out + received_out.astype(f32)], axis=-1)
    total = total.reshape(*every_bit[1:], *total.shape[1:])
    sum_in = Halving(total, place, ("gi", "gq", "seq"))
    sum_in.cut(("gi",))
    sum_in.send()
    grad_inputs = finish(me, gf_rows, inputs, grad_middles, gain_one)
    grad_inputs = together(grad_inputs, sum_in)
    sum_in.combine()
    sum_in.cut(("gq", "seq"))
    sum_in.send()
    sum_in.combine()
    columns = natural(columns, member)
    columns = jnp.stack([c.astype(f32) for c in columns])
    grad_expand, grad_shrink = unpack_expert(columns, width // (groups * members * slots))
    total = sum_in.finish()
    grad_in, grad_out = total[:, : 3 * width], total[:, 3 * width :]
    small = jnp.transpose(grad_out[:, width:])
    weighted = jnp.sum(grad_in * w_qkv.astype(bf16).astype(f32), axis=1)
    return (
        output,
        grad_inputs,
        weighted / gain_attn.astype(bf16).astype(f32),
        grad_in,
        grad_out[:, :width],
        small[0],
        small[1 : 1 + experts],
        grad_expand,
        grad_shrink,
    )


def solution(mesh):
    dp_count, seq_count = mesh.shape["dp"], mesh.shape["seq"]

    def run(inputs, *args):
        members = GROUP * dp_count // inputs.shape[0]
        sizes = (dp_count // members, members, seq_count)
        fine = Mesh(mesh.devices.reshape(sizes), ("gq", "gi", "seq"))
        dp, both = ("gq", "gi"), ("gq", "gi", "seq")
        return jax.shard_map(
            functools.partial(on_device, sizes),
            mesh=fine,
            in_specs=(
                P(dp, "seq", None),
                P(dp, "seq"),
                P(dp, "seq", None),
                P(both),
                P(both, None),
                P(both, None),
                P(both),
                P(None, both),
                P(None, both, None),
                P(None, both, None),
            ),
            out_specs=(
                P(dp, "seq", None),
                P(dp, "seq", None),
                P(both),
                P(both, None),
                P(both, None),
                P(both),
                P(None, both),
                P(None, both, None),
                P(None, both, None),
            ),
            check_vma=False,
        )(inputs, *args)

    return run
```

```python
import functools
import math

import jax
import jax.numpy as jnp
from jax import lax
from jax.experimental import pallas as pl
from jax.experimental.pallas import tpu as pltpu
from jax.sharding import Mesh
from jax.sharding import PartitionSpec as P

HEADS = 8
GROUP = 32
BLOCK = 256
LANES = 128
MARKS = 16

LOG2E = math.log2(math.e)
LN2 = math.log(2.0)
BIG = 1e30

bf16 = jnp.bfloat16
f32 = jnp.float32

NN = (((1,), (0,)), ((), ()))
NT = (((1,), (1,)), ((), ()))
TN = (((0,), (0,)), ((), ()))


def dot(a, b, dims=NN):
    return lax.dot_general(a, b, dims, preferred_element_type=f32)


def normalize(values):
    center = values - jnp.mean(values, axis=-1, keepdims=True)
    scaled = lax.rsqrt(jnp.mean(center * center, axis=-1, keepdims=True) + 1e-05)
    return center * scaled, scaled


def norm_back(incoming, normed, scaled):
    return scaled * (
        incoming
        - jnp.mean(incoming, axis=-1, keepdims=True)
        - normed * jnp.mean(incoming * normed, axis=-1, keepdims=True)
    )


def split3(value):
    high = value.astype(bf16).astype(f32)
    rest = value - high
    mid = rest.astype(bf16).astype(f32)
    low = (rest - mid).astype(bf16).astype(f32)
    return high, mid, low


def partner(value, axis, size, mask):
    return lax.ppermute(value, axis, [(i, i ^ mask) for i in range(size)])


def swap_slots(slots, axis):
    size = len(slots)
    return [slots[0]] + [partner(slots[j], axis, size, j) for j in range(1, size)]


def natural(slots, me):
    out = list(slots)
    bit = 1
    while bit < len(out):
        flip = (me & bit) != 0
        out = [jnp.where(flip, out[k ^ bit], out[k]) for k in range(len(out))]
        bit *= 2
    return out


def bits_of(sizes):
    bits = []
    for axis, size in sizes:
        mask = size // 2
        while mask:
            bits.append((axis, size, mask))
            mask //= 2
    return bits


def named(bit):
    axis, _, mask = bit
    return "core" if axis == "seq" and mask == 1 else axis


class Steps:
    def __init__(self, value, sizes, order):
        self.order = [bit for axis in order for bit in reversed(bits_of(sizes)) if named(bit) == axis]
        self.value = value

    def steps(self, axis):
        while self.order and named(self.order[0]) == axis:
            self.step(self.order.pop(0))
        return self

    def finish(self):
        while self.order:
            self.step(self.order.pop(0))
        return self.value


class Doubling(Steps):
    def __init__(self, value, sizes, order, inner=0):
        super().__init__(value, sizes, order)
        self.inner = inner
        self.place = bits_of(sizes)
        self.have = []

    def step(self, bit):
        axis, size, mask = bit
        depth = sum(self.place.index(other) < self.place.index(bit) for other in self.have)
        depth += self.inner if axis == "seq" else 0
        other = partner(self.value, axis, size, mask)
        high = (lax.axis_index(axis) & mask) != 0
        first = jnp.where(high, other, self.value)
        second = jnp.where(high, self.value, other)
        self.value = jnp.stack([first, second], axis=depth)
        self.have.append(bit)

    def at_once(self, axis):
        bits = [bit for bit in self.place if bit[0] == axis]
        self.order = [bit for bit in self.order if bit[0] != axis]
        depth = sum(self.place.index(other) < self.place.index(bits[0]) for other in self.have)
        depth += self.inner if axis == "seq" else 0
        slots = natural(swap_slots([self.value] * 2 ** len(bits), axis), lax.axis_index(axis))
        shape = self.value.shape
        value = jnp.stack(slots, axis=depth)
        self.value = value.reshape(shape[:depth] + (2,) * len(bits) + shape[depth:])
        self.have += bits


def total_of(terms):
    return functools.reduce(jnp.add, [term.astype(f32) for term in terms])


class Halving(Steps):
    def __init__(self, value, sizes, order, inner=0):
        super().__init__(None, sizes, order)
        self.terms = value if isinstance(value, list) else [value]
        self.sizes = sizes
        self.left = [bit for bit in bits_of(sizes) if bit in self.order]
        self.inner = inner

    def prepare(self):
        bit = self.order.pop(0)
        depth = self.left.index(bit)
        self.left.pop(depth)
        axis, size, mask = bit
        depth += self.inner if axis == "seq" else 0
        high = ((lax.axis_index(axis) & mask) != 0).astype(jnp.int32)
        keep, send = [
            [lax.dynamic_index_in_dim(term, at, depth, keepdims=False) for term in self.terms]
            for at in (high, 1 - high)
        ]
        self.terms = keep
        self.value = total_of(send).astype(bf16)
        self.link = bit

    def exchange(self):
        axis, size, mask = self.link
        self.value = partner(self.value, axis, size, mask)

    def combine(self):
        if isinstance(self.value, list):
            self.terms = self.value
        else:
            self.terms = self.terms + [self.value]
        self.value = None

    def finish(self):
        super().finish()
        return total_of(self.terms)

    def step(self, bit):
        self.order.insert(0, bit)
        self.prepare()
        self.exchange()
        self.combine()

    def cut(self, axes):
        bits = [bit for bit in self.left if bit[0] in axes]
        self.order = [bit for bit in self.order if bit not in bits]
        depth = self.left.index(bits[0])
        if self.inner or bits != self.left[depth : depth + len(bits)]:
            raise NotImplementedError
        self.left = [bit for bit in self.left if bit not in bits]
        value = total_of(self.terms)
        shape = value.shape
        value = value.reshape(shape[:depth] + (2 ** len(bits),) + shape[depth + len(bits) :])
        place = 0
        for axis, size, mask in bits:
            place = 2 * place + ((lax.axis_index(axis) & mask) != 0).astype(jnp.int32)
        parts = [
            lax.dynamic_index_in_dim(value, place ^ j, depth, keepdims=False)
            for j in range(2 ** len(bits))
        ]
        self.value = [parts[0]] + [part.astype(bf16) for part in parts[1:]]
        self.link = bits

    def send(self):
        bits = self.link
        sizes = [(axis, size) for axis, size in self.sizes if axis in [bit[0] for bit in bits]]
        names = tuple(axis for axis, _ in sizes)
        for j in range(1, 2 ** len(bits)):
            masks = {axis: 0 for axis in names}
            for i, (axis, _, mask) in enumerate(bits):
                if j >> (len(bits) - 1 - i) & 1:
                    masks[axis] |= mask
            pairs = []
            for source in range(math.prod(size for _, size in sizes)):
                target, rest, unit = 0, source, 1
                for axis, size in reversed(sizes):
                    target += ((rest % size) ^ masks[axis]) * unit
                    rest, unit = rest // size, unit * size
                pairs.append((source, target))
            self.value[j] = lax.ppermute(self.value[j], names, pairs)


hold = lax.optimization_barrier


def together(values, *sums):
    values, held = lax.optimization_barrier((values, [item.value for item in sums]))
    for item, value in zip(sums, held):
        item.value = value
    return values


def call(kernel, name, grid, in_specs, outs, scratch, args, micros, aliases=None, room=10):
    def full(shape):
        return pl.BlockSpec(shape, lambda *_: (0,) * len(shape))

    in_specs = [spec or full(arg.shape) for spec, arg in zip(in_specs, args[1:], strict=True)]
    outs = [(spec or full(shape), shape, dtype) for spec, shape, dtype in outs]
    return pl.pallas_call(
        kernel,
        grid_spec=pltpu.PrefetchScalarGridSpec(
            num_scalar_prefetch=1,
            grid=grid,
            in_specs=in_specs,
            out_specs=[spec for spec, _, _ in outs],
            scratch_shapes=[pltpu.VMEM(shape, dtype) for shape, dtype in scratch],
        ),
        out_shape=[jax.ShapeDtypeStruct(shape, dtype) for _, shape, dtype in outs],
        input_output_aliases=aliases or {},
        compiler_params=pltpu.CompilerParams(vmem_limit_bytes=room << 20),
        cost_estimate=pl.CostEstimate(
            flops=int(micros * 1e9), bytes_accessed=1 << 20, transcendentals=0
        ),
        name=name,
    )(*args)


def per_row(*shape):
    return pl.BlockSpec((1,) + shape, lambda r, me: (r,) + (0,) * len(shape))


def whole(*shape):
    return pl.BlockSpec(shape, lambda r, me: (0,) * len(shape))


def fourth(width):
    return pl.BlockSpec((width, width), lambda b, me: (0, 3))


def by_core(me, pairs):
    odd = me % 2 == 1
    first, second = pairs[:, 0], pairs[:, 1]
    return jnp.where(odd, second, first), jnp.where(odd, first, second)


def causal_bias(step=LANES):
    rows = LANES + step * (BLOCK // LANES - 1)
    key = lax.broadcasted_iota(jnp.int32, (rows, BLOCK), 0)
    query = lax.broadcasted_iota(jnp.int32, (rows, BLOCK), 1)
    query = query + (query // LANES) * (step - LANES)
    return jnp.where(key <= query, 0.0, -BIG).astype(f32)


def key_features(segment_row, length):
    row = lax.broadcasted_iota(jnp.int32, (LANES, length), 0)
    marks = (row == segment_row) | ((row >= 7) & (row < 10))
    return jnp.where(marks, 1.0, 0.0).astype(f32).T.astype(bf16)


def query_features(segment_row, length):
    row = lax.broadcasted_iota(jnp.int32, (16, length), 0)
    return jnp.where((row < 7) & (row != segment_row), -BIG, 0.0).astype(f32)


def padded_head(head, features, odd):
    blank = jnp.zeros_like(head)
    rest = jnp.zeros((LANES - 16, head.shape[1]), bf16)
    both = [blank, head] if odd else [head, blank]
    return jnp.concatenate(both + [features, rest], axis=0)


def attend_queries(part, parts, slots, me, seg_ref, q_t, k_ref, v_t, att_refs, ot_ref, lse_ref, aux):
    k_aux, q_aux, causal = aux
    length = k_ref.shape[1]
    piece = length // slots
    some = piece // parts
    step = piece if parts > 1 else LANES
    segment_row = seg_ref[0]
    q_aux[...] = query_features(segment_row, length)
    k_aux[...] = key_features(segment_row, length)
    blocks = slots * some // BLOCK
    count = BLOCK // some if parts > 1 else 1

    def head_pair(pair, carry):
        base = pl.multiple_of(pair * LANES, LANES)
        for odd in range(2):
            rows = pl.ds(pl.multiple_of(pair * LANES + odd * 64, 64), 64)
            for block in range(blocks):
                if parts > 1:
                    first = block * count * piece + part * some
                    places = [pl.ds(first + i * piece, some) for i in range(count)]
                else:
                    first = block * BLOCK
                    places = [pl.ds(first, BLOCK)]
                feats = jnp.concatenate([q_aux[:, p] for p in places], axis=1).astype(bf16)
                head = jnp.concatenate([q_t[0, rows, p] for p in places], axis=1)
                query = padded_head(head, feats, odd)
                chunks = [(k, min(BLOCK, first - k)) for k in range(0, first, BLOCK)]
                chunks.append((first, causal.shape[0]))
                scores = []
                for start, size in chunks:
                    keys = pl.ds(start, size)
                    key = jnp.concatenate([k_ref[0, keys, pl.ds(base, LANES)], k_aux[keys]], axis=1)
                    score = dot(key, query)
                    scores.append(score + causal[...] if start == first else score)
                top = functools.reduce(
                    jnp.maximum, [jnp.max(score, axis=0, keepdims=True) for score in scores]
                )
                total = jnp.zeros((1, BLOCK), f32)
                out = jnp.zeros((64, BLOCK), f32)
                for (start, size), score in zip(chunks, scores):
                    prob = jnp.exp2(score - top)
                    total = total + jnp.sum(prob, axis=0, keepdims=True)
                    out = out + dot(v_t[0, rows, pl.ds(start, size)], prob.astype(bf16))
                held = pl.ds(block * BLOCK, BLOCK)
                ot_ref[0, rows, held] = (out / total).astype(bf16)
                lse_ref[0, pl.ds(pair * 2 + odd, 1), held] = top + jnp.log2(total)
        return carry

    lax.fori_loop(0, HEADS // 2, head_pair, 0)
    for j in range(slots):
        place = pl.ds(pl.multiple_of((me ^ j) * some, some), some)
        att_refs[j][0] = ot_ref[0, :, place].T


def attend_first_kernel(parts, slots, old, *refs):
    me_ref = refs[0]
    x_refs = refs[1 : 1 + slots]
    vector_ref, w_ref = refs[1 + slots : 3 + slots]
    rest = refs[3 + slots + old :]
    att_refs = rest[:slots]
    seg_ref, qt_ref, k_ref, v_ref, q_ref, vt_ref, ot_ref, lse_ref, rows_ref = rest[slots : slots + 9]
    w_t, *aux = rest[slots + 9 :]
    width = w_ref.shape[0]
    piece = x_refs[0].shape[1] - MARKS
    me = me_ref[0]
    score_scale = LOG2E / math.sqrt(width // HEADS)

    w_t[:width] = w_ref[:, :width].T
    w_t[width:] = w_ref[:, 2 * width :].T
    aux[2][...] = causal_bias(piece if parts > 1 else LANES)
    rows_ref[...] = vector_ref[...].astype(f32).T
    gain = rows_ref[0:1]
    for j in range(slots):
        place = pl.ds(pl.multiple_of((me ^ j) * piece, piece), piece)
        marks = x_refs[j][0, piece:].astype(f32)
        seg_ref[0, :, place] = marks[0:1, :piece].astype(jnp.int32)
        normed, _ = normalize(x_refs[j][0, :piece].astype(f32))
        first_in = (normed * gain).astype(bf16)
        projected = dot(first_in, w_ref[...])
        q_ref[0, place] = (projected[:, :width] * score_scale).astype(bf16)
        k_ref[0, place] = projected[:, width : 2 * width].astype(bf16)
        v_ref[0, place] = projected[:, 2 * width :].astype(bf16)
        turned = dot(w_t[...], first_in, NT)
        qt_ref[0, :, place] = (turned[:width] * score_scale).astype(bf16)
        vt_ref[0, :, place] = turned[width:].astype(bf16)
    attend_queries(
        0, parts, slots, me, seg_ref, qt_ref, k_ref, vt_ref, att_refs, ot_ref, lse_ref, aux
    )


def attend_next_kernel(part, parts, slots, *refs):
    me_ref, seg_ref, qt_ref, k_ref, vt_ref = refs[:5]
    att_refs = refs[5 : 5 + slots]
    ot_ref, lse_ref, *aux = refs[5 + slots :]

    @pl.when(pl.program_id(0) == 0)
    def _():
        aux[2][...] = causal_bias(k_ref.shape[1] // slots if parts > 1 else LANES)

    attend_queries(
        part, parts, slots, me_ref[0], seg_ref, qt_ref, k_ref, vt_ref, att_refs, ot_ref, lse_ref, aux
    )


def attend_outs(rows, slots, some, width):
    return [(per_row(some, width), (rows, some, width), bf16)] * slots, [
        (per_row(width, slots * some), (rows, width, slots * some), bf16),
        (per_row(HEADS, slots * some), (rows, HEADS, slots * some), f32),
    ]


def attend_scratch(length, piece, parts):
    span = LANES + (piece if parts > 1 else LANES) * (BLOCK // LANES - 1)
    return [((length, LANES), bf16), ((16, length), f32), ((span, BLOCK), f32)]


def attend_first(me, row, rows, x_slots, weights, parts, old):
    slots = len(x_slots)
    _, packed, width = x_slots[0].shape
    piece = packed - MARKS
    length = piece * slots

    def this(*shape):
        return pl.BlockSpec((1,) + shape, lambda r, me: (row,) + (0,) * len(shape))

    some = piece // parts
    turned = (this(width, length), (rows, width, length), bf16)
    plain = (this(length, width), (rows, length, width), bf16)
    outs = (
        [(this(some, width), (rows, some, width), bf16)] * slots
        + [(this(1, length), (rows, 1, length), jnp.int32)]
        + [turned, plain, plain, plain, turned]
        + [
            (this(width, slots * some), (rows, width, slots * some), bf16),
            (this(HEADS, slots * some), (rows, HEADS, slots * some), f32),
            (whole(LANES, width), (LANES, width), f32),
        ]
    )
    result = call(
        functools.partial(attend_first_kernel, parts, slots, len(old)),
        "attend_first",
        (1,),
        [per_row(packed, width)] * slots
        + [
            pl.BlockSpec((width, LANES), lambda r, me: (0, 4 * width // LANES)),
            whole(width, 3 * width),
        ]
        + [pl.BlockSpec(memory_space=pl.ANY)] * len(old),
        outs,
        [((2 * width, width), bf16)] + attend_scratch(length, piece, parts),
        (me, *x_slots, weights, weights, *old),
        12,
        {3 + slots + i: i for i in range(len(old))},
        room=26,
    )
    return result


def attend_next(me, part, parts, projected, slots):
    segment_rows, q_t, k, _, _, v_t = projected
    rows, length, width = k.shape
    piece = length // slots
    att, more = attend_outs(rows, slots, piece // parts, width)
    result = call(
        functools.partial(attend_next_kernel, part, parts, slots),
        "attend_next",
        (rows,),
        [
            per_row(1, length),
            per_row(width, length),
            per_row(length, width),
            per_row(width, length),
        ],
        att + more,
        attend_scratch(length, piece, parts),
        (me, segment_rows, q_t, k, v_t),
        28 / parts,
        room=16,
    )
    return result[:slots], result[slots:]


def attend_back_kernel(row, last, parts, slot_count, *refs):
    me_ref = refs[0]
    x_refs = refs[1 : 1 + slot_count]
    rest = refs[1 + slot_count :]
    do_refs, rest = rest[: parts * slot_count], rest[parts * slot_count :]
    seg_ref, gain_ref, w_ref, qt_ref, k_ref, v_ref, q_ref = rest[:7]
    ot_refs, lse_refs = rest[7 : 7 + parts], rest[7 + parts : 7 + 2 * parts]
    rest = rest[7 + 2 * parts :]
    if row:
        before_ref, rest = rest[0], rest[1:]
    gf_refs, rest = rest[:slot_count], rest[slot_count:]
    dw_refs, rest = rest[: 1 + last], rest[1 + last :]
    (
        k_aux, q_aux, v_aux, causal, do, first_t, work_t, k_t, grads, prob, grad_score, delta, lse
    ) = rest
    width = w_ref.shape[0]
    piece = x_refs[0].shape[1] - MARKS
    some = piece // parts
    length = piece * slot_count
    me = me_ref[0]
    score_scale = 1.0 / math.sqrt(width // HEADS)
    causal[...] = causal_bias()
    lane = lax.broadcasted_iota(jnp.int32, (length, LANES), 1)
    v_aux[...] = jnp.where(lane < 3, 1.0, 0.0).astype(bf16)
    for part in range(parts):
        for i in range(slot_count):
            held = pl.ds(i * some, some)
            lse[:, pl.ds(i * piece + part * some, some)] = lse_refs[part][0, :, held]

    segment_row = seg_ref[0]
    q_aux[...] = query_features(segment_row, length)
    k_aux[...] = key_features(segment_row, length)
    gain = gain_ref[...]
    for j in range(slot_count):
        place = pl.ds(pl.multiple_of((me ^ j) * piece, piece), piece)
        normed, _ = normalize(x_refs[j][0, :piece].astype(f32))
        first_t[:, place] = (normed * gain).astype(bf16).T
        k_t[:, place] = k_ref[0, place].T
        for part in range(parts):
            start = (me ^ j) * piece + part * some
            place = pl.ds(pl.multiple_of(start, some), some)
            held = pl.ds(pl.multiple_of((me ^ j) * some, some), some)
            grad = do_refs[part * slot_count + j][0]
            do[place] = grad
            turned = grad.T
            work_t[:, place] = turned
            product = turned.astype(f32) * ot_refs[part][0, :, held].astype(f32)
            delta[:, place] = jnp.sum(product.reshape(HEADS, width // HEADS, some), axis=1)
    lane = lax.broadcasted_iota(jnp.int32, (1, LANES), 1)
    feature = lax.broadcasted_iota(jnp.int32, (16, BLOCK), 0)
    blocks = length // BLOCK

    def head_pair(pair, carry):
        base = pl.multiple_of(pair * LANES, LANES)
        for odd in range(2):
            rows = pl.ds(pl.multiple_of(pair * LANES + odd * 64, 64), 64)
            head = pl.ds(pair * 2 + odd, 1)
            for qb in range(blocks):
                queries = pl.ds(qb * BLOCK, BLOCK)
                a, b, c = split3(lse[head, queries])
                feats = jnp.where(feature == 7, -a, q_aux[:, queries])
                feats = jnp.where(feature == 8, -b, jnp.where(feature == 9, -c, feats))
                query = padded_head(qt_ref[0, rows, queries], feats.astype(bf16), odd)
                a, b, c = split3(delta[head, queries])
                feats = jnp.where(feature == 0, -a, jnp.where(feature == 1, -b, 0.0))
                feats = jnp.where(feature == 2, -c, feats)
                grad = padded_head(work_t[rows, queries], feats.astype(bf16), odd)
                held = pl.ds(odd * length + qb * BLOCK, BLOCK)
                for kb in range(qb + 1):
                    keys = pl.ds(kb * BLOCK, BLOCK)
                    key = jnp.concatenate([k_ref[0, keys, pl.ds(base, LANES)], k_aux[keys]], axis=1)
                    score = dot(key, query)
                    if kb == qb:
                        score = score + causal[...]
                    value = jnp.concatenate(
                        [v_ref[0, keys, pl.ds(base, LANES)], v_aux[keys]], axis=1
                    )
                    grad_prob = dot(value, grad)
                    weight = jnp.exp2(score)
                    prob[keys, held] = weight.astype(bf16)
                    grad_score[keys, held] = (weight * grad_prob).astype(bf16)
                end = (qb + 1) * BLOCK
                grad_q = dot(k_t[rows, 0:end], grad_score[0:end, held])
                work_t[rows, queries] = (grad_q * score_scale).astype(bf16)
        for kb in range(blocks):
            keys = pl.ds(kb * BLOCK, BLOCK)
            later = pl.ds(kb * BLOCK, length - kb * BLOCK)
            grad_v = jnp.zeros((BLOCK, LANES), f32)
            grad_k = jnp.zeros((BLOCK, LANES), f32)
            for odd in range(2):
                mine = (lane >= 64) if odd else (lane < 64)
                held = pl.ds(odd * length + kb * BLOCK, length - kb * BLOCK)
                zero = jnp.zeros((), bf16)
                grad = jnp.where(mine, do[later, pl.ds(base, LANES)], zero)
                query = jnp.where(mine, q_ref[0, later, pl.ds(base, LANES)], zero)
                grad_v = grad_v + dot(prob[keys, held], grad)
                grad_k = grad_k + dot(grad_score[keys, held], query)
            grads[keys, pl.ds(pl.multiple_of(width + pair * LANES, LANES), LANES)] = (
                grad_k * LN2
            ).astype(bf16)
            grads[keys, pl.ds(pl.multiple_of(2 * width + pair * LANES, LANES), LANES)] = (
                grad_v.astype(bf16)
            )
        return carry

    lax.fori_loop(0, HEADS // 2, head_pair, 0)
    for j in range(slot_count):
        place = pl.ds(pl.multiple_of((me ^ j) * piece, piece), piece)
        grads[place, :width] = work_t[:, place].T
        gf_refs[j][0] = dot(grads[place], w_ref[...], NT).astype(bf16)
    update = dot(first_t[...], grads[...])
    if row:
        update = before_ref[...] + update
    if last:
        keep, send = by_core(me, update.reshape(-1, 2, *dw_refs[0].shape[1:]))
        dw_refs[0][...] = keep
        dw_refs[1][...] = send.astype(bf16)
    else:
        dw_refs[0][...] = update


def attend_back(me, row, rows, shards, x_slots, do_parts, gain, w_qkv, projected, kept, before):
    slot_count, parts = len(x_slots), len(do_parts)
    _, packed, width = x_slots[0].shape
    piece = packed - MARKS
    length = piece * slot_count
    some = piece // parts
    last = row == rows - 1

    def this(*shape):
        return pl.BlockSpec((1,) + shape, lambda r, me: (row,) + (0,) * len(shape))

    half = (shards // 2, width // shards, 3 * width)
    outs = [(per_row(piece, width), (1, piece, width), bf16)] * slot_count
    if last:
        outs += [(whole(*half), half, f32), (whole(*half), half, bf16)]
    else:
        outs += [(whole(width, 3 * width), (width, 3 * width), f32)]
    segment_rows, q_t, k, v, q, _ = projected
    result = call(
        functools.partial(attend_back_kernel, row, last, parts, slot_count),
        "attend_back",
        (1,),
        [per_row(packed, width)] * slot_count
        + [this(some, width)] * (parts * slot_count)
        + [this(1, length), whole(1, width), whole(width, 3 * width)]
        + [this(width, length)]
        + [this(length, width)] * 3
        + [this(width, some * slot_count)] * parts
        + [this(HEADS, some * slot_count)] * parts
        + ([whole(width, 3 * width)] if row else []),
        outs,
        [
            ((length, LANES), bf16),
            ((16, length), f32),
            ((length, LANES), bf16),
            ((BLOCK, BLOCK), f32),
            ((length, width), bf16),
            ((width, length), bf16),
            ((width, length), bf16),
            ((width, length), bf16),
            ((length, 3 * width), bf16),
            ((length, 2 * length), bf16),
            ((length, 2 * length), bf16),
            ((HEADS, length), f32),
            ((HEADS, length), f32),
        ],
        (
            me,
            *x_slots,
            *[do for part in do_parts for do in part],
            segment_rows,
            gain,
            w_qkv,
            q_t,
            k,
            v,
            q,
            *[o for o, _ in kept],
            *[l for _, l in kept],
            *([before] if row else []),
        ),
        28,
        room=60,
    )
    return result[:slot_count], result[slot_count:]


def tokens_of(refs, span):
    return jnp.concatenate([ref[:, span] for ref in refs], axis=0).reshape(-1, refs[0].shape[-1])


def rows_of(ref, me, rows, slot_count, span):
    parts = [ref[pl.ds((me ^ j) * rows, rows), span] for j in range(slot_count)]
    return jnp.concatenate(parts, axis=0).reshape(-1, ref.shape[-1])


def diagonal(piece):
    place = lax.broadcasted_iota(jnp.int32, (piece, LANES), 0)
    lane = lax.broadcasted_iota(jnp.int32, (piece, LANES), 1)
    return place == lane % piece, lane // piece, lane


def mix_kernel(slot_count, experts, piece, *refs):
    me_ref = refs[0]
    att_refs = refs[1 : 1 + slot_count]
    inputs_ref, cot_ref, w_out_ref, gain_ref, control_ref = refs[1 + slot_count : 6 + slot_count]
    pay_refs = refs[6 + slot_count :]
    rows, positions, width = att_refs[0].shape
    tokens = rows * slot_count
    me = me_ref[0]
    own, _, lane = diagonal(piece)
    w_out = w_out_ref[...]
    for sub in range(positions // piece):
        span = slice(sub * piece, (sub + 1) * piece)
        added = dot(tokens_of(att_refs, span), w_out)
        second = []
        for token in range(tokens):
            row = (me ^ (token // rows)) * rows + token % rows
            middle = inputs_ref[row, span].astype(f32) + added[token * piece : (token + 1) * piece]
            normed, _ = normalize(middle)
            second.append((normed * gain_ref[...]).astype(bf16))
        second = jnp.concatenate(second, axis=0)
        grad = rows_of(cot_ref, me, rows, slot_count, span)
        logits = dot(second, control_ref[...], NT).reshape(tokens, piece, LANES)
        top = jnp.max(logits, axis=0)
        weights = jnp.exp(logits - top)
        total = jnp.sum(weights, axis=0)
        log_total = top + jnp.log(total)
        weights = jnp.where(own, weights * (1.0 / total), 0.0)
        spread_out = weights.reshape(-1, LANES).astype(bf16)
        mixed = dot(spread_out, second, TN).astype(bf16)
        grad_results = dot(spread_out, grad, TN).astype(bf16)
        a, b, c = split3(log_total)
        for e in range(experts):
            mine = slice(e * piece, (e + 1) * piece)
            first = slice(e * piece, e * piece + 1)
            stats = jnp.where(lane == 0, a[:, first], jnp.where(lane == 1, b[:, first], c[:, first]))
            pay_refs[e][span, :width] = mixed[mine]
            pay_refs[e][span, width : 2 * width] = grad_results[mine]
            pay_refs[e][span, 2 * width :] = stats.astype(bf16)


def mix(me, part, att_slots, inputs, cotangent, w_out, gain, control, experts):
    slot_count = len(att_slots)
    rows, positions, width = att_slots[0].shape
    tokens = rows * slot_count
    half = pl.BlockSpec((tokens, positions, width), lambda b, me: (0, part, 0))
    pay = (None, (positions, 2 * width + LANES), bf16)
    return call(
        functools.partial(mix_kernel, slot_count, experts, LANES // experts),
        "mix",
        (1,),
        [None] * slot_count + [half, half, fourth(width), None, None],
        [pay] * experts,
        [],
        (me, *att_slots, inputs, cotangent, w_out, gain, control),
        positions * 8 / 256,
    )


def expert_kernel(part, parts, tiled, slot_count, *refs):
    me_ref = refs[0]
    pay_refs = refs[1 : 1 + slot_count]
    rest = refs[1 + slot_count :]
    count = 4 if tiled else 2
    weight_refs, rest = rest[:count], rest[count:]
    expand_ref = weight_refs[0]
    last = part == parts - 1
    earlier, rest = rest[: 4 * part], rest[4 * part :]
    if last:
        back_ref, keep_ref, send_ref = rest[:3]
        mixed_acc, grad_acc, result_acc, back_acc, stat, *more, mixed_low, grad_low = rest[3:]
    else:
        back_ref, mixed_low, grad_low, hidden_ref, pre_ref = rest[:5]
        mixed_acc, grad_acc, result_acc, back_acc, stat, *more = rest[5:]
    me = me_ref[0]
    width = expand_ref.shape[-1]
    step = pl.program_id(0)

    @pl.when(step == 0)
    def _():
        logs = []
        for j in range(slot_count):
            stats = pay_refs[j][:, 2 * width :].astype(f32)
            logs.append(stats[:, 0:1] + stats[:, 1:2] + stats[:, 2:3])
        top = functools.reduce(jnp.maximum, logs)
        total = functools.reduce(jnp.add, [jnp.exp(log - top) for log in logs])
        log_total = top + jnp.log(total)
        mixed, grad = 0.0, 0.0
        for j in range(slot_count):
            share = jnp.exp(logs[j] - log_total)
            mixed = mixed + share * pay_refs[j][:, :width].astype(f32)
            grad = grad + share * pay_refs[j][:, width : 2 * width].astype(f32)
        mixed_acc[...] = mixed
        grad_acc[...] = grad
        mixed_low[...] = mixed.astype(bf16)
        grad_low[...] = grad.astype(bf16)
        result_acc[...] = jnp.zeros_like(result_acc)
        back_acc[...] = jnp.zeros_like(back_acc)
        stat[...] = jnp.broadcast_to(log_total, stat.shape)

    mixed, grad = mixed_low[...], grad_low[...]
    if tiled:
        for i in range(2):
            own, other = weight_refs[2 * i][...], weight_refs[2 * i + 1][...]
            odd = me % 2 == 1
            more[i][:, 0] = jnp.where(odd, other, own)
            more[i][:, 1] = jnp.where(odd, own, other)
        expand, shrink = [ref[...].reshape(-1, width) for ref in more]
    else:
        expand, shrink = [ref[...].reshape(-1, width) for ref in weight_refs]
    value = dot(mixed, expand)
    coeff = math.sqrt(2.0 / math.pi)
    square = value * value
    turn = jnp.tanh(coeff * (value + 0.044715 * (square * value)))
    half = 0.5 * (1.0 + turn)
    hidden = (value * half).astype(bf16)
    slope = half + (0.5 * coeff) * value * (1.0 - turn * turn) * (1.0 + (3 * 0.044715) * square)
    result_acc[...] += dot(hidden, shrink)
    grad_pre = (dot(grad, shrink, NT) * slope).astype(bf16)
    back_acc[...] += dot(grad_pre, expand, NT)
    if last:
        sets = [earlier[4 * i : 4 * i + 4] for i in range(part)]
        mixed = jnp.concatenate([m[...] for m, _, _, _ in sets] + [mixed], axis=0)
        grad = jnp.concatenate([g[...] for _, g, _, _ in sets] + [grad], axis=0)
        hidden = jnp.concatenate([h[...] for _, _, h, _ in sets] + [hidden], axis=0)
        grad_pre = jnp.concatenate([p[...] for _, _, _, p in sets] + [grad_pre], axis=0)
        grad_expand = dot(mixed, grad_pre, TN).astype(bf16)
        grad_shrink = dot(hidden, grad, TN).astype(bf16)
        if tiled:
            shards = 2 * keep_ref.shape[0]
            lines = width // shards
            both = keep_ref.shape[1]
            keep, send = by_core(me, grad_expand.reshape(shards // 2, 2, lines, width))
            place = pl.ds(pl.multiple_of(step * lines, lines), lines)
            keep_ref[:, place] = keep
            send_ref[:, place] = send
            count = 2 * width // both // 2
            keep, send = by_core(me, grad_shrink.reshape(count, 2, both // 2, width))
            place = pl.ds(step * count, count)
            keep_ref[place, both // 2 :] = keep
            send_ref[place, both // 2 :] = send
        else:
            keep_ref[...] = grad_expand.reshape(keep_ref.shape)
            send_ref[...] = grad_shrink.reshape(send_ref.shape)
    else:
        hidden_ref[...] = hidden
        pre_ref[...] = grad_pre

    @pl.when(step == pl.num_programs(0) - 1)
    def _():
        results = result_acc[...].astype(bf16)
        back = back_acc[...].astype(bf16)
        back_ref[:, :width] = results
        back_ref[:, width : 2 * width] = back
        inner = jnp.sum(
            results.astype(f32) * grad_acc[...] + back.astype(f32) * mixed_acc[...],
            axis=-1,
            keepdims=True,
        )
        lane = lax.broadcasted_iota(jnp.int32, stat.shape, 1)
        a, b, c = split3(stat[...])
        d, e, f = split3(inner)
        stats = jnp.where(lane == 0, a, jnp.where(lane == 1, b, c))
        stats = jnp.where(lane < 3, stats, jnp.where(lane == 3, d, jnp.where(lane == 4, e, f)))
        back_ref[:, 2 * width :] = stats.astype(bf16)


def pack_expert(expand, shrink):
    experts, lines, hidden = expand.shape
    width = shrink.shape[-1]
    expand = expand.reshape(experts, lines, hidden // width, width)
    expand = jnp.swapaxes(expand, 1, 2).reshape(experts, -1, width)
    return jnp.concatenate([expand, shrink], axis=1)


def unpack_expert(packed, lines):
    experts, both, width = packed.shape
    expand = packed[:, : both // 2].reshape(experts, -1, lines, width)
    expand = jnp.swapaxes(expand, 1, 2).reshape(experts, lines, -1)
    return expand, packed[:, both // 2 :]


def expert(me, core, part, parts, pay_slots, halves, earlier):
    slot_count = len(pay_slots)
    groups, packed = pay_slots[0].shape
    shards = 2 * halves[0][0].shape[0]
    tail, width = halves[0][0].shape[1:]
    hidden = shards * tail
    chunks = hidden // width
    lines = width // shards
    acc = ((groups, width), f32)
    low = ((groups, width), bf16)
    tiled = lines % 16 == 0
    group = shards // chunks // 2
    if tiled:
        columns = pl.BlockSpec((shards // 2, lines, width), lambda f, me: (0, f, 0))
        lower = pl.BlockSpec((group, tail, width), lambda f, me: (f, 0, 0))
        weights = [*halves[0], *halves[1]]
        specs = [columns, columns, lower, lower]
        built = [((shards // 2, 2, lines, width), bf16), ((group, 2, tail, width), bf16)]
        both = (shards // 2, 2 * tail, width)
        grads = [(whole(*both), both, bf16)] * 2
    else:
        odd = core == 1
        weights = [
            jnp.stack([jnp.where(odd, b, a), jnp.where(odd, a, b)], axis=1) for a, b in halves
        ]
        expand = weights[0].reshape(shards, chunks, lines, width)
        expand = jnp.swapaxes(expand, 0, 1).reshape(chunks, width, width)
        weights = [expand, weights[1].reshape(chunks, width, width)]
        specs = [pl.BlockSpec((1, width, width), lambda f, me: (f, 0, 0))] * 2
        built = []
        grads = [(specs[0], (chunks, width, width), bf16)] * 2
    token = whole(groups, width)
    inner = pl.BlockSpec((groups, width), lambda f, me: (0, f))
    last = part == parts - 1
    outs = [(whole(groups, packed), (groups, packed), bf16)]
    scratch = [acc, acc, acc, acc, ((groups, LANES), f32)] + built
    if last:
        outs += grads
        scratch += [low, low]
    else:
        outs += [(token, (groups, width), bf16)] * 2 + [(inner, (groups, hidden), bf16)] * 2
    result = call(
        functools.partial(expert_kernel, part, parts, tiled, slot_count),
        "expert",
        (chunks,),
        [whole(groups, packed)] * slot_count + specs + [token, token, inner, inner] * part,
        outs,
        scratch,
        (me, *pay_slots, *weights, *earlier),
        7,
        room=18,
    )
    more = list(result[1:])
    if last and not tiled:
        grad = jnp.swapaxes(more[0].reshape(chunks, shards, lines, width), 0, 1)
        more = [grad.reshape(shards, tail, width), more[1].reshape(shards, tail, width)]
        more = jnp.concatenate(more, axis=1).reshape(shards // 2, 2, 2 * tail, width)
        odd = core == 1
        more = [
            jnp.where(odd, more[:, 1], more[:, 0]),
            jnp.where(odd, more[:, 0], more[:, 1]),
        ]
    return result[0], more


def unmix_kernel(slot_count, experts, piece, part, last, *refs):
    me_ref = refs[0]
    ret_refs = refs[1 : 1 + experts]
    att_refs = refs[1 + experts : 1 + experts + slot_count]
    rest = refs[1 + experts + slot_count :]
    inputs_ref, cot_ref, w_out_ref, gain_ref, control_ref = rest[:5]
    rest = rest[5:]
    if part:
        old_out_ref, old_control_ref, old_gain_ref = rest[1:4]
        rest = rest[4:]
    out_ref, grad_middle_ref = rest[:2]
    back_refs = rest[2 : 2 + slot_count]
    rest = rest[2 + slot_count :]
    if last:
        keep_ref, send_ref, middle_scratch, small = rest
    else:
        grad_out_ref, grad_control_ref, grad_gain_ref, middle_scratch = rest
    rows, positions, width = att_refs[0].shape
    tokens = rows * slot_count
    me = me_ref[0]

    own, group, _ = diagonal(piece)
    control = control_ref[...]
    w_out = w_out_ref[...]
    grad_out, grad_control, grad_gain = 0.0, 0.0, 0.0
    if part:
        grad_out, grad_control = old_out_ref[...], old_control_ref[...]
        grad_gain = old_gain_ref[...]
    for sub in range(positions // piece):
        span = slice(sub * piece, (sub + 1) * piece)
        attended = tokens_of(att_refs, span)
        added = dot(attended, w_out)
        second = []
        for token in range(tokens):
            row = (me ^ (token // rows)) * rows + token % rows
            middle = inputs_ref[row, span].astype(f32) + added[token * piece : (token + 1) * piece]
            middle_scratch[token] = middle
            normed, _ = normalize(middle)
            second.append((normed * gain_ref[...]).astype(bf16))
        second = jnp.concatenate(second, axis=0)
        cot = rows_of(cot_ref, me, rows, slot_count, span)
        log_total = jnp.zeros((piece, LANES), f32)
        inner = jnp.zeros((piece, LANES), f32)
        for e in range(experts):
            stats = ret_refs[e][span, 2 * width :].astype(f32)
            mine = group == e
            log_total = jnp.where(mine, stats[:, 0:1] + stats[:, 1:2] + stats[:, 2:3], log_total)
            inner = jnp.where(mine, stats[:, 3:4] + stats[:, 4:5] + stats[:, 5:6], inner)
        results = jnp.concatenate([ref[span, :width] for ref in ret_refs], axis=0)
        back = jnp.concatenate([ref[span, width : 2 * width] for ref in ret_refs], axis=0)
        logits = dot(second, control, NT).reshape(tokens, piece, LANES)
        weights = jnp.where(own, jnp.exp(logits - log_total), 0.0)
        low = weights.reshape(-1, LANES).astype(bf16)
        spread = dot(low, results)
        grad_weights = (dot(cot, results, NT) + dot(second, back, NT)).reshape(tokens, piece, LANES)
        grad_logits = (weights * (grad_weights - inner)).reshape(-1, LANES).astype(bf16)
        grad_second = dot(low, back) + dot(grad_logits, control)
        grad_control = grad_control + dot(grad_logits, second, TN)
        grad_middles = []
        for token in range(tokens):
            row = (me ^ (token // rows)) * rows + token % rows
            mine = slice(token * piece, (token + 1) * piece)
            middle = middle_scratch[token]
            out_ref[row, span] = (middle + spread[mine].astype(bf16).astype(f32)).astype(bf16)
            grad = grad_second[mine].astype(bf16).astype(f32)
            normed, scaled = normalize(middle)
            grad_gain = grad_gain + jnp.sum((grad * normed).reshape(-1, 8, width), axis=0)
            grad_middle = norm_back(grad * gain_ref[...], normed, scaled)
            grad_middle = (cot_ref[row, span].astype(f32) + grad_middle).astype(bf16)
            grad_middle_ref[token, span] = grad_middle
            grad_middles.append(grad_middle)
        grad_middle = jnp.concatenate(grad_middles, axis=0)
        grad_attended = dot(grad_middle, w_out, NT).astype(bf16)
        grad_attended = grad_attended.reshape(tokens, piece, width)
        for j in range(slot_count):
            back_refs[j][:, span] = grad_attended[j * rows : (j + 1) * rows]
        grad_out = grad_out + dot(attended, grad_middle, TN)
    if last:
        small[...] = jnp.zeros_like(small)
        small[0:1] = jnp.sum(grad_gain, axis=0, keepdims=True)
        for e in range(experts):
            total = grad_control[e * piece : (e + 1) * piece]
            small[pl.ds(1 + (me_ref[1] ^ e), 1)] = jnp.sum(total, axis=0, keepdims=True)
        blocks, lines = keep_ref.shape[:2]
        for columns, value in (
            (slice(0, width), grad_out),
            (slice(width, width + LANES), small[...].T),
        ):
            keep, send = by_core(me, value.reshape(blocks, 2, lines, -1))
            keep_ref[:, :, columns] = keep
            send_ref[:, :, columns] = send.astype(bf16)
    else:
        grad_control_ref[...] = grad_control
        grad_gain_ref[...] = grad_gain
        grad_out_ref[...] = grad_out


def unmix(
    me, part, last, shards, ret_slots, att_slots, inputs, cotangent, w_out, gain, control, before
):
    slot_count, experts = len(att_slots), len(ret_slots)
    rows, positions, width = att_slots[0].shape
    tokens = rows * slot_count
    half = pl.BlockSpec((tokens, positions, width), lambda b, me: (0, part, 0))
    count = 1 + experts + slot_count + 5
    if last:
        kept = (shards // 2, width // shards, width + LANES)
        made = [(None, kept, f32), (None, kept, bf16)]
    else:
        made = [
            (None, (width, width), f32),
            (None, (LANES, width), f32),
            (None, (8, width), f32),
        ]
    result = call(
        functools.partial(unmix_kernel, slot_count, experts, LANES // experts, part, last),
        "unmix",
        (1,),
        [None] * (experts + slot_count)
        + [half, half, fourth(width), None, None]
        + ([pl.BlockSpec(memory_space=pl.ANY)] + [None] * 3 if part else []),
        [(half, cotangent.shape, bf16), (None, (tokens, positions, width), bf16)]
        + [(None, (rows, positions, width), bf16)] * slot_count
        + made,
        [((tokens, LANES // experts, width), f32)] + ([((LANES, width), f32)] if last else []),
        (me, *ret_slots, *att_slots, inputs, cotangent, w_out, gain, control, *before),
        positions * 12 / 256,
        {count: 0} if part else None,
        room=58,
    )
    do_slots = result[2 : 2 + slot_count]
    return do_slots, result[1], [result[0], *result[2 + slot_count :]]


def finish_kernel(slot_count, row_count, parts, *refs):
    me_ref = refs[0]
    gf_refs = refs[1 : 1 + slot_count * row_count]
    rest = refs[1 + slot_count * row_count :]
    inputs_ref, grad_middle_refs, (gain_ref, out_ref) = rest[0], rest[1 : 1 + parts], rest[1 + parts :]
    me = me_ref[0]
    piece = 64
    positions = out_ref.shape[1]
    some = positions // parts
    for start in range(0, positions, piece):
        span = slice(start, start + piece)
        inner = slice(start % some, start % some + piece)
        for j in range(slot_count):
            for row in range(row_count):
                place = (me ^ j) * row_count + row
                normed, scaled = normalize(inputs_ref[place, span].astype(f32))
                incoming = gf_refs[row * slot_count + j][0, span].astype(f32) * gain_ref[...]
                grad = norm_back(incoming, normed, scaled)
                middle = grad_middle_refs[start // some][j * row_count + row, inner]
                out_ref[place, span] = (grad + middle.astype(f32)).astype(bf16)


def finish(me, gf_rows, inputs, grad_middles, gain):
    slot_count, row_count, parts = len(gf_rows[0]), len(gf_rows), len(grad_middles)
    return call(
        functools.partial(finish_kernel, slot_count, row_count, parts),
        "finish",
        (1,),
        [None] * (slot_count * row_count + 2 + parts),
        [(None, inputs.shape, bf16)],
        [],
        (me, *[gf for row in gf_rows for gf in row], inputs, *grad_middles, gain),
        4,
    )[0]


def on_device(
    sizes,
    inputs,
    segments,
    cotangent,
    gain_attn,
    w_qkv,
    w_out,
    gain_mix,
    w_control,
    w_expand,
    w_shrink,
):
    groups, members, slots = sizes
    local_rows, positions, width = inputs.shape
    experts = w_expand.shape[0]
    rows = local_rows // slots
    place = (("gq", groups), ("gi", members), ("seq", slots))
    owners = (("gq", groups), ("seq", slots))
    seq_me = lax.axis_index("seq")
    member = lax.axis_index("gi")
    me = jnp.stack([seq_me, member]).astype(jnp.int32)

    parts = 2 if positions % BLOCK == 0 else 1

    marks = segments.astype(bf16)[:, None, :]
    marks = jnp.pad(marks, ((0, 0), (0, MARKS - 1), (0, width - positions)))

    def row_part(row, j):
        index = (seq_me ^ j) * rows + row
        parts = [lax.dynamic_slice_in_dim(array, index, 1, axis=0) for array in (inputs, marks)]
        return jnp.concatenate(parts, axis=1)

    x_parts = [[row_part(row, j) for j in range(slots)] for row in range(rows)]
    x_rows = [[x_parts[0][0]]]

    def send_some(slots_of, done, first, last):
        for j in range(first, last):
            done.append(partner(slots_of[j], "seq", slots, j))

    small = jnp.concatenate([gain_attn[None], gain_mix[None], w_control], axis=0)
    small = jnp.pad(jnp.transpose(small), ((0, 0), (0, LANES - 2 - experts)))
    packed = jnp.concatenate([w_qkv, w_out, small], axis=1).astype(bf16)
    packed = Doubling(packed, place, ("seq", "gq", "core"))
    packed.steps("seq")
    x_rows, x_parts, w_expand, w_shrink = together((x_rows, x_parts, w_expand, w_shrink), packed)

    def member_parts(array):
        return [
            lax.dynamic_index_in_dim(array, member ^ j, 0, keepdims=False) for j in range(members)
        ]

    send_some(x_parts[0], x_rows[0], 1, slots // 2 + 1)
    weights = member_parts(pack_expert(w_expand.astype(bf16), w_shrink.astype(bf16)))
    weights = swap_slots(weights, "gi")
    packed.steps("gq")
    x_rows, x_parts, weights = together((x_rows, x_parts, weights), packed)
    send_some(x_parts[0], x_rows[0], slots // 2 + 1, slots)
    packed.at_once("gi")
    weights = jnp.stack(natural(weights, member))
    x_rows, x_parts, weights = together((x_rows, x_parts, weights), packed)
    packed.steps("core")
    x_rows, x_parts, weights = together((x_rows, x_parts, weights), packed)
    tail = weights.shape[1] // 2
    halves = [
        Doubling(half, owners, ("gq", "seq"), 1) for half in (weights[:, :tail], weights[:, tail:])
    ]
    halves[0].steps("gq")
    packed = packed.value.reshape(width, -1)

    old = []
    for row in range(rows):
        old = attend_first(me, row, rows, x_rows[row], packed, parts, old)
        if row == 0:
            vectors = old[-1]
            gains = [vectors[0:1], vectors[1:2]]
            control = natural([vectors[2 + e : 3 + e] for e in range(experts)], member)
            control = jnp.concatenate(
                [jnp.broadcast_to(c, (LANES // experts, width)) for c in control], axis=0
            ).astype(bf16)
        if row + 1 < rows:
            x_rows.append(swap_slots(x_parts[row + 1], "seq"))
            old, x_rows[row + 1] = together((old, x_rows[row + 1]), *halves)
        if row == max(0, rows - 2):
            halves[0].steps("seq")
            halves[1].steps("gq")
        if row == rows - 1:
            old, (gain_one, gain_two), control = together((old, gains, control), *halves)
    att, projected, kept = old[:slots], old[slots : slots + 6], old[slots + 6 : slots + 8]
    att_parts, kept = [swap_slots(att, "seq")], [kept]
    for part in range(1, parts):
        att, more = attend_next(me, part, parts, projected, slots)
        more, att_parts[-1] = hold((more, att_parts[-1]))
        att_parts.append(swap_slots(att, "seq"))
        kept.append(more)
    pay_parts = []
    for part in range(parts):
        pay = mix(
            me, part, att_parts[part], inputs, cotangent, packed, gain_two, control, experts
        )
        if part + 1 < parts:
            pay, att_parts[part + 1] = together((pay, att_parts[part + 1]), halves[1])
        if part == 0:
            halves[1].steps("seq")
        if part == parts - 1:
            pay, pay_parts = together((pay, pay_parts), halves[1])
        pay_parts.append(swap_slots(pay, "gi"))
    halves = [half.value.reshape(-1, *half.value.shape[-2:]) for half in halves]
    halves = [(half, partner(half, "seq", slots, 1)) for half in halves]
    ret_parts, earlier = [], []
    for part in range(parts):
        back, more = expert(me, seq_me % 2, part, parts, pay_parts[part], halves, earlier)
        earlier = earlier + list(more)
        if part + 1 < parts:
            pay_parts[part + 1][1], back = hold((pay_parts[part + 1][1], back))
        elif part:
            back, more, ret_parts = hold((back, more, ret_parts))
        ret_parts.append(swap_slots([back] * members, "gi"))

    kept_grad, send = more
    received = partner(send, "seq", slots, 1)
    bits = [2] * len(bits_of((("gq", groups),)))
    bits += [members] + [2] * (len(bits_of((("seq", slots),))) - 1)

    def to_bits(*terms):
        return [term.reshape(*bits, *term.shape[1:]) for term in terms]

    do_parts, grad_middles, before = [], [], []
    for part in range(parts):
        last = part == parts - 1
        if last:
            sum_expert = Halving(to_bits(kept_grad, received), owners, ("seq", "gq"), 1)
            sum_expert.prepare()
            ret_parts[part], before = together((ret_parts[part], before), sum_expert)
        do, grad_middle, before = unmix(
            me,
            part,
            last,
            groups * members * slots,
            ret_parts[part],
            att_parts[part],
            inputs,
            cotangent,
            packed,
            gain_two,
            control,
            before,
        )
        grad_middles.append(grad_middle)
        do_parts.append(swap_slots(do, "seq"))
    output, keep_out, send_out = before
    every_bit = [2] * len(bits_of(place))
    do_parts, send_out = together((do_parts, send_out), sum_expert)
    sum_expert.exchange()
    received_out = partner(send_out, "seq", slots, 1)

    gf_rows, grad_in = [], None
    for row in range(rows):
        gf_slots, grad_in = attend_back(
            me,
            row,
            rows,
            groups * members * slots,
            x_rows[row],
            do_parts,
            gain_one,
            packed,
            projected,
            kept,
            grad_in,
        )
        grad_in = grad_in[0] if row < rows - 1 else grad_in
        if row == 0:
            gf_slots, grad_in, received_out = together((gf_slots, grad_in, received_out), sum_expert)
            sum_expert.combine()
            while sum_expert.order[0][0] == "seq":
                sum_expert.step(sum_expert.order.pop(0))
            sum_expert.prepare()
            gf_slots, grad_in = together((gf_slots, grad_in), sum_expert)
            sum_expert.exchange()
        if row:
            gf_slots, grad_in, gf_rows = together((gf_slots, grad_in, gf_rows), sum_expert)
        if row < rows - 1:
            gf_rows.append(swap_slots(gf_slots, "seq"))
    gf_rows.append([gf_slots[0]])
    send_some(gf_slots, gf_rows[-1], 1, slots // 2 + 1)
    keep, send = grad_in
    received = partner(send, "seq", slots, 1)
    sum_expert.combine()
    sums = sum_expert.finish()
    columns = [p if j == 0 else p.astype(bf16) for j, p in enumerate(member_parts(sums))]
    columns = swap_slots(columns, "gi")
    gf_rows, gf_slots, received = hold((gf_rows, gf_slots, received))
    send_some(gf_slots, gf_rows[-1], slots // 2 + 1, slots)
    total = keep + received.astype(f32)
    total = jnp.concatenate([total, keep_out + received_out.astype(f32)], axis=-1)
    total = total.reshape(*every_bit[1:], *total.shape[1:])
    sum_in = Halving(total, place, ("gi", "gq", "seq"))
    sum_in.cut(("gi",))
    sum_in.send()
    grad_inputs = finish(me, gf_rows, inputs, grad_middles, gain_one)
    grad_inputs, columns = together((grad_inputs, columns), sum_in)
    sum_in.combine()
    sum_in.cut(("gq", "seq"))
    sum_in.send()
    sum_in.combine()
    columns = natural(columns, member)
    columns = jnp.stack([c.astype(f32) for c in columns])
    grad_expand, grad_shrink = unpack_expert(columns, width // (groups * members * slots))
    total = sum_in.finish()
    grad_in, grad_out = total[:, : 3 * width], total[:, 3 * width :]
    small = jnp.transpose(grad_out[:, width:])
    weighted = jnp.sum(grad_in * w_qkv.astype(bf16).astype(f32), axis=1)
    return (
        output,
        grad_inputs,
        weighted / gain_attn.astype(bf16).astype(f32),
        grad_in,
        grad_out[:, :width],
        small[0],
        small[1 : 1 + experts],
        grad_expand,
        grad_shrink,
    )


def solution(mesh):
    dp_count, seq_count = mesh.shape["dp"], mesh.shape["seq"]

    def run(inputs, *args):
        members = GROUP * dp_count // inputs.shape[0]
        sizes = (dp_count // members, members, seq_count)
        fine = Mesh(mesh.devices.reshape(sizes), ("gq", "gi", "seq"))
        dp, both = ("gq", "gi"), ("gq", "gi", "seq")
        return jax.shard_map(
            functools.partial(on_device, sizes),
            mesh=fine,
            in_specs=(
                P(dp, "seq", None),
                P(dp, "seq"),
                P(dp, "seq", None),
                P(both),
                P(both, None),
                P(both, None),
                P(both),
                P(None, both),
                P(None, both, None),
                P(None, both, None),
            ),
            out_specs=(
                P(dp, "seq", None),
                P(dp, "seq", None),
                P(both),
                P(both, None),
                P(both, None),
                P(both),
                P(None, both),
                P(None, both, None),
                P(None, both, None),
            ),
            check_vma=False,
        )(inputs, *args)

    return run
```
